32 devices in a mesh: fsdp: 16 (over z, y, x), dp: 2 (over core).
Axes of the slice: x: 2, y: 2, z: 4, core: 2. Of those that a mesh axis runs over, the one named last changes fastest.
Arguments:
- tokens: bfloat16 [65536, 512], P(('fsdp', 'dp')), may hold values from -6 to 6
- cotangent: bfloat16 [65536, 512], P(('fsdp', 'dp')), may hold values from -6 to 6
- segment_ids: int32 [64, 1024], P(('fsdp', 'dp')), may hold values from 0 to 5, as said below
- valid_counts: int32 [64], P(('fsdp', 'dp')), may hold values from 768 to 960, as said below
- weight_qkv: float32 [512, 1536], P('fsdp'), may hold values from -0.25 to 0.25
- weight_out: float32 [512, 512], P('fsdp'), may hold values from -1 to 1
- weight_up: float32 [512, 2048], P('fsdp'), may hold values from -0.25 to 0.25
- weight_down: float32 [2048, 512], P('fsdp'), may hold values from -0.125 to 0.125
- vectors: float32 [8, 512], P(None, 'fsdp'), may hold values from -1.2 to 2.6, as said below
- up_bias: float32 [2048], P('fsdp'), may hold values from -1.5 to 1.5
- momentum_qkv: float32 [512, 1536], P('fsdp'), may hold values from -8 to 8
- momentum_out: float32 [512, 512], P('fsdp'), may hold values from -8 to 8
- momentum_up: float32 [512, 2048], P('fsdp'), may hold values from -8 to 8
- momentum_down: float32 [2048, 512], P('fsdp'), may hold values from -8 to 8
- momentum_vectors: float32 [8, 512], P(None, 'fsdp'), may hold values from -32 to 32
- momentum_bias: float32 [2048], P('fsdp'), may hold values from -4 to 4
- squares_qkv: float32 [512, 1536], P('fsdp'), may hold values from 1.6384 to 6.5536
- squares_out: float32 [512, 512], P('fsdp'), may hold values from 1.6384 to 6.5536
- squares_up: float32 [512, 2048], P('fsdp'), may hold values from 1.6384 to 6.5536
- squares_down: float32 [2048, 512], P('fsdp'), may hold values from 1.6384 to 6.5536
- squares_vectors: float32 [8, 512], P(None, 'fsdp'), may hold values from 26.2144 to 104.8576
- squares_bias: float32 [2048], P('fsdp'), may hold values from 0.524288 to 2.097152
Outputs:
- layer_out: bfloat16 [65536, 512], P(('fsdp', 'dp'))
- token_grad: float32 [65536, 512], P(('fsdp', 'dp'))
- grad_norm: float32 [], replicated
- weight_qkv_new: float32 [512, 1536], P('fsdp')
- weight_out_new: float32 [512, 512], P('fsdp')
- weight_up_new: float32 [512, 2048], P('fsdp')
- weight_down_new: float32 [2048, 512], P('fsdp')
- vectors_new: float32 [8, 512], P(None, 'fsdp')
- up_bias_new: float32 [2048], P('fsdp')
- momentum_qkv_new: float32 [512, 1536], P('fsdp')
- momentum_out_new: float32 [512, 512], P('fsdp')
- momentum_up_new: float32 [512, 2048], P('fsdp')
- momentum_down_new: float32 [2048, 512], P('fsdp')
- momentum_vectors_new: float32 [8, 512], P(None, 'fsdp')
- momentum_bias_new: float32 [2048], P('fsdp')
- squares_qkv_new: float32 [512, 1536], P('fsdp')
- squares_out_new: float32 [512, 512], P('fsdp')
- squares_up_new: float32 [512, 2048], P('fsdp')
- squares_down_new: float32 [2048, 512], P('fsdp')
- squares_vectors_new: float32 [8, 512], P(None, 'fsdp')
- squares_bias_new: float32 [2048], P('fsdp')
The draws below stay inside these ranges and needn't reach their ends.
Inputs may be any that keep to these rules, and one draw needn't show every extreme that they name: `segment_ids`: within a packed sequence the ids number its images 0, 1, 2 and on in order, each image 192 or 384 positions long; positions from the sequence's valid count on hold 5. `valid_counts`: the total length of the images of the sequence, a multiple of 192. `vectors`: rows 0 and 5 are positive.
All inputs are finite; a program needn't handle non-finite values.
Results may differ from the reference program's by a relative error of at most 0.017.
The reference program's roundings to bfloat16 on the way count: a program that leaves them out, or rounds other values in their place, can miss the bound.
Values may be sent and summed in bfloat16 or wider, within the bound.
A program may use at most 256 MiB of HBM per device.

```python
import math
import jax
import jax.numpy as jnp
from jax import lax

D = 512
HEADS = 8
HEAD_DIM = 64
FF = 2048
SEQ_LEN = 1024
IMG = 192
STEP = 5
NSEQ = 64
TOKENS = 65536
PARAMS = 3151872


def packing(key):
    kinds = SEQ_LEN // IMG
    picks = jax.random.randint(jax.random.fold_in(key, 7), (NSEQ, kinds), 1, 3)
    row_index = jnp.arange(NSEQ, dtype=jnp.int32)[:, None]
    col_index = jnp.arange(kinds, dtype=jnp.int32)[None, :]
    picks = jnp.where(row_index == 0, 1, picks)
    second_row = jnp.where(col_index == kinds - 1, 2, 1)
    picks = jnp.where(row_index == 1, second_row, picks)
    ends = jnp.cumsum(picks * IMG, axis=1)
    kept = ends <= SEQ_LEN
    valid = jnp.max(jnp.where(kept, ends, 0), axis=1)
    positions = jnp.arange(SEQ_LEN, dtype=jnp.int32)
    crossed = (positions[None, :, None] >= ends[:, None, :]) & kept[:, None, :]
    segments = jnp.sum(crossed.astype(jnp.int32), axis=2)
    segments = jnp.where(positions[None, :] < valid[:, None], segments, kinds)
    return (segments.astype(jnp.int32), valid.astype(jnp.int32))


def draw_segment_ids(key, part):
    return packing(key)[0]


def draw_valid_counts(key, part):
    return packing(key)[1]


def draw_vectors(key, part):
    index = jnp.arange(D, dtype=jnp.float32) / (D - 1)
    ramp = 0.6 + 1.2 * index
    jitter = jax.random.uniform(jax.random.fold_in(key, 3), (8, D), minval=0.8, maxval=1.2)
    shifts = jnp.clip(0.3 * jax.random.normal(jax.random.fold_in(key, 5), (8, D)), -1.2, 1.2)
    gains = ramp[None, :] * jitter
    rows = jnp.arange(8, dtype=jnp.int32)[:, None]
    is_gain = (rows == 0) | (rows == 5)
    return jnp.where(is_gain, gains, shifts).astype(jnp.float32)


def spiked(values, own_key, source, target, shards_of, factor):
    owner, partner = [(jnp.arange(values.shape[axis_at]) // (values.shape[axis_at] // shards_of)).reshape([-1 if axis == axis_at else 1 for axis in range(values.ndim)]) for axis_at in (source, target)]
    chosen = jax.random.permutation(own_key, shards_of)[partner]
    strong = (owner == chosen) | (owner == (partner + shards_of // 2) % shards_of)
    return jnp.where(strong, factor * values, values)


def level_of(stream_key, extent, pieces, low, top_value):
    def one(position, shards_of):
        heights = jax.random.uniform(jax.random.fold_in(jax.random.fold_in(stream_key, 6), position), (shards_of,), jnp.float32, low / len(pieces), top_value / len(pieces))
        return jnp.repeat(jnp.exp(heights), extent[position] // shards_of).reshape((-1,) + (1,) * (len(extent) - position - 1))

    loudness = one(*pieces[0])
    for cut in pieces[1:]:
        loudness = loudness * one(*cut)
    return loudness


def bell_draw(rng, shape, scale, most, cuts=(), kind=jnp.bfloat16):
    values = jax.random.normal(rng, shape, jnp.float32) * scale
    if len(cuts) > 0:
        values = level_of(rng, shape, cuts, -0.22, 0.18) * values
    return jnp.clip(values, min=-most, max=most).astype(kind)


def gaussian_with(own_key, shape, deviation, reach, cuts, heavy, kind=jnp.bfloat16):
    result = deviation * jax.random.normal(own_key, shape, jnp.float32)
    if cuts:
        result = result * level_of(own_key, shape, cuts, -0.22, 0.18)
    return jnp.clip(spiked(result, jax.random.fold_in(own_key, 3), *heavy), -reach, reach).astype(kind)


def setup_inputs(seed: int = 0) -> dict:
    splits = jax.random.split(jax.random.key(seed), 23)
    tokens = gaussian_with(splits[0], (TOKENS, D), 1.0, 6.0, ((0, 32),), (0, 1, 32, 2.75))
    cotangent = bell_draw(splits[1], (TOKENS, D), 1.0, 6.0, ((0, 32),))
    segment_ids = draw_segment_ids(jax.random.fold_in(splits[22], 71), 0)
    valid_counts = draw_valid_counts(jax.random.fold_in(splits[22], 71), 0)
    weight_qkv = bell_draw(splits[4], (D, 3 * D), D ** -0.5, 0.25, ((0, 16),), jnp.float32)
    weight_out = bell_draw(splits[5], (D, D), (D // 16) ** -0.5, 1.0, ((0, 16),), jnp.float32)
    weight_up = bell_draw(splits[6], (D, FF), D ** -0.5, 0.25, ((0, 16),), jnp.float32)
    weight_down = bell_draw(splits[7], (FF, D), FF ** -0.5, 0.125, ((0, 16),), jnp.float32)
    vectors = draw_vectors(jax.random.fold_in(splits[22], 71), 0)
    up_bias = bell_draw(splits[9], (FF,), 0.3, 1.5, ((0, 16),), jnp.float32)
    momentum_qkv = bell_draw(splits[10], (D, 3 * D), (0.005 * TOKENS ** 0.5), 8.0, ((0, 16),), jnp.float32)
    momentum_out = bell_draw(splits[11], (D, D), (0.005 * TOKENS ** 0.5), 8.0, ((0, 16),), jnp.float32)
    momentum_up = bell_draw(splits[12], (D, FF), (0.005 * TOKENS ** 0.5), 8.0, ((0, 16),), jnp.float32)
    momentum_down = bell_draw(splits[13], (FF, D), (0.005 * TOKENS ** 0.5), 8.0, ((0, 16),), jnp.float32)
    momentum_vectors = bell_draw(splits[14], (8, D), (0.02 * TOKENS ** 0.5), 32.0, ((1, 16),), jnp.float32)
    momentum_bias = bell_draw(splits[15], (FF,), (0.003 * TOKENS ** 0.5), 4.0, ((0, 16),), jnp.float32)
    squares_qkv = jnp.clip(jnp.exp(math.log(6.5536) - 1.3862944 * jax.random.uniform(splits[16], (D, 3 * D), jnp.float32) ** level_of(splits[16], (D, 3 * D), ((0, 16),), -0.2, 0.2)), 1.6384, 6.5536)
    squares_out = jnp.clip(jnp.exp(math.log(6.5536) - 1.3862944 * jax.random.uniform(splits[17], (D, D), jnp.float32) ** level_of(splits[17], (D, D), ((0, 16),), -0.2, 0.2)), 1.6384, 6.5536)
    squares_up = jnp.clip(jnp.exp(math.log(6.5536) - 1.3862944 * jax.random.uniform(splits[18], (D, FF), jnp.float32) ** level_of(splits[18], (D, FF), ((0, 16),), -0.2, 0.2)), 1.6384, 6.5536)
    squares_down = jnp.clip(jnp.exp(math.log(6.5536) - 1.3862944 * jax.random.uniform(splits[19], (FF, D), jnp.float32) ** level_of(splits[19], (FF, D), ((0, 16),), -0.2, 0.2)), 1.6384, 6.5536)
    squares_vectors = jnp.clip(jnp.exp(math.log(104.8576) - 1.3862944 * jax.random.uniform(splits[20], (8, D), jnp.float32) ** level_of(splits[20], (8, D), ((1, 16),), -0.2, 0.2)), 26.2144, 104.8576)
    squares_bias = jnp.clip(jnp.exp(math.log(2.097152) - 1.3862944 * jax.random.uniform(splits[21], (FF,), jnp.float32) ** level_of(splits[21], (FF,), ((0, 16),), -0.2, 0.2)), 0.524288, 2.097152)
    return dict(tokens=tokens, cotangent=cotangent, segment_ids=segment_ids, valid_counts=valid_counts, weight_qkv=weight_qkv, weight_out=weight_out, weight_up=weight_up, weight_down=weight_down, vectors=vectors, up_bias=up_bias, momentum_qkv=momentum_qkv, momentum_out=momentum_out, momentum_up=momentum_up, momentum_down=momentum_down, momentum_vectors=momentum_vectors, momentum_bias=momentum_bias, squares_qkv=squares_qkv, squares_out=squares_out, squares_up=squares_up, squares_down=squares_down, squares_vectors=squares_vectors, squares_bias=squares_bias)


@jax.custom_vjp
def low(v):
    return lax.optimization_barrier(v.astype(jnp.bfloat16)).astype(jnp.float32)

@jax.custom_vjp
def low_back(v):
    return v

def low_keep(v):
    return (low(v), None)

def low_pass(kept, grad):
    return (grad,)

def back_keep(v):
    return (v, None)

def back_low(kept, grad):
    return (low(grad),)
low.defvjp(low_keep, low_pass)
low_back.defvjp(back_keep, back_low)
norm_eps = 1e-06
adam_eps = 1e-08
decay_rate = 0.05
beta_first = 0.5
beta_second = 0.5
masked_score = -1e+30

def product(left, right):
    return jnp.dot(left, right, precision=lax.Precision.HIGHEST, preferred_element_type=jnp.float32)

def layer_norm(values, gain, shift):
    center = values - lax.optimization_barrier(jnp.mean(values, axis=-1, keepdims=True))
    spread = lax.rsqrt(lax.optimization_barrier(jnp.mean(center * center, axis=-1, keepdims=True)) + norm_eps)
    return center * spread * gain + shift

def gelu_value(values):
    return 0.5 * values * (1.0 + lax.erf(values * (1.0 / math.sqrt(2.0))))

def group_size():
    size = 1
    while size * 2 * SEQ_LEN <= 4096 and NSEQ % (size * 2) == 0:
        size = size * 2
    return size

def group_forward(rows, segs, valids, low_qkv, low_out, low_up, low_down, low_vectors, low_bias):
    group = segs.shape[0]
    length = segs.shape[1]
    low_one = low(layer_norm(rows, low_vectors[0], low_vectors[1]))
    qkv_bias = jnp.concatenate([low_vectors[2], jnp.zeros((D,), jnp.float32), low_vectors[3]])
    qkv = low(low_back(product(low_one, low_qkv)) + qkv_bias)
    split = qkv.reshape(group, length, 3, HEADS, HEAD_DIM)
    query = split[:, :, 0]
    keys = split[:, :, 1]
    values = split[:, :, 2]
    positions = jnp.arange(length, dtype=jnp.int32)
    same = (segs[:, :, None] == segs[:, None, :]) & (positions[None, None, :] < valids[:, None, None])
    allowed = same | (positions[:, None] == positions[None, :])[None]
    scores = jnp.einsum('gqhd,gkhd->ghqk', query, keys, precision=lax.Precision.HIGHEST)
    scores = low_back(scores * (1.0 / math.sqrt(HEAD_DIM)))
    scores = jnp.where(allowed[:, None], scores, masked_score)
    top = lax.optimization_barrier(jnp.max(scores, axis=-1, keepdims=True))
    expo = jnp.exp(scores - top)
    probs = low(expo / lax.optimization_barrier(jnp.sum(expo, axis=-1, keepdims=True)))
    mixed = jnp.einsum('ghqk,gkhd->gqhd', probs, values, precision=lax.Precision.HIGHEST)
    attended = low_back(low(mixed.reshape(group * length, D)))
    resid = rows + low_back(product(attended, low_out)) + low_vectors[4]
    low_two = low(layer_norm(resid, low_vectors[5], low_vectors[6]))
    hidden = low_back(product(low_two, low_up)) + low_bias
    active = low(gelu_value(hidden))
    return resid + low_back(product(active, low_down)) + low_vectors[7]

def adam_step(weight, moment, square, grad, factor, rate):
    clipped = grad * factor
    moment_new = beta_first * moment + (1.0 - beta_first) * clipped
    square_new = beta_second * square + (1.0 - beta_second) * clipped * clipped
    first_hat = moment_new / (1.0 - beta_first ** STEP)
    second_hat = square_new / (1.0 - beta_second ** STEP)
    weight_new = weight - rate * (first_hat / (jnp.sqrt(second_hat) + adam_eps) + decay_rate * weight)
    return (weight_new, moment_new, square_new)

def reference(tokens, cotangent, segment_ids, valid_counts, weight_qkv, weight_out, weight_up, weight_down, vectors, up_bias, momentum_qkv, momentum_out, momentum_up, momentum_down, momentum_vectors, momentum_bias, squares_qkv, squares_out, squares_up, squares_down, squares_vectors, squares_bias):
    masters = (weight_qkv, weight_out, weight_up, weight_down, vectors, up_bias)
    group = group_size()
    count = NSEQ // group
    seg_groups = segment_ids.reshape(count, group, SEQ_LEN)
    valid_groups = valid_counts.reshape(count, group)

    def layer(rows, params):
        lowered = [low(item) for item in params]

        def one_group(items):
            return group_forward(items[0], items[1], items[2], lowered[0], lowered[1], lowered[2], lowered[3], lowered[4], lowered[5])
        blocks = lax.map(jax.checkpoint(one_group), (rows.reshape(count, group * SEQ_LEN, D), seg_groups, valid_groups))
        return blocks.reshape(TOKENS, D)
    rows = tokens.astype(jnp.float32)
    layer_out, pullback = jax.vjp(layer, rows, masters)
    live = (jnp.arange(SEQ_LEN, dtype=jnp.int32)[None, :] < valid_counts[:, None]).astype(jnp.float32).reshape(TOKENS, 1)
    token_grad, grads = pullback(cotangent.astype(jnp.float32) * live)
    total = jnp.sum(grads[0] * grads[0])
    for item in grads[1:]:
        total = total + jnp.sum(item * item)
    grad_norm = jnp.sqrt(total)
    factor = jnp.minimum(1.0, 0.005 * math.sqrt(TOKENS * PARAMS) / grad_norm)
    rates = (2.0 / math.sqrt(D), 8.0 / math.sqrt(D), 2.0 / math.sqrt(D), 2.0 / math.sqrt(FF), 0.5, 0.5)
    moments = (momentum_qkv, momentum_out, momentum_up, momentum_down, momentum_vectors, momentum_bias)
    squares = (squares_qkv, squares_out, squares_up, squares_down, squares_vectors, squares_bias)
    fresh = [adam_step(masters[k], moments[k], squares[k], grads[k], factor, rates[k]) for k in range(6)]
    return (layer_out.astype(jnp.bfloat16), token_grad, grad_norm, fresh[0][0], fresh[1][0], fresh[2][0], fresh[3][0], fresh[4][0], fresh[5][0], fresh[0][1], fresh[1][1], fresh[2][1], fresh[3][1], fresh[4][1], fresh[5][1], fresh[0][2], fresh[1][2], fresh[2][2], fresh[3][2], fresh[4][2], fresh[5][2])
```

```python
import functools
import math

import jax
import jax.numpy as jnp
from jax import lax
from jax.experimental import pallas as pl
from jax.experimental.pallas import tpu as pltpu
from jax.sharding import PartitionSpec as P

D = 512
HEADS = 8
HEAD_DIM = 64
FF = 2048
SEQ = 1024
IMG = 192
BLOCKS = 5
STEP = 5
PARAMS = 3151872
GROUP = 256
PER_GROUP = GROUP // HEAD_DIM

F32 = jnp.float32
BF16 = jnp.bfloat16

norm_eps = 1e-06
adam_eps = 1e-08
decay_rate = 0.05
beta_first = 0.5
beta_second = 0.5
masked_score = -1e30


def dot(left, right):
    return lax.dot_general(left, right, (((1,), (0,)), ((), ())), preferred_element_type=F32)


def dot_nt(left, right):
    return lax.dot_general(left, right, (((1,), (1,)), ((), ())), preferred_element_type=F32)


def dot_tn(left, right):
    return lax.dot_general(left, right, (((0,), (0,)), ((), ())), preferred_element_type=F32)


def norm_forward(values, gain, shift):
    center = values - jnp.mean(values, axis=-1, keepdims=True)
    spread = lax.rsqrt(jnp.mean(center * center, axis=-1, keepdims=True) + norm_eps)
    hat = center * spread
    return hat * gain + shift, hat, spread


def norm_backward(incoming, hat, spread, gain):
    scaled = incoming * gain
    return spread * (
        scaled
        - jnp.mean(scaled, axis=-1, keepdims=True)
        - hat * jnp.mean(scaled * hat, axis=-1, keepdims=True)
    )


def gelu_pair(values):
    half = 0.5 * (1.0 + lax.erf(values * (1.0 / math.sqrt(2.0))))
    bell = jnp.exp(-0.5 * values * values) * (1.0 / math.sqrt(2.0 * math.pi))
    return values * half, half + values * bell


def col_sum(values):
    return jnp.sum(values, axis=0, keepdims=True)


def head_of_lane():
    return lax.broadcasted_iota(jnp.int32, (1, GROUP), 1) // HEAD_DIM


def stack_heads(rows):
    head = head_of_lane()
    zero = jnp.zeros_like(rows)
    return jnp.concatenate([jnp.where(head == h, rows, zero) for h in range(PER_GROUP)], axis=0)


def unstack_heads(stacked):
    head = head_of_lane()
    n = stacked.shape[0] // PER_GROUP
    rows = stacked[(PER_GROUP - 1) * n :]
    for h in range(PER_GROUP - 2, -1, -1):
        rows = jnp.where(head == h, stacked[h * n : (h + 1) * n], rows)
    return rows


def links(seg, counts, s):
    return [
        (seg[s, b * IMG] == seg[s, (b + 1) * IMG]) & ((b + 1) * IMG < counts[s])
        for b in range(BLOCKS - 1)
    ]


def neighbour(b, linked):
    below = slice((b + 1) * IMG, (b + 2) * IMG) if b < BLOCKS - 1 else None
    above = slice((b - 1) * IMG, b * IMG) if b > 0 else None
    with_below = linked[b] if b < BLOCKS - 1 else jnp.bool_(False)
    with_above = linked[b - 1] if b > 0 else jnp.bool_(False)
    offset = jnp.where(with_below | with_above, 0.0, masked_score)
    return below, above, with_below, with_above, offset


def other_rows(ref, cols, below, above, with_below):
    if above is None:
        return ref[below, cols]
    if below is None:
        return ref[above, cols]
    return jnp.where(with_below, ref[below, cols], ref[above, cols])


def attend_block(query, keys, values, offset):
    stacked = stack_heads(query * jnp.asarray(HEAD_DIM**-0.5, BF16))
    scores = dot_nt(keys, stacked)
    own, other = scores[:IMG], scores[IMG:]
    top = jnp.maximum(
        jnp.max(own, axis=0, keepdims=True), jnp.max(other, axis=0, keepdims=True) + offset
    )
    own = jnp.exp(own - top)
    other = jnp.exp(other - (top - offset))
    total = col_sum(own) + col_sum(other)
    inverse = 1.0 / total
    probs = jnp.concatenate([own * inverse, other * inverse], axis=0).astype(BF16)
    return unstack_heads(dot_tn(probs, values)), top + jnp.log(total)


def attend_block_backward(query, keys, values, grad, lse, offset):
    stacked = stack_heads(query * jnp.asarray(HEAD_DIM**-0.5, BF16))
    grads = stack_heads(grad)
    scores = dot_nt(keys, stacked)
    grad_probs = dot_nt(values, grads)
    own = jnp.exp(scores[:IMG] - lse)
    other = jnp.exp(scores[IMG:] - (lse - offset))
    own_t = own * grad_probs[:IMG]
    other_t = other * grad_probs[IMG:]
    delta = col_sum(own_t) + col_sum(other_t)
    grad_scores = jnp.concatenate([own_t - own * delta, other_t - other * delta], axis=0)
    grad_scores = grad_scores.astype(BF16)
    probs = jnp.concatenate([own, other], axis=0).astype(BF16)
    grad_values = dot(probs, grads)
    grad_keys = dot(grad_scores, stacked)
    grad_query = unstack_heads(dot_tn(grad_scores, keys)) * (HEAD_DIM**-0.5)
    return grad_query, grad_keys, grad_values


def forward_kernel(chunk, seg, counts, tokens, vectors, low_qkv, qkv, attended, lse):
    s = pl.program_id(0)
    bias = jnp.concatenate([vectors[2:3, :], jnp.zeros((1, D), F32), vectors[3:4, :]], axis=1)
    for c in range(SEQ // chunk):
        rows = slice(c * chunk, (c + 1) * chunk)
        normed, _, _ = norm_forward(tokens[rows, :].astype(F32), vectors[0:1, :], vectors[1:2, :])
        qkv[rows, :] = (dot(normed.astype(BF16), low_qkv[...]) + bias).astype(BF16)
    linked = links(seg, counts, s)
    for g in range(D // GROUP):
        query_cols, key_cols, value_cols = [
            slice(j * D + g * GROUP, j * D + (g + 1) * GROUP) for j in range(3)
        ]
        out_cols = slice(g * GROUP, (g + 1) * GROUP)
        for b in range(BLOCKS):
            rows = slice(b * IMG, (b + 1) * IMG)
            below, above, with_below, with_above, offset = neighbour(b, linked)
            keys = jnp.concatenate(
                [qkv[rows, key_cols], other_rows(qkv, key_cols, below, above, with_below)], axis=0
            )
            own_values = qkv[rows, value_cols]
            values = jnp.concatenate(
                [own_values, other_rows(qkv, value_cols, below, above, with_below)], axis=0
            )
            mixed, block_lse = attend_block(qkv[rows, query_cols], keys, values, offset)
            mixed = mixed.astype(BF16)
            if b == BLOCKS - 1:
                mixed = jnp.where(b * IMG >= counts[s], own_values, mixed)
            attended[rows, out_cols] = mixed
            lse[g * BLOCKS + b] = block_lse
        attended[BLOCKS * IMG :, out_cols] = qkv[BLOCKS * IMG :, value_cols]


def feed_kernel(
    rows_in,
    chunk,
    counts,
    tokens,
    cotangent,
    attended,
    vectors,
    up_bias,
    low_out,
    low_up,
    low_down,
    layer_out,
    grad_resid,
    grad_attended,
    grad_down,
    grad_up,
    grad_out_w,
    grad_vectors,
    grad_bias,
):
    i = pl.program_id(0)

    @pl.when(i == 0)
    def _():
        for ref in (grad_down, grad_up, grad_out_w, grad_vectors, grad_bias):
            ref[...] = jnp.zeros_like(ref)

    per = SEQ // rows_in
    mixed = attended[...]
    resid = tokens[...].astype(F32) + (dot(mixed, low_out[...]) + vectors[4:5, :])
    normed, hat, spread = norm_forward(resid, vectors[5:6, :], vectors[6:7, :])
    low_two = normed.astype(BF16)
    position = (i % per) * rows_in + lax.broadcasted_iota(jnp.int32, (rows_in, 1), 0)
    grad = jnp.where(position < counts[i // per], cotangent[...].astype(F32), 0.0)
    grad_low = grad.astype(BF16)
    out = jnp.zeros((rows_in, D), F32)
    grad_two = jnp.zeros((rows_in, D), F32)
    for c in range(FF // chunk):
        cols = slice(c * chunk, (c + 1) * chunk)
        hidden = dot(low_two, low_up[:, cols]) + up_bias[:, cols]
        grad_active = dot_nt(grad_low, low_down[cols, :])
        active, slope = gelu_pair(hidden)
        active = active.astype(BF16)
        grad_hidden = grad_active * slope
        grad_hidden_low = grad_hidden.astype(BF16)
        out += dot(active, low_down[cols, :])
        grad_bias[:, cols] += col_sum(grad_hidden)
        grad_down[cols, :] += dot_tn(active, grad_low)
        grad_up[:, cols] += dot_tn(low_two, grad_hidden_low)
        grad_two += dot_nt(grad_hidden_low, low_up[:, cols])
    layer_out[...] = (resid + (out + vectors[7:8, :])).astype(BF16)
    back = grad + norm_backward(grad_two, hat, spread, vectors[5:6, :])
    back_low = back.astype(BF16)
    grad_resid[...] = back
    grad_out_w[...] += dot_tn(mixed, back_low)
    grad_attended[...] = dot_nt(back_low, low_out[...]).astype(BF16)
    grad_vectors[4:5, :] += col_sum(back)
    grad_vectors[5:6, :] += col_sum(grad_two * hat)
    grad_vectors[6:7, :] += col_sum(grad_two)
    grad_vectors[7:8, :] += col_sum(grad)


def backward_kernel(
    chunk,
    seg,
    counts,
    tokens,
    vectors,
    low_qkv,
    qkv,
    grad_attended,
    grad_resid,
    lse,
    token_grad,
    grad_qkv_w,
    grad_vectors,
    grad_qkv,
    key_sum,
    value_sum,
):
    s = pl.program_id(0)

    @pl.when(s == 0)
    def _():
        grad_qkv_w[...] = jnp.zeros_like(grad_qkv_w)
        grad_vectors[...] = jnp.zeros_like(grad_vectors)

    linked = links(seg, counts, s)
    padded = (BLOCKS - 1) * IMG >= counts[s]
    covered = slice(0, BLOCKS * IMG)
    tail = slice(BLOCKS * IMG, SEQ)
    for g in range(D // GROUP):
        query_cols, key_cols, value_cols = [
            slice(j * D + g * GROUP, j * D + (g + 1) * GROUP) for j in range(3)
        ]
        grad_cols = slice(g * GROUP, (g + 1) * GROUP)
        query_bias = jnp.zeros((1, GROUP), F32)
        for b in range(BLOCKS):
            rows = slice(b * IMG, (b + 1) * IMG)
            below, above, with_below, with_above, offset = neighbour(b, linked)
            keys = jnp.concatenate(
                [qkv[rows, key_cols], other_rows(qkv, key_cols, below, above, with_below)], axis=0
            )
            values = jnp.concatenate(
                [qkv[rows, value_cols], other_rows(qkv, value_cols, below, above, with_below)],
                axis=0,
            )
            grad = grad_attended[rows, grad_cols]
            grad_query, grad_keys, grad_values = attend_block_backward(
                qkv[rows, query_cols], keys, values, grad, lse[g * BLOCKS + b], offset
            )
            own_keys, own_values = grad_keys[:IMG], grad_values[:IMG]
            if b == BLOCKS - 1:
                grad_query = jnp.where(padded, 0.0, grad_query)
                own_keys = jnp.where(padded, 0.0, own_keys)
                own_values = jnp.where(padded, grad.astype(F32), own_values)
            query_bias += col_sum(grad_query)
            grad_qkv[rows, query_cols] = grad_query.astype(BF16)
            if b > 0:
                own_keys += jnp.where(with_above, key_sum[rows, :], 0.0)
                own_values += jnp.where(with_above, value_sum[rows, :], 0.0)
            key_sum[rows, :] = own_keys
            value_sum[rows, :] = own_values
            if below is not None:
                key_sum[below, :] = grad_keys[IMG:]
                value_sum[below, :] = grad_values[IMG:]
            if above is not None:
                key_sum[above, :] += jnp.where(with_above, grad_keys[IMG:], 0.0)
                value_sum[above, :] += jnp.where(with_above, grad_values[IMG:], 0.0)
        grad_tail = grad_attended[tail, grad_cols]
        grad_qkv[tail, query_cols] = jnp.zeros_like(grad_tail)
        grad_qkv[tail, key_cols] = jnp.zeros_like(grad_tail)
        grad_qkv[tail, value_cols] = grad_tail
        grad_qkv[covered, key_cols] = key_sum[...].astype(BF16)
        all_values = value_sum[...]
        grad_qkv[covered, value_cols] = all_values.astype(BF16)
        grad_vectors[2:3, grad_cols] += query_bias
        grad_vectors[3:4, grad_cols] += col_sum(all_values) + col_sum(grad_tail.astype(F32))
    for c in range(SEQ // chunk):
        rows = slice(c * chunk, (c + 1) * chunk)
        normed, hat, spread = norm_forward(
            tokens[rows, :].astype(F32), vectors[0:1, :], vectors[1:2, :]
        )
        grad = grad_qkv[rows, :]
        grad_qkv_w[...] += dot_tn(normed.astype(BF16), grad)
        grad_one = dot_nt(grad, low_qkv[...])
        token_grad[rows, :] = grad_resid[rows, :] + norm_backward(
            grad_one, hat, spread, vectors[0:1, :]
        )
        grad_vectors[0:1, :] += col_sum(grad_one * hat)
        grad_vectors[1:2, :] += col_sum(grad_one)


def vmem_params():
    return pltpu.CompilerParams(vmem_limit_bytes=60 * 2**20)


def by_rows(rows, cols):
    return pl.BlockSpec((rows, cols), lambda i: (i, 0))


def whole(*shape):
    return pl.BlockSpec(shape, lambda i: (0,) * len(shape))


def stats_spec():
    return pl.BlockSpec((2 * BLOCKS, 1, PER_GROUP * IMG), lambda i: (i, 0, 0))


def shaped(shape, dtype):
    return jax.ShapeDtypeStruct(shape, dtype)


SCALAR = pl.BlockSpec(memory_space=pltpu.SMEM)


def run_forward(seg, counts, tokens, vectors, low_qkv):
    rows = tokens.shape[0]
    seqs = rows // SEQ
    return pl.pallas_call(
        functools.partial(forward_kernel, 256),
        grid=(seqs,),
        in_specs=[SCALAR, SCALAR, by_rows(SEQ, D), whole(8, D), whole(D, 3 * D)],
        out_specs=[by_rows(SEQ, 3 * D), by_rows(SEQ, D), stats_spec()],
        out_shape=[
            shaped((rows, 3 * D), BF16),
            shaped((rows, D), BF16),
            shaped((seqs * 2 * BLOCKS, 1, PER_GROUP * IMG), F32),
        ],
        compiler_params=vmem_params(),
        name="attend_forward",
    )(seg, counts, tokens, vectors, low_qkv)


def run_feed(counts, tokens, cotangent, attended, vectors, up_bias, low_out, low_up, low_down):
    rows = tokens.shape[0]
    step = 512
    return pl.pallas_call(
        functools.partial(feed_kernel, step, 512),
        grid=(rows // step,),
        in_specs=[
            SCALAR,
            by_rows(step, D),
            by_rows(step, D),
            by_rows(step, D),
            whole(8, D),
            whole(1, FF),
            whole(D, D),
            whole(D, FF),
            whole(FF, D),
        ],
        out_specs=[
            by_rows(step, D),
            by_rows(step, D),
            by_rows(step, D),
            whole(FF, D),
            whole(D, FF),
            whole(D, D),
            whole(8, D),
            whole(1, FF),
        ],
        out_shape=[
            shaped((rows, D), BF16),
            shaped((rows, D), F32),
            shaped((rows, D), BF16),
            shaped((FF, D), F32),
            shaped((D, FF), F32),
            shaped((D, D), F32),
            shaped((8, D), F32),
            shaped((1, FF), F32),
        ],
        compiler_params=vmem_params(),
        name="feed_forward",
    )(counts, tokens, cotangent, attended, vectors, up_bias, low_out, low_up, low_down)


def run_backward(seg, counts, tokens, vectors, low_qkv, qkv, grad_attended, grad_resid, lse):
    rows = tokens.shape[0]
    return pl.pallas_call(
        functools.partial(backward_kernel, 512),
        grid=(rows // SEQ,),
        in_specs=[
            SCALAR,
            SCALAR,
            by_rows(SEQ, D),
            whole(8, D),
            whole(D, 3 * D),
            by_rows(SEQ, 3 * D),
            by_rows(SEQ, D),
            by_rows(SEQ, D),
            stats_spec(),
        ],
        out_specs=[by_rows(SEQ, D), whole(D, 3 * D), whole(8, D)],
        out_shape=[
            shaped((rows, D), F32),
            shaped((D, 3 * D), F32),
            shaped((8, D), F32),
        ],
        scratch_shapes=[
            pltpu.VMEM((SEQ, 3 * D), BF16),
            pltpu.VMEM((BLOCKS * IMG, GROUP), F32),
            pltpu.VMEM((BLOCKS * IMG, GROUP), F32),
        ],
        compiler_params=vmem_params(),
        name="attend_backward",
    )(seg, counts, tokens, vectors, low_qkv, qkv, grad_attended, grad_resid, lse)


def adam_step(weight, moment, square, grad, factor, rate):
    clipped = grad * factor
    moment_new = beta_first * moment + (1.0 - beta_first) * clipped
    square_new = beta_second * square + (1.0 - beta_second) * clipped * clipped
    first_hat = moment_new / (1.0 - beta_first**STEP)
    second_hat = square_new / (1.0 - beta_second**STEP)
    weight_new = weight - rate * (
        first_hat / (jnp.sqrt(second_hat) + adam_eps) + decay_rate * weight
    )
    return (weight_new, moment_new, square_new)


RATES = (
    2.0 / math.sqrt(D),
    8.0 / math.sqrt(D),
    2.0 / math.sqrt(D),
    2.0 / math.sqrt(FF),
    0.5,
    0.5,
)


def body(tokens, cotangent, segment_ids, valid_counts, *state):
    masters, moments, squares = state[:6], state[6:12], state[12:18]
    wide = lax.axis_size("fsdp")
    replicas = lax.axis_size("dp")
    low = [item.astype(BF16) for item in masters]
    full = [
        lax.all_gather(item, "fsdp", axis=1 if k == 4 else 0, tiled=True)
        for k, item in enumerate(low)
    ]
    low_qkv, low_out, low_up, low_down = full[:4]
    vectors = full[4].astype(F32)
    up_bias = full[5].astype(F32).reshape(1, FF)
    qkv, attended, lse = run_forward(segment_ids, valid_counts, tokens, vectors, low_qkv)
    (
        layer_out,
        grad_resid,
        grad_attended,
        grad_down,
        grad_up,
        grad_out_w,
        late_vectors,
        grad_bias,
    ) = run_feed(
        valid_counts, tokens, cotangent, attended, vectors, up_bias, low_out, low_up, low_down
    )
    token_grad, grad_qkv_w, early_vectors = run_backward(
        segment_ids,
        valid_counts,
        tokens,
        vectors,
        low_qkv,
        qkv,
        grad_attended,
        grad_resid,
        lse,
    )
    partial = (
        grad_qkv_w,
        grad_out_w,
        grad_up,
        grad_down,
        early_vectors + late_vectors,
        grad_bias.reshape(FF),
    )
    grads = []
    for k, item in enumerate(partial):
        shard = lax.psum_scatter(item, "fsdp", scatter_dimension=1 if k == 4 else 0, tiled=True)
        grads.append(lax.psum(shard.astype(BF16), "dp").astype(F32))
    local_total = jnp.sum(grads[0] * grads[0])
    for item in grads[1:]:
        local_total = local_total + jnp.sum(item * item)
    grad_norm = jnp.sqrt(lax.psum(local_total, "fsdp"))
    bound = 0.005 * math.sqrt(tokens.shape[0] * wide * replicas * PARAMS)
    factor = jnp.minimum(1.0, bound / grad_norm)
    fresh = [
        adam_step(masters[k], moments[k], squares[k], grads[k], factor, RATES[k]) for k in range(6)
    ]
    return (
        layer_out,
        token_grad,
        grad_norm,
        *(item[0] for item in fresh),
        *(item[1] for item in fresh),
        *(item[2] for item in fresh),
    )


def solution(mesh):
    rows = P(("fsdp", "dp"), None)
    state = (
        P("fsdp", None),
        P("fsdp", None),
        P("fsdp", None),
        P("fsdp", None),
        P(None, "fsdp"),
        P("fsdp"),
    )
    return jax.shard_map(
        body,
        mesh=mesh,
        in_specs=(rows, rows, rows, P(("fsdp", "dp")), *state, *state, *state),
        out_specs=(rows, rows, P(), *state, *state, *state),
        check_vma=False,
    )
```

```python
import functools
import math

import jax
import jax.numpy as jnp
from jax import lax
from jax.experimental import pallas as pl
from jax.experimental.pallas import tpu as pltpu
from jax.sharding import PartitionSpec as P

D = 512
HEADS = 8
HEAD_DIM = 64
FF = 2048
SEQ = 1024
IMG = 192
BLOCKS = 5
STEP = 5
PARAMS = 3151872
GROUP = 256
PER_GROUP = GROUP // HEAD_DIM

F32 = jnp.float32
BF16 = jnp.bfloat16

norm_eps = 1e-06
adam_eps = 1e-08
decay_rate = 0.05
beta_first = 0.5
beta_second = 0.5
masked_score = -1e30


def dot(left, right):
    return lax.dot_general(left, right, (((1,), (0,)), ((), ())), preferred_element_type=F32)


def dot_nt(left, right):
    return lax.dot_general(left, right, (((1,), (1,)), ((), ())), preferred_element_type=F32)


def dot_tn(left, right):
    return lax.dot_general(left, right, (((0,), (0,)), ((), ())), preferred_element_type=F32)


def norm_forward(values, gain, shift):
    center = values - jnp.mean(values, axis=-1, keepdims=True)
    spread = lax.rsqrt(jnp.mean(center * center, axis=-1, keepdims=True) + norm_eps)
    hat = center * spread
    return hat * gain + shift, hat, spread


def norm_backward(incoming, hat, spread, gain):
    scaled = incoming * gain
    return spread * (
        scaled
        - jnp.mean(scaled, axis=-1, keepdims=True)
        - hat * jnp.mean(scaled * hat, axis=-1, keepdims=True)
    )


def gelu_pair(values):
    half = 0.5 * (1.0 + lax.erf(values * (1.0 / math.sqrt(2.0))))
    bell = jnp.exp(-0.5 * values * values) * (1.0 / math.sqrt(2.0 * math.pi))
    return values * half, half + values * bell


def col_sum(values):
    return jnp.sum(values, axis=0, keepdims=True)


def head_of_lane():
    return lax.broadcasted_iota(jnp.int32, (1, GROUP), 1) // HEAD_DIM


def stack_heads(rows):
    head = head_of_lane()
    zero = jnp.zeros_like(rows)
    return jnp.concatenate([jnp.where(head == h, rows, zero) for h in range(PER_GROUP)], axis=0)


def unstack_heads(stacked):
    head = head_of_lane()
    n = stacked.shape[0] // PER_GROUP
    rows = stacked[(PER_GROUP - 1) * n :]
    for h in range(PER_GROUP - 2, -1, -1):
        rows = jnp.where(head == h, stacked[h * n : (h + 1) * n], rows)
    return rows


def links(seg, counts, s):
    return [
        (seg[s, b * IMG] == seg[s, (b + 1) * IMG]) & ((b + 1) * IMG < counts[s])
        for b in range(BLOCKS - 1)
    ]


def neighbour(b, linked):
    below = slice((b + 1) * IMG, (b + 2) * IMG) if b < BLOCKS - 1 else None
    above = slice((b - 1) * IMG, b * IMG) if b > 0 else None
    with_below = linked[b] if b < BLOCKS - 1 else jnp.bool_(False)
    with_above = linked[b - 1] if b > 0 else jnp.bool_(False)
    offset = jnp.where(with_below | with_above, 0.0, masked_score)
    return below, above, with_below, with_above, offset


def other_rows(ref, cols, below, above, with_below):
    if above is None:
        return ref[below, cols]
    if below is None:
        return ref[above, cols]
    return jnp.where(with_below, ref[below, cols], ref[above, cols])


def attend_block(query, keys, values, offset):
    stacked = stack_heads(query * jnp.asarray(HEAD_DIM**-0.5, BF16))
    scores = dot_nt(keys, stacked)
    own, other = scores[:IMG], scores[IMG:]
    top = jnp.maximum(
        jnp.max(own, axis=0, keepdims=True), jnp.max(other, axis=0, keepdims=True) + offset
    )
    own = jnp.exp(own - top)
    other = jnp.exp(other - (top - offset))
    total = col_sum(own) + col_sum(other)
    inverse = 1.0 / total
    probs = jnp.concatenate([own * inverse, other * inverse], axis=0).astype(BF16)
    return unstack_heads(dot_tn(probs, values)), top + jnp.log(total)


def attend_block_backward(query, keys, values, grad, lse, offset):
    stacked = stack_heads(query * jnp.asarray(HEAD_DIM**-0.5, BF16))
    grads = stack_heads(grad)
    scores = dot_nt(keys, stacked)
    grad_probs = dot_nt(values, grads)
    own = jnp.exp(scores[:IMG] - lse)
    other = jnp.exp(scores[IMG:] - (lse - offset))
    own_t = own * grad_probs[:IMG]
    other_t = other * grad_probs[IMG:]
    delta = col_sum(own_t) + col_sum(other_t)
    grad_scores = jnp.concatenate([own_t - own * delta, other_t - other * delta], axis=0)
    grad_scores = grad_scores.astype(BF16)
    probs = jnp.concatenate([own, other], axis=0).astype(BF16)
    grad_values = dot(probs, grads)
    grad_keys = dot(grad_scores, stacked)
    grad_query = unstack_heads(dot_tn(grad_scores, keys)) * (HEAD_DIM**-0.5)
    return grad_query, grad_keys, grad_values


def forward_kernel(chunk, seg, counts, tokens, vectors, low_qkv, qkv, attended, lse):
    s = pl.program_id(0)
    bias = jnp.concatenate([vectors[2:3, :], jnp.zeros((1, D), F32), vectors[3:4, :]], axis=1)
    for c in range(SEQ // chunk):
        rows = slice(c * chunk, (c + 1) * chunk)
        normed, _, _ = norm_forward(tokens[rows, :].astype(F32), vectors[0:1, :], vectors[1:2, :])
        qkv[rows, :] = (dot(normed.astype(BF16), low_qkv[...]) + bias).astype(BF16)
    linked = links(seg, counts, s)
    for g in range(D // GROUP):
        query_cols, key_cols, value_cols = [
            slice(j * D + g * GROUP, j * D + (g + 1) * GROUP) for j in range(3)
        ]
        out_cols = slice(g * GROUP, (g + 1) * GROUP)
        for b in range(BLOCKS):
            rows = slice(b * IMG, (b + 1) * IMG)
            below, above, with_below, with_above, offset = neighbour(b, linked)
            keys = jnp.concatenate(
                [qkv[rows, key_cols], other_rows(qkv, key_cols, below, above, with_below)], axis=0
            )
            own_values = qkv[rows, value_cols]
            values = jnp.concatenate(
                [own_values, other_rows(qkv, value_cols, below, above, with_below)], axis=0
            )
            mixed, block_lse = attend_block(qkv[rows, query_cols], keys, values, offset)
            mixed = mixed.astype(BF16)
            if b == BLOCKS - 1:
                mixed = jnp.where(b * IMG >= counts[s], own_values, mixed)
            attended[rows, out_cols] = mixed
            lse[g * BLOCKS + b] = block_lse
        attended[BLOCKS * IMG :, out_cols] = qkv[BLOCKS * IMG :, value_cols]


def feed_kernel(
    rows_in,
    chunk,
    counts,
    tokens,
    cotangent,
    attended,
    vectors,
    up_bias,
    low_out,
    low_up,
    low_down,
    layer_out,
    grad_resid,
    grad_attended,
    grad_down,
    grad_up,
    grad_out_w,
    grad_vectors,
    grad_bias,
):
    i = pl.program_id(0)

    @pl.when(i == 0)
    def _():
        for ref in (grad_down, grad_up, grad_out_w, grad_vectors, grad_bias):
            ref[...] = jnp.zeros_like(ref)

    per = SEQ // rows_in
    mixed = attended[...]
    resid = tokens[...].astype(F32) + (dot(mixed, low_out[...]) + vectors[4:5, :])
    normed, hat, spread = norm_forward(resid, vectors[5:6, :], vectors[6:7, :])
    low_two = normed.astype(BF16)
    position = (i % per) * rows_in + lax.broadcasted_iota(jnp.int32, (rows_in, 1), 0)
    grad = jnp.where(position < counts[i // per], cotangent[...].astype(F32), 0.0)
    grad_low = grad.astype(BF16)
    out = jnp.zeros((rows_in, D), F32)
    grad_two = jnp.zeros((rows_in, D), F32)
    for c in range(FF // chunk):
        cols = slice(c * chunk, (c + 1) * chunk)
        hidden = dot(low_two, low_up[:, cols]) + up_bias[:, cols]
        grad_active = dot_nt(grad_low, low_down[cols, :])
        active, slope = gelu_pair(hidden)
        active = active.astype(BF16)
        grad_hidden = grad_active * slope
        grad_hidden_low = grad_hidden.astype(BF16)
        out += dot(active, low_down[cols, :])
        grad_bias[:, cols] += col_sum(grad_hidden)
        grad_down[cols, :] += dot_tn(active, grad_low)
        grad_up[:, cols] += dot_tn(low_two, grad_hidden_low)
        grad_two += dot_nt(grad_hidden_low, low_up[:, cols])
    layer_out[...] = (resid + (out + vectors[7:8, :])).astype(BF16)
    back = grad + norm_backward(grad_two, hat, spread, vectors[5:6, :])
    back_low = back.astype(BF16)
    grad_resid[...] = back
    grad_out_w[...] += dot_tn(mixed, back_low)
    grad_attended[...] = dot_nt(back_low, low_out[...]).astype(BF16)
    grad_vectors[4:5, :] += col_sum(back)
    grad_vectors[5:6, :] += col_sum(grad_two * hat)
    grad_vectors[6:7, :] += col_sum(grad_two)
    grad_vectors[7:8, :] += col_sum(grad)


def backward_kernel(
    chunk,
    seg,
    counts,
    tokens,
    vectors,
    low_qkv,
    qkv,
    grad_attended,
    grad_resid,
    lse,
    token_grad,
    grad_qkv_w,
    grad_vectors,
    grad_qkv,
    key_sum,
    value_sum,
):
    s = pl.program_id(0)

    @pl.when(s == 0)
    def _():
        grad_qkv_w[...] = jnp.zeros_like(grad_qkv_w)
        grad_vectors[...] = jnp.zeros_like(grad_vectors)

    linked = links(seg, counts, s)
    padded = (BLOCKS - 1) * IMG >= counts[s]
    covered = slice(0, BLOCKS * IMG)
    tail = slice(BLOCKS * IMG, SEQ)
    for g in range(D // GROUP):
        query_cols, key_cols, value_cols = [
            slice(j * D + g * GROUP, j * D + (g + 1) * GROUP) for j in range(3)
        ]
        grad_cols = slice(g * GROUP, (g + 1) * GROUP)
        query_bias = jnp.zeros((1, GROUP), F32)
        for b in range(BLOCKS):
            rows = slice(b * IMG, (b + 1) * IMG)
            below, above, with_below, with_above, offset = neighbour(b, linked)
            keys = jnp.concatenate(
                [qkv[rows, key_cols], other_rows(qkv, key_cols, below, above, with_below)], axis=0
            )
            values = jnp.concatenate(
                [qkv[rows, value_cols], other_rows(qkv, value_cols, below, above, with_below)],
                axis=0,
            )
            grad = grad_attended[rows, grad_cols]
            grad_query, grad_keys, grad_values = attend_block_backward(
                qkv[rows, query_cols], keys, values, grad, lse[g * BLOCKS + b], offset
            )
            own_keys, own_values = grad_keys[:IMG], grad_values[:IMG]
            if b == BLOCKS - 1:
                grad_query = jnp.where(padded, 0.0, grad_query)
                own_keys = jnp.where(padded, 0.0, own_keys)
                own_values = jnp.where(padded, grad.astype(F32), own_values)
            query_bias += col_sum(grad_query)
            grad_qkv[rows, query_cols] = grad_query.astype(BF16)
            if b > 0:
                own_keys += jnp.where(with_above, key_sum[rows, :], 0.0)
                own_values += jnp.where(with_above, value_sum[rows, :], 0.0)
            key_sum[rows, :] = own_keys
            value_sum[rows, :] = own_values
            if below is not None:
                key_sum[below, :] = grad_keys[IMG:]
                value_sum[below, :] = grad_values[IMG:]
            if above is not None:
                key_sum[above, :] += jnp.where(with_above, grad_keys[IMG:], 0.0)
                value_sum[above, :] += jnp.where(with_above, grad_values[IMG:], 0.0)
        grad_tail = grad_attended[tail, grad_cols]
        grad_qkv[tail, query_cols] = jnp.zeros_like(grad_tail)
        grad_qkv[tail, key_cols] = jnp.zeros_like(grad_tail)
        grad_qkv[tail, value_cols] = grad_tail
        grad_qkv[covered, key_cols] = key_sum[...].astype(BF16)
        all_values = value_sum[...]
        grad_qkv[covered, value_cols] = all_values.astype(BF16)
        grad_vectors[2:3, grad_cols] += query_bias
        grad_vectors[3:4, grad_cols] += col_sum(all_values) + col_sum(grad_tail.astype(F32))
    for c in range(SEQ // chunk):
        rows = slice(c * chunk, (c + 1) * chunk)
        normed, hat, spread = norm_forward(
            tokens[rows, :].astype(F32), vectors[0:1, :], vectors[1:2, :]
        )
        grad = grad_qkv[rows, :]
        grad_qkv_w[...] += dot_tn(normed.astype(BF16), grad)
        grad_one = dot_nt(grad, low_qkv[...])
        token_grad[rows, :] = grad_resid[rows, :] + norm_backward(
            grad_one, hat, spread, vectors[0:1, :]
        )
        grad_vectors[0:1, :] += col_sum(grad_one * hat)
        grad_vectors[1:2, :] += col_sum(grad_one)


def vmem_params():
    return pltpu.CompilerParams(vmem_limit_bytes=60 * 2**20)


def by_rows(rows, cols):
    return pl.BlockSpec((rows, cols), lambda i: (i, 0))


def whole(*shape):
    return pl.BlockSpec(shape, lambda i: (0,) * len(shape))


def stats_spec():
    return pl.BlockSpec((2 * BLOCKS, 1, PER_GROUP * IMG), lambda i: (i, 0, 0))


def shaped(shape, dtype):
    return jax.ShapeDtypeStruct(shape, dtype)


SCALAR = pl.BlockSpec(memory_space=pltpu.SMEM)


def run_forward(seg, counts, tokens, vectors, low_qkv):
    rows = tokens.shape[0]
    seqs = rows // SEQ
    return pl.pallas_call(
        functools.partial(forward_kernel, 256),
        grid=(seqs,),
        in_specs=[SCALAR, SCALAR, by_rows(SEQ, D), whole(8, D), whole(D, 3 * D)],
        out_specs=[by_rows(SEQ, 3 * D), by_rows(SEQ, D), stats_spec()],
        out_shape=[
            shaped((rows, 3 * D), BF16),
            shaped((rows, D), BF16),
            shaped((seqs * 2 * BLOCKS, 1, PER_GROUP * IMG), F32),
        ],
        compiler_params=vmem_params(),
        name="attend_forward",
    )(seg, counts, tokens, vectors, low_qkv)


def run_feed(counts, tokens, cotangent, attended, vectors, up_bias, low_out, low_up, low_down):
    rows = tokens.shape[0]
    step = 512
    return pl.pallas_call(
        functools.partial(feed_kernel, step, 512),
        grid=(rows // step,),
        in_specs=[
            SCALAR,
            by_rows(step, D),
            by_rows(step, D),
            by_rows(step, D),
            whole(8, D),
            whole(1, FF),
            whole(D, D),
            whole(D, FF),
            whole(FF, D),
        ],
        out_specs=[
            by_rows(step, D),
            by_rows(step, D),
            by_rows(step, D),
            whole(FF, D),
            whole(D, FF),
            whole(D, D),
            whole(8, D),
            whole(1, FF),
        ],
        out_shape=[
            shaped((rows, D), BF16),
            shaped((rows, D), F32),
            shaped((rows, D), BF16),
            shaped((FF, D), F32),
            shaped((D, FF), F32),
            shaped((D, D), F32),
            shaped((8, D), F32),
            shaped((1, FF), F32),
        ],
        compiler_params=vmem_params(),
        name="feed_forward",
    )(counts, tokens, cotangent, attended, vectors, up_bias, low_out, low_up, low_down)


def run_backward(seg, counts, tokens, vectors, low_qkv, qkv, grad_attended, grad_resid, lse):
    rows = tokens.shape[0]
    return pl.pallas_call(
        functools.partial(backward_kernel, 512),
        grid=(rows // SEQ,),
        in_specs=[
            SCALAR,
            SCALAR,
            by_rows(SEQ, D),
            whole(8, D),
            whole(D, 3 * D),
            by_rows(SEQ, 3 * D),
            by_rows(SEQ, D),
            by_rows(SEQ, D),
            stats_spec(),
        ],
        out_specs=[by_rows(SEQ, D), whole(D, 3 * D), whole(8, D)],
        out_shape=[
            shaped((rows, D), F32),
            shaped((D, 3 * D), F32),
            shaped((8, D), F32),
        ],
        scratch_shapes=[
            pltpu.VMEM((SEQ, 3 * D), BF16),
            pltpu.VMEM((BLOCKS * IMG, GROUP), F32),
            pltpu.VMEM((BLOCKS * IMG, GROUP), F32),
        ],
        compiler_params=vmem_params(),
        name="attend_backward",
    )(seg, counts, tokens, vectors, low_qkv, qkv, grad_attended, grad_resid, lse)


def adam_step(weight, moment, square, grad, factor, rate):
    clipped = grad * factor
    moment_new = beta_first * moment + (1.0 - beta_first) * clipped
    square_new = beta_second * square + (1.0 - beta_second) * clipped * clipped
    first_hat = moment_new / (1.0 - beta_first**STEP)
    second_hat = square_new / (1.0 - beta_second**STEP)
    weight_new = weight - rate * (
        first_hat / (jnp.sqrt(second_hat) + adam_eps) + decay_rate * weight
    )
    return (weight_new, moment_new, square_new)


RATES = (
    2.0 / math.sqrt(D),
    8.0 / math.sqrt(D),
    2.0 / math.sqrt(D),
    2.0 / math.sqrt(FF),
    0.5,
    0.5,
)


MESH = pl.DeviceIdType.MESH
COLS = 4


class Place:
    def __init__(self, planes):
        self.planes = planes
        self.i = lax.axis_index("fsdp")
        self.c = c = lax.axis_index("dp")
        self.q = q = lax.rem(self.i, COLS)
        self.z = self.i // COLS
        x, y = lax.rem(q, 2), q // 2
        self.qx = y * 2 + (1 - x)
        self.qy = (1 - y) * 2 + x
        self.qa = c * self.qx + (1 - c) * self.qy
        self.qb = c * self.qy + (1 - c) * self.qx
        self.qd = COLS - 1 - q
        self.at_a = (self.z * COLS + self.qa, c)
        self.at_b = (self.z * COLS + self.qb, c)
        self.at_x = (self.z * COLS + self.qx, c)
        self.at_y = (self.z * COLS + self.qy, c)
        self.partner = (self.i, 1 - c)

    def plane(self, step):
        return lax.rem(self.z + step, self.planes)

    def along(self, step):
        return (self.plane(step) * COLS + self.q, self.c)

    def greet(self):
        barrier = pltpu.get_barrier_semaphore()
        friends = [self.along(step) for step in range(1, self.planes)]
        friends += [self.at_a, self.at_b, self.partner]
        for device in friends:
            pl.semaphore_signal(barrier, inc=1, device_id=device, device_id_type=MESH)
        pl.semaphore_wait(barrier, len(friends))


def remote(source, target, send, recv, device):
    return pltpu.make_async_remote_copy(
        src_ref=source,
        dst_ref=target,
        send_sem=send,
        recv_sem=recv,
        device_id=device,
        device_id_type=MESH,
    )


class Gather:
    def __init__(self, place, full, send, recv):
        self.full, self.place = full, place
        p, c = place, place.c
        self.first = [
            remote(full.at[p.z, p.q, c], full.at[p.z, p.q, c], send.at[k], recv.at[k], p.along(k + 1))
            for k in range(p.planes - 1)
        ]
        base = p.planes - 1
        moves = [
            (p.q, p.at_a),
            (p.q, p.at_b),
            (p.qa, p.at_b),
            (p.q, p.partner),
            (p.qa, p.partner),
            (p.qb, p.partner),
            (p.qd, p.partner),
        ]
        self.moves = [
            remote(full.at[:, col, c], full.at[:, col, c], send.at[base + k], recv.at[base + k], device)
            for k, (col, device) in enumerate(moves)
        ]

    @staticmethod
    def count(planes):
        return planes + 6

    def begin(self):
        for copy in self.first:
            copy.start()

    def spread(self):
        for copy in self.first:
            copy.wait_recv()
        for k in (0, 1, 3):
            self.moves[k].start()

    def forward(self):
        self.moves[0].wait_recv()
        self.moves[2].start()
        self.moves[4].start()
        self.moves[1].wait_recv()
        self.moves[5].start()

    def last(self):
        self.moves[2].wait_recv()
        self.moves[6].start()

    def arrive(self):
        for k in range(3, 7):
            self.moves[k].wait_recv()

    def drain(self):
        for copy in (*self.first, *self.moves):
            copy.wait_send()


class Scatter:
    def __init__(self, place, total, bufs, result, send, recv):
        self.place, self.total, self.result = place, total, result
        self.out_c, self.in_c, self.out_b, self.in_b = bufs[:4]
        self.out_a, self.in_a, self.out_z, self.in_z = bufs[4:]
        p = place
        self.order = (p.qa, p.qd, p.qb, p.q)
        self.to_core = [
            remote(self.out_c.at[k], self.in_c.at[k], send.at[k], recv.at[k], p.partner)
            for k in range(4)
        ]
        self.to_b = [
            remote(self.out_b.at[k], self.in_b.at[k], send.at[4 + k], recv.at[4 + k], p.at_b)
            for k in range(2)
        ]
        self.to_a = remote(self.out_a, self.in_a, send.at[6], recv.at[6], p.at_a)
        self.to_z = [
            remote(self.out_z.at[k], self.in_z.at[k], send.at[7 + k], recv.at[7 + k], p.along(k + 1))
            for k in range(p.planes - 1)
        ]
        n = 6 + p.planes
        half = result.at[p.c]
        self.to_both = remote(half, half, send.at[n], recv.at[n], p.partner)

    @staticmethod
    def count(planes):
        return planes + 7

    @staticmethod
    def buffers(planes, rows, cols):
        shapes = [(4, planes)] * 2 + [(2, planes)] * 2 + [(planes,)] * 2 + [(planes - 1,)] * 2
        return [pltpu.VMEM((*shape, rows, cols), BF16) for shape in shapes]

    def begin(self):
        for k in range(4):
            self.out_c[k] = self.total[:, self.order[k], 1 - self.place.c].astype(BF16)
            self.to_core[k].start()

    def second(self):
        p = self.place
        for k, col in ((1, p.qd), (0, p.qb)):
            self.to_core[k].wait_recv()
            mine = self.total[:, col, p.c] + self.in_c[k].astype(F32)
            self.out_b[k] = mine.astype(BF16)
            self.to_b[k].start()

    def first(self):
        p = self.place
        self.to_core[2].wait_recv()
        self.to_b[1].wait_recv()
        mine = self.total[:, p.qa, p.c] + self.in_c[2].astype(F32) + self.in_b[1].astype(F32)
        self.out_a[...] = mine.astype(BF16)
        self.to_a.start()

    def planes(self):
        p = self.place
        self.to_core[3].wait_recv()
        self.to_b[0].wait_recv()
        self.to_a.wait_recv()

        def mine(z):
            local = self.total[z, p.q, p.c] + self.in_c[3, z].astype(F32)
            return local + self.in_b[0, z].astype(F32) + self.in_a[z].astype(F32)

        for k in range(p.planes - 1):
            self.out_z[k] = mine(p.plane(k + 1)).astype(BF16)
            self.to_z[k].start()
        self.result[p.c] = mine(p.z)

    def finish(self):
        p = self.place
        for copy in self.to_z:
            copy.wait_recv()
        shard = self.result[p.c]
        for k in range(p.planes - 1):
            shard = shard + self.in_z[k].astype(F32)
        self.result[p.c] = shard
        self.to_both.start()
        square = shard * shard
        lanes = sum(square[:, k : k + 128] for k in range(0, square.shape[1], 128))
        return jnp.sum(lanes.reshape(-1, 8, 128), axis=0)

    def drain(self):
        self.to_both.wait_recv()
        for copy in (*self.to_core, *self.to_b, self.to_a, *self.to_z, self.to_both):
            copy.wait_send()


def sum_over_all(place, part, out, slots, send, recv):
    p = place
    out[0] = part
    slots[p.z] = part
    copies = [
        remote(out.at[0], slots.at[p.z], send.at[k], recv.at[k], p.along(k + 1))
        for k in range(p.planes - 1)
    ]
    for copy in copies:
        copy.start()
    for copy in copies:
        copy.wait_recv()
    total = slots[0]
    for k in range(1, p.planes):
        total = total + slots[k]
    for k, device in enumerate((p.at_x, p.at_y, p.partner)):
        out[1 + k] = total
        n = p.planes - 1 + k
        copy = remote(out.at[1 + k], slots.at[n + 1], send.at[n], recv.at[n], device)
        copy.start()
        copy.wait_recv()
        copies.append(copy)
        total = total + slots[n + 1]
    for copy in copies:
        copy.wait_send()
    return total


def small_shard(place, vectors, up_bias):
    def tile(rows):
        for axis, full in ((1, 128), (0, 8)):
            short = list(rows.shape)
            short[axis] = full - short[axis]
            if short[axis]:
                rows = jnp.concatenate([rows, jnp.zeros(short, F32)], axis=axis)
        return rows

    rows, bias = tile(vectors[...]), tile(up_bias[...])
    half = jnp.where(place.c == 0, rows, bias)
    return jnp.concatenate([half, jnp.zeros((8, 128), F32)], axis=0).astype(BF16)


def gather_kernel(planes, *refs):
    shards, vectors, up_bias = refs[:4], refs[4], refs[5]
    full, all_vectors, all_bias = refs[6:10], refs[10], refs[11]
    small, send, recv = refs[12:]
    p = Place(planes)
    per, long = vectors.shape[1], up_bias.shape[1]
    small[p.z, p.q, p.c] = small_shard(p, vectors, up_bias)
    for shard, target in zip(shards, full):
        target[p.z, p.q, p.c] = shard[p.c].astype(BF16)
    p.greet()
    gathers = [
        Gather(p, ref, send.at[k], recv.at[k]) for k, ref in enumerate((small, *full))
    ]
    for stage in (Gather.begin, Gather.spread, Gather.forward, Gather.last, Gather.arrive):
        for item in gathers:
            stage(item)
    for s in range(planes * COLS):
        rows = small[s // COLS, s % COLS, 0].astype(F32)
        bias = small[s // COLS, s % COLS, 1].astype(F32)
        all_vectors[:, s * per : (s + 1) * per] = rows[:8, :per]
        all_bias[:, s * long : (s + 1) * long] = bias[:1, :long]
    for item in gathers:
        item.drain()


def run_gather(planes, masters):
    shards = [item.reshape(2, item.shape[0] // 2, item.shape[1]) for item in masters[:4]]
    vmem = pl.BlockSpec(memory_space=pltpu.VMEM)
    sems = pltpu.SemaphoreType.DMA((5, Gather.count(planes)))
    full = pl.pallas_call(
        functools.partial(gather_kernel, planes),
        in_specs=[vmem] * 6,
        out_specs=[vmem] * 6,
        out_shape=[shaped((planes, COLS, *item.shape), BF16) for item in shards]
        + [shaped((8, D), F32), shaped((1, FF), F32)],
        scratch_shapes=[pltpu.VMEM((planes, COLS, 2, 16, 128), BF16), sems, sems],
        compiler_params=pltpu.CompilerParams(
            vmem_limit_bytes=60 * 2**20, collective_id=1, has_side_effects=True
        ),
        name="gather_weights",
    )(*shards, masters[4], masters[5].reshape(1, -1))
    return [item.reshape(-1, item.shape[-1]) for item in full[:4]] + list(full[4:])


def scatter_kernel(planes, per, long, *refs):
    totals, early, late, bias = refs[:4], refs[4], refs[5], refs[6]
    results, norm, rest = refs[7:12], refs[12], refs[13:]
    small, rest = rest[0], rest[1:]
    bufs, (send, recv, out, slots, norm_send, norm_recv) = rest[:40], rest[40:]
    p = Place(planes)
    small[...] = jnp.zeros_like(small)
    for s in range(planes * COLS):
        cols = slice(s * per, (s + 1) * per)
        small[s // COLS, s % COLS, 0, 0:8, 0:per] = early[:, cols] + late[:, cols]
        small[s // COLS, s % COLS, 1, 0:1, 0:long] = bias[:, s * long : (s + 1) * long]
    scatters = [
        Scatter(p, total, bufs[8 * k : 8 * k + 8], results[k], send.at[k], recv.at[k])
        for k, total in enumerate((*totals, small))
    ]
    p.greet()
    for stage in (Scatter.begin, Scatter.second, Scatter.first, Scatter.planes):
        for item in scatters:
            stage(item)
    part = scatters[0].finish()
    for item in scatters[1:]:
        part = part + item.finish()
    norm[...] = sum_over_all(p, part, out, slots, norm_send, norm_recv)
    for item in scatters:
        item.drain()


def run_scatter(planes, per, long, totals, early, late, bias):
    halves = [
        item.reshape(planes, COLS, 2, item.shape[0] // (planes * COLS * 2), item.shape[1])
        for item in totals
    ]
    shapes = [item.shape[3:] for item in halves] + [(16, 128)]
    vmem = pl.BlockSpec(memory_space=pltpu.VMEM)
    sems = pltpu.SemaphoreType.DMA((5, Scatter.count(planes)))
    norm_sems = pltpu.SemaphoreType.DMA((planes + 2,))
    scratch = [pltpu.VMEM((planes, COLS, 2, 16, 128), F32)]
    for shape in shapes:
        scratch += Scatter.buffers(planes, *shape)
    scratch += [sems, sems]
    scratch += [pltpu.VMEM((4, 8, 128), F32), pltpu.VMEM((planes + 3, 8, 128), F32)]
    scratch += [norm_sems, norm_sems]
    return pl.pallas_call(
        functools.partial(scatter_kernel, planes, per, long),
        in_specs=[vmem] * 7,
        out_specs=[vmem] * 6,
        out_shape=[shaped((2, *shape), F32) for shape in shapes] + [shaped((8, 128), F32)],
        scratch_shapes=scratch,
        compiler_params=pltpu.CompilerParams(
            vmem_limit_bytes=62 * 2**20, collective_id=2, has_side_effects=True
        ),
        name="scatter_gradients",
    )(*halves, early, late, bias)


def update_kernel(bound, *refs):
    grads, norm = refs[:5], refs[5]
    masters, moments, squares = refs[6:12], refs[12:18], refs[18:24]
    total, fresh = refs[24], refs[25:]
    root = jnp.sqrt(jnp.sum(norm[...], axis=(0, 1), keepdims=True))
    total[...] = root
    factor = jnp.minimum(1.0, bound / root)
    for k in range(6):
        if k < 4:
            grad = grads[k][...]
        elif k == 4:
            grad = grads[4][0, 0:8, 0 : masters[4].shape[1]]
        else:
            grad = grads[4][1, 0:1, 0 : masters[5].shape[1]]
        new = adam_step(
            masters[k][...], moments[k][...], squares[k][...], grad, factor, RATES[k]
        )
        for ref, item in zip((fresh[k], fresh[6 + k], fresh[12 + k]), new):
            ref[...] = item


def run_update(bound, grads, norm, masters, moments, squares):
    def flat(items):
        return [*items[:5], items[5].reshape(1, -1)]

    grads = [item.reshape(-1, item.shape[-1]) for item in grads[:4]] + [grads[4]]
    state = flat(masters) + flat(moments) + flat(squares)
    vmem = pl.BlockSpec(memory_space=pltpu.VMEM)
    done = pl.pallas_call(
        functools.partial(update_kernel, bound),
        in_specs=[vmem] * 24,
        out_specs=[vmem] * 19,
        out_shape=[shaped((1, 1), F32)] + [shaped(item.shape, F32) for item in state],
        compiler_params=vmem_params(),
        name="update_state",
    )(*grads, norm, *state)
    fresh = [item.reshape(-1) if k % 6 == 5 else item for k, item in enumerate(done[1:])]
    return [done[0].reshape(()), *fresh]


def compute(tokens, cotangent, segment_ids, valid_counts, full):
    low_qkv, low_out, low_up, low_down, vectors, up_bias = full
    qkv, attended, lse = run_forward(segment_ids, valid_counts, tokens, vectors, low_qkv)
    (
        layer_out,
        grad_resid,
        grad_attended,
        grad_down,
        grad_up,
        grad_out_w,
        late,
        grad_bias,
    ) = run_feed(
        valid_counts, tokens, cotangent, attended, vectors, up_bias, low_out, low_up, low_down
    )
    token_grad, grad_qkv_w, early = run_backward(
        segment_ids,
        valid_counts,
        tokens,
        vectors,
        low_qkv,
        qkv,
        grad_attended,
        grad_resid,
        lse,
    )
    return layer_out, token_grad, (grad_qkv_w, grad_out_w, grad_up, grad_down), early, late, grad_bias


def fast_body(tokens, cotangent, segment_ids, valid_counts, *state):
    masters, moments, squares = state[:6], state[6:12], state[12:18]
    wide = lax.axis_size("fsdp")
    planes = wide // COLS
    full = run_gather(planes, masters)
    layer_out, token_grad, totals, early, late, bias = compute(
        tokens, cotangent, segment_ids, valid_counts, full
    )
    *grads, norm = run_scatter(planes, D // wide, FF // wide, totals, early, late, bias)
    bound = 0.005 * math.sqrt(tokens.shape[0] * wide * lax.axis_size("dp") * PARAMS)
    return (layer_out, token_grad, *run_update(bound, grads, norm, masters, moments, squares))


def plain_body(tokens, cotangent, segment_ids, valid_counts, *state):
    masters, moments, squares = state[:6], state[6:12], state[12:18]
    wide = lax.axis_size("fsdp")
    replicas = lax.axis_size("dp")
    low = [item.astype(BF16) for item in masters]
    full = [
        lax.all_gather(item, "fsdp", axis=1 if k == 4 else 0, tiled=True)
        for k, item in enumerate(low)
    ]
    full[4] = full[4].astype(F32)
    full[5] = full[5].astype(F32).reshape(1, FF)
    layer_out, token_grad, totals, early, late, bias = compute(
        tokens, cotangent, segment_ids, valid_counts, full
    )
    grads = []
    for k, item in enumerate((*totals, early + late, bias.reshape(FF))):
        shard = lax.psum_scatter(item, "fsdp", scatter_dimension=1 if k == 4 else 0, tiled=True)
        grads.append(lax.psum(shard.astype(BF16), "dp").astype(F32))
    local_total = jnp.sum(grads[0] * grads[0])
    for item in grads[1:]:
        local_total = local_total + jnp.sum(item * item)
    grad_norm = jnp.sqrt(lax.psum(local_total, "fsdp"))
    bound = 0.005 * math.sqrt(tokens.shape[0] * wide * replicas * PARAMS)
    factor = jnp.minimum(1.0, bound / grad_norm)
    fresh = [
        adam_step(masters[k], moments[k], squares[k], grads[k], factor, RATES[k]) for k in range(6)
    ]
    return (
        layer_out,
        token_grad,
        grad_norm,
        *(item[0] for item in fresh),
        *(item[1] for item in fresh),
        *(item[2] for item in fresh),
    )


def solution(mesh):
    rows = P(("fsdp", "dp"), None)
    state = (
        P("fsdp", None),
        P("fsdp", None),
        P("fsdp", None),
        P("fsdp", None),
        P(None, "fsdp"),
        P("fsdp"),
    )
    wide, replicas = mesh.shape["fsdp"], mesh.shape["dp"]
    fits = replicas == 2 and wide % COLS == 0 and D % (32 * wide) == 0
    return jax.shard_map(
        fast_body if fits else plain_body,
        mesh=mesh,
        in_specs=(rows, rows, rows, P(("fsdp", "dp")), *state, *state, *state),
        out_specs=(rows, rows, P(), *state, *state, *state),
        check_vma=False,
    )
```

```python
import functools
import math

import jax
import jax.numpy as jnp
from jax import lax
from jax.experimental import pallas as pl
from jax.experimental.pallas import tpu as pltpu
from jax.sharding import PartitionSpec as P

D = 512
HEADS = 8
HEAD_DIM = 64
FF = 2048
SEQ = 1024
IMG = 192
BLOCKS = 5
STEP = 5
PARAMS = 3151872
GROUP = 256
PER_GROUP = GROUP // HEAD_DIM

F32 = jnp.float32
BF16 = jnp.bfloat16

norm_eps = 1e-06
adam_eps = 1e-08
decay_rate = 0.05
beta_first = 0.5
beta_second = 0.5
masked_score = -1e30


def dot(left, right):
    return lax.dot_general(left, right, (((1,), (0,)), ((), ())), preferred_element_type=F32)


def dot_nt(left, right):
    return lax.dot_general(left, right, (((1,), (1,)), ((), ())), preferred_element_type=F32)


def dot_tn(left, right):
    return lax.dot_general(left, right, (((0,), (0,)), ((), ())), preferred_element_type=F32)


def norm_forward(values, gain, shift):
    center = values - jnp.mean(values, axis=-1, keepdims=True)
    spread = lax.rsqrt(jnp.mean(center * center, axis=-1, keepdims=True) + norm_eps)
    hat = center * spread
    return hat * gain + shift, hat, spread


def norm_backward(incoming, hat, spread, gain):
    scaled = incoming * gain
    return spread * (
        scaled
        - jnp.mean(scaled, axis=-1, keepdims=True)
        - hat * jnp.mean(scaled * hat, axis=-1, keepdims=True)
    )


def gelu_pair(values):
    half = 0.5 * (1.0 + lax.erf(values * (1.0 / math.sqrt(2.0))))
    bell = jnp.exp(-0.5 * values * values) * (1.0 / math.sqrt(2.0 * math.pi))
    return values * half, half + values * bell


def col_sum(values):
    return jnp.sum(values, axis=0, keepdims=True)


def head_of_lane():
    return lax.broadcasted_iota(jnp.int32, (1, GROUP), 1) // HEAD_DIM


def stack_heads(rows):
    head = head_of_lane()
    zero = jnp.zeros_like(rows)
    return jnp.concatenate([jnp.where(head == h, rows, zero) for h in range(PER_GROUP)], axis=0)


def unstack_heads(stacked):
    head = head_of_lane()
    n = stacked.shape[0] // PER_GROUP
    rows = stacked[(PER_GROUP - 1) * n :]
    for h in range(PER_GROUP - 2, -1, -1):
        rows = jnp.where(head == h, stacked[h * n : (h + 1) * n], rows)
    return rows


def links(seg, counts, s):
    return [
        (seg[s, b * IMG] == seg[s, (b + 1) * IMG]) & ((b + 1) * IMG < counts[s])
        for b in range(BLOCKS - 1)
    ]


def neighbour(b, linked):
    below = slice((b + 1) * IMG, (b + 2) * IMG) if b < BLOCKS - 1 else None
    above = slice((b - 1) * IMG, b * IMG) if b > 0 else None
    with_below = linked[b] if b < BLOCKS - 1 else jnp.bool_(False)
    with_above = linked[b - 1] if b > 0 else jnp.bool_(False)
    offset = jnp.where(with_below | with_above, 0.0, masked_score)
    return below, above, with_below, with_above, offset


def other_rows(ref, cols, below, above, with_below):
    if above is None:
        return ref[below, cols]
    if below is None:
        return ref[above, cols]
    return jnp.where(with_below, ref[below, cols], ref[above, cols])


def attend_block(query, keys, values, offset):
    stacked = stack_heads(query * jnp.asarray(HEAD_DIM**-0.5, BF16))
    scores = dot_nt(keys, stacked)
    own, other = scores[:IMG], scores[IMG:]
    top = jnp.maximum(
        jnp.max(own, axis=0, keepdims=True), jnp.max(other, axis=0, keepdims=True) + offset
    )
    own = jnp.exp(own - top)
    other = jnp.exp(other - (top - offset))
    total = col_sum(own) + col_sum(other)
    inverse = 1.0 / total
    probs = jnp.concatenate([own * inverse, other * inverse], axis=0).astype(BF16)
    return unstack_heads(dot_tn(probs, values)), top + jnp.log(total)


def attend_block_backward(query, keys, values, grad, lse, offset):
    stacked = stack_heads(query * jnp.asarray(HEAD_DIM**-0.5, BF16))
    grads = stack_heads(grad)
    scores = dot_nt(keys, stacked)
    grad_probs = dot_nt(values, grads)
    own = jnp.exp(scores[:IMG] - lse)
    other = jnp.exp(scores[IMG:] - (lse - offset))
    own_t = own * grad_probs[:IMG]
    other_t = other * grad_probs[IMG:]
    delta = col_sum(own_t) + col_sum(other_t)
    grad_scores = jnp.concatenate([own_t - own * delta, other_t - other * delta], axis=0)
    grad_scores = grad_scores.astype(BF16)
    probs = jnp.concatenate([own, other], axis=0).astype(BF16)
    grad_values = dot(probs, grads)
    grad_keys = dot(grad_scores, stacked)
    grad_query = unstack_heads(dot_tn(grad_scores, keys)) * (HEAD_DIM**-0.5)
    return grad_query, grad_keys, grad_values


def forward_kernel(chunk, seg, counts, tokens, vectors, low_qkv, qkv, attended, lse):
    s = pl.program_id(0)
    bias = jnp.concatenate([vectors[2:3, :], jnp.zeros((1, D), F32), vectors[3:4, :]], axis=1)
    for c in range(SEQ // chunk):
        rows = slice(c * chunk, (c + 1) * chunk)
        normed, _, _ = norm_forward(tokens[rows, :].astype(F32), vectors[0:1, :], vectors[1:2, :])
        qkv[rows, :] = (dot(normed.astype(BF16), low_qkv[...]) + bias).astype(BF16)
    linked = links(seg, counts, s)
    for g in range(D // GROUP):
        query_cols, key_cols, value_cols = [
            slice(j * D + g * GROUP, j * D + (g + 1) * GROUP) for j in range(3)
        ]
        out_cols = slice(g * GROUP, (g + 1) * GROUP)
        for b in range(BLOCKS):
            rows = slice(b * IMG, (b + 1) * IMG)
            below, above, with_below, with_above, offset = neighbour(b, linked)
            keys = jnp.concatenate(
                [qkv[rows, key_cols], other_rows(qkv, key_cols, below, above, with_below)], axis=0
            )
            own_values = qkv[rows, value_cols]
            values = jnp.concatenate(
                [own_values, other_rows(qkv, value_cols, below, above, with_below)], axis=0
            )
            mixed, block_lse = attend_block(qkv[rows, query_cols], keys, values, offset)
            mixed = mixed.astype(BF16)
            if b == BLOCKS - 1:
                mixed = jnp.where(b * IMG >= counts[s], own_values, mixed)
            attended[rows, out_cols] = mixed
            lse[g * BLOCKS + b] = block_lse
        attended[BLOCKS * IMG :, out_cols] = qkv[BLOCKS * IMG :, value_cols]


def feed_kernel(
    rows_in,
    chunk,
    counts,
    tokens,
    cotangent,
    attended,
    vectors,
    up_bias,
    low_out,
    low_up,
    low_down,
    layer_out,
    grad_resid,
    grad_attended,
    grad_down,
    grad_up,
    grad_out_w,
    grad_vectors,
    grad_bias,
):
    i = pl.program_id(0)

    @pl.when(i == 0)
    def _():
        for ref in (grad_down, grad_up, grad_out_w, grad_vectors, grad_bias):
            ref[...] = jnp.zeros_like(ref)

    per = SEQ // rows_in
    mixed = attended[...]
    resid = tokens[...].astype(F32) + (dot(mixed, low_out[...]) + vectors[4:5, :])
    normed, hat, spread = norm_forward(resid, vectors[5:6, :], vectors[6:7, :])
    low_two = normed.astype(BF16)
    position = (i % per) * rows_in + lax.broadcasted_iota(jnp.int32, (rows_in, 1), 0)
    grad = jnp.where(position < counts[i // per], cotangent[...].astype(F32), 0.0)
    grad_low = grad.astype(BF16)
    out = jnp.zeros((rows_in, D), F32)
    grad_two = jnp.zeros((rows_in, D), F32)
    for c in range(FF // chunk):
        cols = slice(c * chunk, (c + 1) * chunk)
        hidden = dot(low_two, low_up[:, cols]) + up_bias[:, cols]
        grad_active = dot_nt(grad_low, low_down[cols, :])
        active, slope = gelu_pair(hidden)
        active = active.astype(BF16)
        grad_hidden = grad_active * slope
        grad_hidden_low = grad_hidden.astype(BF16)
        out += dot(active, low_down[cols, :])
        grad_bias[:, cols] += col_sum(grad_hidden)
        grad_down[cols, :] += dot_tn(active, grad_low)
        grad_up[:, cols] += dot_tn(low_two, grad_hidden_low)
        grad_two += dot_nt(grad_hidden_low, low_up[:, cols])
    layer_out[...] = (resid + (out + vectors[7:8, :])).astype(BF16)
    back = grad + norm_backward(grad_two, hat, spread, vectors[5:6, :])
    back_low = back.astype(BF16)
    grad_resid[...] = back
    grad_out_w[...] += dot_tn(mixed, back_low)
    grad_attended[...] = dot_nt(back_low, low_out[...]).astype(BF16)
    grad_vectors[4:5, :] += col_sum(back)
    grad_vectors[5:6, :] += col_sum(grad_two * hat)
    grad_vectors[6:7, :] += col_sum(grad_two)
    grad_vectors[7:8, :] += col_sum(grad)


def backward_kernel(
    chunk,
    seg,
    counts,
    tokens,
    vectors,
    low_qkv,
    qkv,
    grad_attended,
    grad_resid,
    lse,
    token_grad,
    grad_qkv_w,
    grad_vectors,
    grad_qkv,
    key_sum,
    value_sum,
):
    s = pl.program_id(0)

    @pl.when(s == 0)
    def _():
        grad_qkv_w[...] = jnp.zeros_like(grad_qkv_w)
        grad_vectors[...] = jnp.zeros_like(grad_vectors)

    linked = links(seg, counts, s)
    padded = (BLOCKS - 1) * IMG >= counts[s]
    covered = slice(0, BLOCKS * IMG)
    tail = slice(BLOCKS * IMG, SEQ)
    for g in range(D // GROUP):
        query_cols, key_cols, value_cols = [
            slice(j * D + g * GROUP, j * D + (g + 1) * GROUP) for j in range(3)
        ]
        grad_cols = slice(g * GROUP, (g + 1) * GROUP)
        query_bias = jnp.zeros((1, GROUP), F32)
        for b in range(BLOCKS):
            rows = slice(b * IMG, (b + 1) * IMG)
            below, above, with_below, with_above, offset = neighbour(b, linked)
            keys = jnp.concatenate(
                [qkv[rows, key_cols], other_rows(qkv, key_cols, below, above, with_below)], axis=0
            )
            values = jnp.concatenate(
                [qkv[rows, value_cols], other_rows(qkv, value_cols, below, above, with_below)],
                axis=0,
            )
            grad = grad_attended[rows, grad_cols]
            grad_query, grad_keys, grad_values = attend_block_backward(
                qkv[rows, query_cols], keys, values, grad, lse[g * BLOCKS + b], offset
            )
            own_keys, own_values = grad_keys[:IMG], grad_values[:IMG]
            if b == BLOCKS - 1:
                grad_query = jnp.where(padded, 0.0, grad_query)
                own_keys = jnp.where(padded, 0.0, own_keys)
                own_values = jnp.where(padded, grad.astype(F32), own_values)
            query_bias += col_sum(grad_query)
            grad_qkv[rows, query_cols] = grad_query.astype(BF16)
            if b > 0:
                own_keys += jnp.where(with_above, key_sum[rows, :], 0.0)
                own_values += jnp.where(with_above, value_sum[rows, :], 0.0)
            key_sum[rows, :] = own_keys
            value_sum[rows, :] = own_values
            if below is not None:
                key_sum[below, :] = grad_keys[IMG:]
                value_sum[below, :] = grad_values[IMG:]
            if above is not None:
                key_sum[above, :] += jnp.where(with_above, grad_keys[IMG:], 0.0)
                value_sum[above, :] += jnp.where(with_above, grad_values[IMG:], 0.0)
        grad_tail = grad_attended[tail, grad_cols]
        grad_qkv[tail, query_cols] = jnp.zeros_like(grad_tail)
        grad_qkv[tail, key_cols] = jnp.zeros_like(grad_tail)
        grad_qkv[tail, value_cols] = grad_tail
        grad_qkv[covered, key_cols] = key_sum[...].astype(BF16)
        all_values = value_sum[...]
        grad_qkv[covered, value_cols] = all_values.astype(BF16)
        grad_vectors[2:3, grad_cols] += query_bias
        grad_vectors[3:4, grad_cols] += col_sum(all_values) + col_sum(grad_tail.astype(F32))
    for c in range(SEQ // chunk):
        rows = slice(c * chunk, (c + 1) * chunk)
        normed, hat, spread = norm_forward(
            tokens[rows, :].astype(F32), vectors[0:1, :], vectors[1:2, :]
        )
        grad = grad_qkv[rows, :]
        grad_qkv_w[...] += dot_tn(normed.astype(BF16), grad)
        grad_one = dot_nt(grad, low_qkv[...])
        token_grad[rows, :] = grad_resid[rows, :] + norm_backward(
            grad_one, hat, spread, vectors[0:1, :]
        )
        grad_vectors[0:1, :] += col_sum(grad_one * hat)
        grad_vectors[1:2, :] += col_sum(grad_one)


def vmem_params():
    return pltpu.CompilerParams(vmem_limit_bytes=60 * 2**20)


def by_rows(rows, cols):
    return pl.BlockSpec((rows, cols), lambda i: (i, 0))


def whole(*shape):
    return pl.BlockSpec(shape, lambda i: (0,) * len(shape))


def stats_spec():
    return pl.BlockSpec((2 * BLOCKS, 1, PER_GROUP * IMG), lambda i: (i, 0, 0))


def shaped(shape, dtype):
    return jax.ShapeDtypeStruct(shape, dtype)


SCALAR = pl.BlockSpec(memory_space=pltpu.SMEM)


def run_forward(seg, counts, tokens, vectors, low_qkv):
    rows = tokens.shape[0]
    seqs = rows // SEQ
    return pl.pallas_call(
        functools.partial(forward_kernel, 256),
        grid=(seqs,),
        in_specs=[SCALAR, SCALAR, by_rows(SEQ, D), whole(8, D), whole(D, 3 * D)],
        out_specs=[by_rows(SEQ, 3 * D), by_rows(SEQ, D), stats_spec()],
        out_shape=[
            shaped((rows, 3 * D), BF16),
            shaped((rows, D), BF16),
            shaped((seqs * 2 * BLOCKS, 1, PER_GROUP * IMG), F32),
        ],
        compiler_params=vmem_params(),
        name="attend_forward",
    )(seg, counts, tokens, vectors, low_qkv)


def run_feed(counts, tokens, cotangent, attended, vectors, up_bias, low_out, low_up, low_down):
    rows = tokens.shape[0]
    step = 512
    return pl.pallas_call(
        functools.partial(feed_kernel, step, 512),
        grid=(rows // step,),
        in_specs=[
            SCALAR,
            by_rows(step, D),
            by_rows(step, D),
            by_rows(step, D),
            whole(8, D),
            whole(1, FF),
            whole(D, D),
            whole(D, FF),
            whole(FF, D),
        ],
        out_specs=[
            by_rows(step, D),
            by_rows(step, D),
            by_rows(step, D),
            whole(FF, D),
            whole(D, FF),
            whole(D, D),
            whole(8, D),
            whole(1, FF),
        ],
        out_shape=[
            shaped((rows, D), BF16),
            shaped((rows, D), F32),
            shaped((rows, D), BF16),
            shaped((FF, D), F32),
            shaped((D, FF), F32),
            shaped((D, D), F32),
            shaped((8, D), F32),
            shaped((1, FF), F32),
        ],
        compiler_params=vmem_params(),
        name="feed_forward",
    )(counts, tokens, cotangent, attended, vectors, up_bias, low_out, low_up, low_down)


def run_backward(seg, counts, tokens, vectors, low_qkv, qkv, grad_attended, grad_resid, lse):
    rows = tokens.shape[0]
    return pl.pallas_call(
        functools.partial(backward_kernel, 512),
        grid=(rows // SEQ,),
        in_specs=[
            SCALAR,
            SCALAR,
            by_rows(SEQ, D),
            whole(8, D),
            whole(D, 3 * D),
            by_rows(SEQ, 3 * D),
            by_rows(SEQ, D),
            by_rows(SEQ, D),
            stats_spec(),
        ],
        out_specs=[by_rows(SEQ, D), whole(D, 3 * D), whole(8, D)],
        out_shape=[
            shaped((rows, D), F32),
            shaped((D, 3 * D), F32),
            shaped((8, D), F32),
        ],
        scratch_shapes=[
            pltpu.VMEM((SEQ, 3 * D), BF16),
            pltpu.VMEM((BLOCKS * IMG, GROUP), F32),
            pltpu.VMEM((BLOCKS * IMG, GROUP), F32),
        ],
        compiler_params=vmem_params(),
        name="attend_backward",
    )(seg, counts, tokens, vectors, low_qkv, qkv, grad_attended, grad_resid, lse)


def adam_step(weight, moment, square, grad, factor, rate):
    clipped = grad * factor
    moment_new = beta_first * moment + (1.0 - beta_first) * clipped
    square_new = beta_second * square + (1.0 - beta_second) * clipped * clipped
    first_hat = moment_new / (1.0 - beta_first**STEP)
    second_hat = square_new / (1.0 - beta_second**STEP)
    weight_new = weight - rate * (
        first_hat / (jnp.sqrt(second_hat) + adam_eps) + decay_rate * weight
    )
    return (weight_new, moment_new, square_new)


RATES = (
    2.0 / math.sqrt(D),
    8.0 / math.sqrt(D),
    2.0 / math.sqrt(D),
    2.0 / math.sqrt(FF),
    0.5,
    0.5,
)


MESH = pl.DeviceIdType.MESH
COLS = 4


class Place:
    def __init__(self, planes):
        self.planes = planes
        self.i = lax.axis_index("fsdp")
        self.c = c = lax.axis_index("dp")
        self.q = q = lax.rem(self.i, COLS)
        self.z = self.i // COLS
        x, y = lax.rem(q, 2), q // 2
        self.qx = y * 2 + (1 - x)
        self.qy = (1 - y) * 2 + x
        self.qa = c * self.qx + (1 - c) * self.qy
        self.qb = c * self.qy + (1 - c) * self.qx
        self.qd = COLS - 1 - q
        self.at_a = (self.z * COLS + self.qa, c)
        self.at_b = (self.z * COLS + self.qb, c)
        self.at_x = (self.z * COLS + self.qx, c)
        self.at_y = (self.z * COLS + self.qy, c)
        self.partner = (self.i, 1 - c)

    def plane(self, step):
        return lax.rem(self.z + step, self.planes)

    def along(self, step):
        return (self.plane(step) * COLS + self.q, self.c)

    def greet(self):
        barrier = pltpu.get_barrier_semaphore()
        friends = [self.along(step) for step in range(1, self.planes)]
        friends += [self.at_a, self.at_b, self.partner]
        for device in friends:
            pl.semaphore_signal(barrier, inc=1, device_id=device, device_id_type=MESH)
        pl.semaphore_wait(barrier, len(friends))


def remote(source, target, send, recv, device):
    return pltpu.make_async_remote_copy(
        src_ref=source,
        dst_ref=target,
        send_sem=send,
        recv_sem=recv,
        device_id=device,
        device_id_type=MESH,
    )


class Gather:
    def __init__(self, place, full, send, recv):
        self.full, self.place = full, place
        p, c = place, place.c
        self.first = [
            remote(full.at[p.z, p.q, c], full.at[p.z, p.q, c], send.at[k], recv.at[k], p.along(k + 1))
            for k in range(p.planes - 1)
        ]
        base = p.planes - 1
        moves = [
            (p.q, p.at_a),
            (p.q, p.at_b),
            (p.qa, p.at_b),
            (p.q, p.partner),
            (p.qa, p.partner),
            (p.qb, p.partner),
            (p.qd, p.partner),
        ]
        self.moves = [
            remote(full.at[:, col, c], full.at[:, col, c], send.at[base + k], recv.at[base + k], device)
            for k, (col, device) in enumerate(moves)
        ]

    @staticmethod
    def count(planes):
        return planes + 6

    def begin(self):
        for copy in self.first:
            copy.start()

    def spread(self):
        for copy in self.first:
            copy.wait_recv()
        for k in (0, 1, 3):
            self.moves[k].start()

    def forward(self):
        self.moves[0].wait_recv()
        self.moves[2].start()
        self.moves[4].start()
        self.moves[1].wait_recv()
        self.moves[5].start()

    def last(self):
        self.moves[2].wait_recv()
        self.moves[6].start()

    def arrive(self):
        for k in range(3, 7):
            self.moves[k].wait_recv()

    def drain(self):
        for copy in (*self.first, *self.moves):
            copy.wait_send()


class Scatter:
    def __init__(self, place, total, bufs, result, send, recv):
        self.place, self.total, self.result = place, total, result
        self.in_c, self.out_b, self.in_b = bufs[:3]
        self.out_a, self.in_a, self.out_z, self.in_z = bufs[3:7]
        self.out_c = bufs[7]
        p = place
        self.order = (p.qa, p.qd, p.qb, p.q)
        self.to_core = [
            remote(self.out_c.at[k], self.in_c.at[k], send.at[k], recv.at[k], p.partner)
            for k in range(4)
        ]
        self.to_b = [
            remote(self.out_b.at[k], self.in_b.at[k], send.at[4 + k], recv.at[4 + k], p.at_b)
            for k in range(2)
        ]
        self.to_a = remote(self.out_a, self.in_a, send.at[6], recv.at[6], p.at_a)
        self.to_z = [
            remote(self.out_z.at[k], self.in_z.at[k], send.at[7 + k], recv.at[7 + k], p.along(k + 1))
            for k in range(p.planes - 1)
        ]
        n = 6 + p.planes
        half = result.at[p.c]
        self.to_both = remote(half, half, send.at[n], recv.at[n], p.partner)

    @staticmethod
    def count(planes):
        return planes + 7

    @staticmethod
    def buffers(planes, rows, cols, own=True):
        shapes = [(4, planes)] + [(2, planes)] * 2 + [(planes,)] * 2 + [(planes - 1,)] * 2
        shapes += [(4, planes)] if own else []
        return [pltpu.VMEM((*shape, rows, cols), BF16) for shape in shapes]

    def begin(self):
        for k in range(4):
            self.out_c[k] = self.total[:, self.order[k], 1 - self.place.c].astype(BF16)
            self.to_core[k].start()

    def second(self):
        p = self.place
        for k, col in ((1, p.qd), (0, p.qb)):
            self.to_core[k].wait_recv()
            mine = self.total[:, col, p.c] + self.in_c[k].astype(F32)
            self.out_b[k] = mine.astype(BF16)
            self.to_b[k].start()

    def first(self):
        p = self.place
        self.to_core[2].wait_recv()
        self.to_b[1].wait_recv()
        mine = self.total[:, p.qa, p.c] + self.in_c[2].astype(F32) + self.in_b[1].astype(F32)
        self.out_a[...] = mine.astype(BF16)
        self.to_a.start()

    def planes(self):
        p = self.place
        self.to_core[3].wait_recv()
        self.to_b[0].wait_recv()
        self.to_a.wait_recv()

        def mine(z):
            local = self.total[z, p.q, p.c] + self.in_c[3, z].astype(F32)
            return local + self.in_b[0, z].astype(F32) + self.in_a[z].astype(F32)

        for k in range(p.planes - 1):
            self.out_z[k] = mine(p.plane(k + 1)).astype(BF16)
            self.to_z[k].start()
        self.result[p.c] = mine(p.z)

    def finish(self):
        p = self.place
        for copy in self.to_z:
            copy.wait_recv()
        shard = self.result[p.c]
        for k in range(p.planes - 1):
            shard = shard + self.in_z[k].astype(F32)
        self.result[p.c] = shard
        self.to_both.start()
        square = shard * shard
        lanes = sum(square[:, k : k + 128] for k in range(0, square.shape[1], 128))
        return jnp.sum(lanes.reshape(-1, 8, 128), axis=0)

    def drain(self):
        self.to_both.wait_recv()
        for copy in (*self.to_core, *self.to_b, self.to_a, *self.to_z, self.to_both):
            copy.wait_send()


def sum_over_all(place, part, out, slots, send, recv):
    p = place
    out[0] = part
    slots[p.z] = part
    copies = [
        remote(out.at[0], slots.at[p.z], send.at[k], recv.at[k], p.along(k + 1))
        for k in range(p.planes - 1)
    ]
    for copy in copies:
        copy.start()
    for copy in copies:
        copy.wait_recv()
    total = slots[0]
    for k in range(1, p.planes):
        total = total + slots[k]
    for k, device in enumerate((p.at_x, p.at_y, p.partner)):
        out[1 + k] = total
        n = p.planes - 1 + k
        copy = remote(out.at[1 + k], slots.at[n + 1], send.at[n], recv.at[n], device)
        copy.start()
        copy.wait_recv()
        copies.append(copy)
        total = total + slots[n + 1]
    for copy in copies:
        copy.wait_send()
    return total


def small_shard(place, vectors, up_bias):
    def tile(rows):
        for axis, full in ((1, 128), (0, 8)):
            short = list(rows.shape)
            short[axis] = full - short[axis]
            if short[axis]:
                rows = jnp.concatenate([rows, jnp.zeros(short, F32)], axis=axis)
        return rows

    rows, bias = tile(vectors[...]), tile(up_bias[...])
    half = jnp.where(place.c == 0, rows, bias)
    return jnp.concatenate([half, jnp.zeros((8, 128), F32)], axis=0).astype(BF16)


ROWS = 512
SPAN = SEQ // IMG * IMG


def five(planes, rows, cols):
    return (planes, COLS, 2, rows, cols)


def flat(value):
    return value.reshape(-1, value.shape[-1])


def layer_kernel(planes, per, long, *refs):
    seg, counts, tokens, cotangent = refs[:4]
    shards, vector_shard, bias_shard = refs[4:8], refs[8], refs[9]
    layer_out, token_grad = refs[10:12]
    results, first_rows, norm, kept = refs[12:18], refs[18], refs[19], refs[20]
    full, small, vectors, up_bias = refs[21:25], refs[25], refs[26], refs[27]
    totals = refs[28:34]
    tok, cot, qkv, mixed, resid, lse, key_sum, value_sum = refs[34:42]
    grad_vectors, grad_bias = refs[42:44]
    bufs = refs[44:89]
    g_send, g_recv, s_send, s_recv = refs[89:93]
    out_tiles, in_tiles, t_send, t_recv, load_sem, out_sem, grad_sem = refs[93:100]
    full_qkv, full_out, full_up, full_down = full
    sum_out, sum_up, sum_down, sum_low, sum_high, sum_small = totals
    p = Place(planes)
    rows_local = tok.shape[0]
    seqs = rows_local // SEQ

    low_one = cot
    load_tokens = pltpu.make_async_copy(tokens, tok, load_sem.at[0])
    load_cotangent = pltpu.make_async_copy(cotangent, cot, load_sem.at[1])
    keep_low = pltpu.make_async_copy(low_one, kept, load_sem.at[2])
    recall_low = pltpu.make_async_copy(kept, low_one, load_sem.at[3])
    load_tokens.start()

    small[p.z, p.q, p.c] = small_shard(p, vector_shard, bias_shard)
    for shard, target in zip(shards, full):
        target[p.z, p.q, p.c] = shard[p.c].astype(BF16)
    p.greet()
    g_small, g_qkv, g_out, g_up, g_down = gathers = [
        Gather(p, ref, g_send.at[k], g_recv.at[k]) for k, ref in enumerate((small, *full))
    ]
    spare = [ref.at[:, :, 0] for ref in full[1:]]
    bufs = [[*bufs[7 * k : 7 * k + 7], spare[k]] for k in range(3)] + [
        bufs[21 + 8 * k : 29 + 8 * k] for k in range(3)
    ]
    scatters = [
        Scatter(p, total, bufs[k], results[k], s_send.at[k], s_recv.at[k])
        for k, total in enumerate(totals)
    ]
    s_out, s_up, s_down, s_low, s_high, s_small = scatters
    for item in gathers:
        item.begin()
    g_small.spread()
    g_qkv.spread()
    g_small.forward()
    g_qkv.forward()
    g_small.last()
    g_out.spread()
    g_qkv.last()
    g_small.arrive()
    for s in range(planes * COLS):
        rows = small[s // COLS, s % COLS, 0].astype(F32)
        bias = small[s // COLS, s % COLS, 1].astype(F32)
        vectors[:, s * per : (s + 1) * per] = rows[:8, :per]
        up_bias[:, s * long : (s + 1) * long] = bias[:1, :long]
    load_tokens.wait()
    g_up.spread()
    g_qkv.arrive()

    qkv_bias = jnp.concatenate([vectors[2:3, :], jnp.zeros((1, D), F32), vectors[3:4, :]], axis=1)
    chunk = 256
    beside_qkv = {
        1: [g_out.forward],
        2: [g_down.spread],
        3: [g_out.last],
        4: [g_up.forward],
        6: [g_up.last],
        7: [g_down.forward],
    }
    for k in range(rows_local // chunk):
        rows = slice(k * chunk, (k + 1) * chunk)
        normed, _, _ = norm_forward(tok[rows, :].astype(F32), vectors[0:1, :], vectors[1:2, :])
        low = normed.astype(BF16)
        low_one[rows, :] = low
        qkv[rows, :] = (dot(low, flat(full_qkv[...])) + qkv_bias).astype(BF16)
        for stage in beside_qkv.get(k, ()):
            stage()
    keep_low.start()

    def block_rows(s, b):
        return pl.ds(pl.multiple_of(s * SEQ + b * IMG, 64), IMG)

    def tail_rows(s):
        return pl.ds(pl.multiple_of(s * SEQ + SPAN, 64), SEQ - SPAN)

    def columns(g):
        return [slice(j * D + g * GROUP, j * D + (g + 1) * GROUP) for j in range(3)]

    def with_other(cols, s, b, with_below):
        own = qkv[block_rows(s, b), cols]
        if b == 0:
            other = qkv[block_rows(s, 1), cols]
        elif b == BLOCKS - 1:
            other = qkv[block_rows(s, b - 1), cols]
        else:
            other = jnp.where(
                with_below, qkv[block_rows(s, b + 1), cols], qkv[block_rows(s, b - 1), cols]
            )
        return jnp.concatenate([own, other], axis=0)

    for g in range(D // GROUP):
        query_cols, key_cols, value_cols = columns(g)
        own_cols = slice(g * GROUP, (g + 1) * GROUP)

        def attend(s, carry):
            linked = links(seg, counts, s)
            for b in range(BLOCKS):
                _, _, with_below, _, offset = neighbour(b, linked)
                keys = with_other(key_cols, s, b, with_below)
                values = with_other(value_cols, s, b, with_below)
                block, block_lse = attend_block(
                    qkv[block_rows(s, b), query_cols], keys, values, offset
                )
                block = block.astype(BF16)
                if b == BLOCKS - 1:
                    block = jnp.where(b * IMG >= counts[s], values[:IMG], block)
                mixed[block_rows(s, b), own_cols] = block
                lse[(s * 2 + g) * BLOCKS + b] = block_lse
            mixed[tail_rows(s), own_cols] = qkv[tail_rows(s), value_cols]
            return carry

        lax.fori_loop(0, seqs, attend, 0)
        if g == 0:
            g_down.last()
            keep_low.wait()
            load_cotangent.start()

    for item in (g_out, g_up, g_down):
        item.arrive()
    load_cotangent.wait()

    for ref in (sum_out, sum_up, sum_down, sum_small, grad_vectors, grad_bias):
        ref[...] = jnp.zeros_like(ref)
    width = FF // planes

    def feed(i, carry):
        rows = pl.ds(pl.multiple_of(i * ROWS, ROWS), ROWS)
        block = mixed[rows, :]
        low_out = flat(full_out[...])
        res = tok[rows, :].astype(F32) + (dot(block, low_out) + vectors[4:5, :])
        normed, hat, spread = norm_forward(res, vectors[5:6, :], vectors[6:7, :])
        low_two = normed.astype(BF16)
        position = (i % (SEQ // ROWS)) * ROWS + lax.broadcasted_iota(jnp.int32, (ROWS, 1), 0)
        grad = jnp.where(position < counts[i // (SEQ // ROWS)], cot[rows, :].astype(F32), 0.0)
        grad_low = grad.astype(BF16)
        out = jnp.zeros((ROWS, D), F32)
        grad_two = jnp.zeros((ROWS, D), F32)
        for k in range(planes):
            cols = slice(k * width, (k + 1) * width)
            up = flat(full_up[:, :, :, :, cols])
            down = flat(full_down[k])
            hidden = dot(low_two, up) + up_bias[:, cols]
            grad_active = dot_nt(grad_low, down)
            active, slope = gelu_pair(hidden)
            active = active.astype(BF16)
            grad_hidden = grad_active * slope
            grad_hidden_low = grad_hidden.astype(BF16)
            out += dot(active, down)
            grad_bias[:, cols] += col_sum(grad_hidden)
            sum_down[k] += dot_tn(active, grad_low).reshape(sum_down.shape[1:])
            sum_up[:, :, :, :, cols] += dot_tn(low_two, grad_hidden_low).reshape(
                *sum_up.shape[:-1], width
            )
            grad_two += dot_nt(grad_hidden_low, up)
        cot[rows, :] = (res + (out + vectors[7:8, :])).astype(BF16)
        pltpu.make_async_copy(cot.at[rows], layer_out.at[rows], out_sem.at[i]).start()
        back = grad + norm_backward(grad_two, hat, spread, vectors[5:6, :])
        back_low = back.astype(BF16)
        resid[rows, :] = back
        sum_out[...] += dot_tn(block, back_low).reshape(sum_out.shape)
        mixed[rows, :] = dot_nt(back_low, low_out).astype(BF16)
        grad_vectors[4:5, :] += col_sum(back)
        grad_vectors[5:6, :] += col_sum(grad_two * hat)
        grad_vectors[6:7, :] += col_sum(grad_two)
        grad_vectors[7:8, :] += col_sum(grad)
        return carry

    lax.fori_loop(0, rows_local // ROWS, feed, 0)

    for item in gathers:
        item.drain()
    s_down.begin()
    s_up.begin()
    s_out.begin()
    parts = [slice(k * ROWS, (k + 1) * ROWS) for k in range(rows_local // ROWS)]
    layer_copies = [
        pltpu.make_async_copy(cot.at[rows], layer_out.at[rows], out_sem.at[k])
        for k, rows in enumerate(parts)
    ]

    def recall():
        for copy in layer_copies:
            copy.wait()
        recall_low.start()

    beside_attention = {
        (0, 0, 1): [s_down.second],
        (0, 0, 3): [s_up.second],
        (0, 1, 1): [s_out.second, s_down.first],
        (0, 1, 3): [recall],
        (1, 0, 1): [s_up.first, s_out.first, s_low.second],
        (1, 0, 3): [s_down.planes],
        (1, 1, 1): [s_low.first, s_up.planes, s_out.planes],
        (1, 1, 3): [s_low.planes],
    }
    for g in range(D // GROUP):
        query_cols, key_cols, value_cols = columns(g)
        own_cols = slice(g * GROUP, (g + 1) * GROUP)

        def attend_back(s, query_bias):
            linked = links(seg, counts, s)
            padded = (BLOCKS - 1) * IMG >= counts[s]
            for b in range(BLOCKS):
                below, above, with_below, with_above, offset = neighbour(b, linked)
                rows = slice(b * IMG, (b + 1) * IMG)
                keys = with_other(key_cols, s, b, with_below)
                values = with_other(value_cols, s, b, with_below)
                grad = mixed[block_rows(s, b), own_cols]
                grad_query, grad_keys, grad_values = attend_block_backward(
                    qkv[block_rows(s, b), query_cols],
                    keys,
                    values,
                    grad,
                    lse[(s * 2 + g) * BLOCKS + b],
                    offset,
                )
                own_keys, own_values = grad_keys[:IMG], grad_values[:IMG]
                if b == BLOCKS - 1:
                    grad_query = jnp.where(padded, 0.0, grad_query)
                    own_keys = jnp.where(padded, 0.0, own_keys)
                    own_values = jnp.where(padded, grad.astype(F32), own_values)
                query_bias += col_sum(grad_query)
                qkv[block_rows(s, b), query_cols] = grad_query.astype(BF16)
                if b > 0:
                    own_keys += jnp.where(with_above, key_sum[rows, :], 0.0)
                    own_values += jnp.where(with_above, value_sum[rows, :], 0.0)
                key_sum[rows, :] = own_keys
                value_sum[rows, :] = own_values
                if below is not None:
                    key_sum[below, :] = grad_keys[IMG:]
                    value_sum[below, :] = grad_values[IMG:]
                if above is not None:
                    key_sum[above, :] += jnp.where(with_above, grad_keys[IMG:], 0.0)
                    value_sum[above, :] += jnp.where(with_above, grad_values[IMG:], 0.0)
                for at in range(2):
                    stages = beside_attention.get((g, at, b), ())
                    if stages:

                        @pl.when(s == at)
                        def _(stages=stages):
                            for stage in stages:
                                stage()

            covered = pl.ds(pl.multiple_of(s * SEQ, SEQ), SPAN)
            grad_tail = mixed[tail_rows(s), own_cols]
            qkv[tail_rows(s), query_cols] = jnp.zeros_like(grad_tail)
            qkv[tail_rows(s), key_cols] = jnp.zeros_like(grad_tail)
            qkv[tail_rows(s), value_cols] = grad_tail
            qkv[covered, key_cols] = key_sum[...].astype(BF16)
            all_values = value_sum[...]
            qkv[covered, value_cols] = all_values.astype(BF16)
            grad_vectors[3:4, own_cols] += col_sum(all_values) + col_sum(grad_tail.astype(F32))
            return query_bias

        grad_vectors[2:3, own_cols] = lax.fori_loop(
            0, seqs, attend_back, jnp.zeros((1, GROUP), F32)
        )
        if g == 0:
            recall_low.wait()
        total = (sum_low, sum_high)[g]
        for j, cols in enumerate(columns(g)):
            part = dot_tn(low_one[...], qkv[:, cols])
            total[:, :, :, :, j * GROUP : (j + 1) * GROUP] = part.reshape(*total.shape[:-1], GROUP)
        (s_low, s_high)[g].begin()

    for s in range(planes * COLS):
        cols = slice(s * per, (s + 1) * per)
        sum_small[s // COLS, s % COLS, 0, 0:8, 0:per] = grad_vectors[:, cols]
        sum_small[s // COLS, s % COLS, 1, 0:1, 0:long] = grad_bias[:, s * long : (s + 1) * long]
    s_small.begin()

    squares = []
    gain_sum, shift_sum = jnp.zeros((1, D), F32), jnp.zeros((1, D), F32)
    beside_last = {
        0: [s_down.finish, s_up.finish, s_high.second, s_small.second],
        1: [s_out.finish, s_high.first, s_small.first],
        2: [s_low.finish, s_high.planes, s_small.planes],
    }
    for k in range(rows_local // ROWS):
        rows = slice(k * ROWS, (k + 1) * ROWS)
        _, hat, spread = norm_forward(tok[rows, :].astype(F32), vectors[0:1, :], vectors[1:2, :])
        grad_one = dot_nt(qkv[rows, :], flat(full_qkv[...]))
        resid[rows, :] += norm_backward(grad_one, hat, spread, vectors[0:1, :])
        pltpu.make_async_copy(resid.at[rows], token_grad.at[rows], grad_sem.at[k]).start()
        gain_sum += col_sum(grad_one * hat)
        shift_sum += col_sum(grad_one)
        for stage in beside_last.get(k, ()):
            squares.append(stage())
    for item in (s_high, s_small):
        squares.append(item.finish())
    part = jnp.zeros((8, 128), F32)
    for item in squares:
        if item is not None:
            part = part + item
    rows = [
        item[:, k * 128 : (k + 1) * 128] for item in (gain_sum, shift_sum) for k in range(D // 128)
    ]
    tiles = jnp.concatenate([*rows, part], axis=0)
    tiles = sum_over_all(p, tiles, out_tiles, in_tiles, t_send, t_recv)
    first_rows[...] = tiles[:8]
    norm[...] = tiles[8:]
    for item in scatters:
        item.drain()
    for k, rows in enumerate(parts):
        pltpu.make_async_copy(resid.at[rows], token_grad.at[rows], grad_sem.at[k]).wait()


def run_layer(planes, seg, counts, tokens, cotangent, masters):
    halves = [item.reshape(2, item.shape[0] // 2, item.shape[1]) for item in masters[:4]]
    per, long = masters[4].shape[1], masters[5].shape[0]
    rows = tokens.shape[0]
    seqs = rows // SEQ
    shapes = [item.shape[1:] for item in halves]
    group = (shapes[0][0], 3 * GROUP)
    sums = [*shapes[1:], group, group, (16, 128)]
    vmem = pl.BlockSpec(memory_space=pltpu.VMEM)
    hbm = pl.BlockSpec(memory_space=pl.ANY)
    dma = pltpu.SemaphoreType.DMA
    scratch = [pltpu.VMEM(five(planes, *shape), BF16) for shape in (*shapes, (16, 128))]
    scratch += [pltpu.VMEM((8, D), F32), pltpu.VMEM((1, FF), F32)]
    scratch += [pltpu.VMEM(five(planes, *shape), F32) for shape in sums]
    scratch += [
        pltpu.VMEM((rows, D), BF16),
        pltpu.VMEM((rows, D), BF16),
        pltpu.VMEM((rows, 3 * D), BF16),
        pltpu.VMEM((rows, D), BF16),
        pltpu.VMEM((rows, D), F32),
        pltpu.VMEM((seqs * 2 * BLOCKS, 1, PER_GROUP * IMG), F32),
        pltpu.VMEM((SPAN, GROUP), F32),
        pltpu.VMEM((SPAN, GROUP), F32),
        pltpu.VMEM((8, D), F32),
        pltpu.VMEM((1, FF), F32),
    ]
    for k, shape in enumerate(sums):
        scratch += Scatter.buffers(planes, *shape, own=k >= 3)
    scratch += [dma((5, Gather.count(planes)))] * 2 + [dma((6, Scatter.count(planes)))] * 2
    scratch += [pltpu.VMEM((4, 16, 128), F32), pltpu.VMEM((planes + 3, 16, 128), F32)]
    scratch += [dma((planes + 2,))] * 2 + [dma((4,))] + [dma((rows // ROWS,))] * 2
    return pl.pallas_call(
        functools.partial(layer_kernel, planes, per, long),
        in_specs=[SCALAR, SCALAR, hbm, hbm] + [vmem] * 6,
        out_specs=[hbm, hbm] + [vmem] * 8 + [hbm],
        out_shape=[shaped((rows, D), BF16), shaped((rows, D), F32)]
        + [shaped((2, *shape), F32) for shape in sums]
        + [shaped((8, 128), F32), shaped((8, 128), F32), shaped((rows, D), BF16)],
        scratch_shapes=scratch,
        compiler_params=pltpu.CompilerParams(
            vmem_limit_bytes=63 * 2**20, collective_id=1, has_side_effects=True
        ),
        name="layer",
    )(seg, counts, tokens, cotangent, *halves, masters[4], masters[5].reshape(1, -1))


def update_kernel(bound, pieces, *refs):
    results, first_rows, norm = refs[:6], refs[6], refs[7]
    masters, moments, squares = refs[8:14], refs[14:20], refs[20:26]
    layer_in, token_in = refs[26:28]
    total, fresh = refs[28], refs[29:47]
    layer_out, token_grad, layer_mid, token_mid, sems = refs[47:]
    into, out_of = [], []
    for n, (source, middle, target) in enumerate(
        ((layer_in, layer_mid, layer_out), (token_in, token_mid, token_grad))
    ):
        rows = source.shape[0] // pieces
        for k in range(pieces):
            part = pl.ds(k * rows, rows)
            sem = sems.at[n, k]
            into.append(pltpu.make_async_copy(source.at[part], middle.at[part], sem))
            out_of.append(pltpu.make_async_copy(middle.at[part], target.at[part], sem))
    for copy in into:
        copy.start()
    for first_half, second_half in zip(into, out_of):
        first_half.wait()
        second_half.start()
    i = lax.axis_index("fsdp")
    first = first_rows[...]
    every = jnp.sum(norm[...], axis=(0, 1), keepdims=True)
    every = every + jnp.sum(first * first, axis=(0, 1), keepdims=True)
    root = jnp.sqrt(every)
    total[...] = root
    factor = jnp.minimum(1.0, bound / root)
    out, up, down, low, high, small = results
    low, high = flat(low[...]), flat(high[...])
    qkv = [item[:, j * GROUP : (j + 1) * GROUP] for j in range(3) for item in (low, high)]
    per = masters[4].shape[1]
    rows = small[0, 0:8, 0:per]
    line = lax.broadcasted_iota(jnp.int32, (8, 1), 0)
    for s in range(D // per):
        at = s * per
        gain = first[at // 128 : at // 128 + 1, at % 128 : at % 128 + per]
        at = D + at
        shift = first[at // 128 : at // 128 + 1, at % 128 : at % 128 + per]
        mine = jnp.where(line == 0, gain, jnp.where(line == 1, shift, rows))
        rows = jnp.where(i == s, mine, rows)
    grads = (
        jnp.concatenate(qkv, axis=1),
        flat(out[...]),
        flat(up[...]),
        flat(down[...]),
        rows,
        small[1, 0:1, 0 : masters[5].shape[1]],
    )
    for k in range(6):
        new = adam_step(
            masters[k][...], moments[k][...], squares[k][...], grads[k], factor, RATES[k]
        )
        for ref, item in zip((fresh[k], fresh[6 + k], fresh[12 + k]), new):
            ref[...] = item
    for copy in out_of:
        copy.wait()


def run_update(bound, layer_out, token_grad, results, masters, moments, squares):
    def lines(items):
        return [*items[:5], items[5].reshape(1, -1)]

    state = lines(masters) + lines(moments) + lines(squares)
    vmem = pl.BlockSpec(memory_space=pltpu.VMEM)
    hbm = pl.BlockSpec(memory_space=pl.ANY)
    pieces = 4
    done = pl.pallas_call(
        functools.partial(update_kernel, bound, pieces),
        in_specs=[vmem] * 26 + [hbm] * 2,
        out_specs=[vmem] * 19 + [hbm] * 2,
        out_shape=[shaped((1, 1), F32)]
        + [shaped(item.shape, F32) for item in state]
        + [shaped(item.shape, item.dtype) for item in (layer_out, token_grad)],
        scratch_shapes=[
            pltpu.VMEM(layer_out.shape, BF16),
            pltpu.VMEM(token_grad.shape, F32),
            pltpu.SemaphoreType.DMA((2, pieces)),
        ],
        compiler_params=vmem_params(),
        name="update_state",
    )(*results, *state, layer_out, token_grad)
    fresh = [item.reshape(-1) if k % 6 == 5 else item for k, item in enumerate(done[1:19])]
    return (done[19], done[20], done[0].reshape(()), *fresh)


def compute(tokens, cotangent, segment_ids, valid_counts, full):
    low_qkv, low_out, low_up, low_down, vectors, up_bias = full
    qkv, attended, lse = run_forward(segment_ids, valid_counts, tokens, vectors, low_qkv)
    (
        layer_out,
        grad_resid,
        grad_attended,
        grad_down,
        grad_up,
        grad_out_w,
        late,
        grad_bias,
    ) = run_feed(
        valid_counts, tokens, cotangent, attended, vectors, up_bias, low_out, low_up, low_down
    )
    token_grad, grad_qkv_w, early = run_backward(
        segment_ids,
        valid_counts,
        tokens,
        vectors,
        low_qkv,
        qkv,
        grad_attended,
        grad_resid,
        lse,
    )
    return layer_out, token_grad, (grad_qkv_w, grad_out_w, grad_up, grad_down), early, late, grad_bias


def fast_body(tokens, cotangent, segment_ids, valid_counts, *state):
    masters, moments, squares = state[:6], state[6:12], state[12:18]
    wide = lax.axis_size("fsdp")
    layer_out, token_grad, *results, _ = run_layer(
        wide // COLS, segment_ids, valid_counts, tokens, cotangent, masters
    )
    bound = 0.005 * math.sqrt(tokens.shape[0] * wide * lax.axis_size("dp") * PARAMS)
    return run_update(bound, layer_out, token_grad, results, masters, moments, squares)


def plain_body(tokens, cotangent, segment_ids, valid_counts, *state):
    masters, moments, squares = state[:6], state[6:12], state[12:18]
    wide = lax.axis_size("fsdp")
    replicas = lax.axis_size("dp")
    low = [item.astype(BF16) for item in masters]
    full = [
        lax.all_gather(item, "fsdp", axis=1 if k == 4 else 0, tiled=True)
        for k, item in enumerate(low)
    ]
    full[4] = full[4].astype(F32)
    full[5] = full[5].astype(F32).reshape(1, FF)
    layer_out, token_grad, totals, early, late, bias = compute(
        tokens, cotangent, segment_ids, valid_counts, full
    )
    grads = []
    for k, item in enumerate((*totals, early + late, bias.reshape(FF))):
        shard = lax.psum_scatter(item, "fsdp", scatter_dimension=1 if k == 4 else 0, tiled=True)
        grads.append(lax.psum(shard.astype(BF16), "dp").astype(F32))
    local_total = jnp.sum(grads[0] * grads[0])
    for item in grads[1:]:
        local_total = local_total + jnp.sum(item * item)
    grad_norm = jnp.sqrt(lax.psum(local_total, "fsdp"))
    bound = 0.005 * math.sqrt(tokens.shape[0] * wide * replicas * PARAMS)
    factor = jnp.minimum(1.0, bound / grad_norm)
    fresh = [
        adam_step(masters[k], moments[k], squares[k], grads[k], factor, RATES[k]) for k in range(6)
    ]
    return (
        layer_out,
        token_grad,
        grad_norm,
        *(item[0] for item in fresh),
        *(item[1] for item in fresh),
        *(item[2] for item in fresh),
    )


def solution(mesh):
    rows = P(("fsdp", "dp"), None)
    state = (
        P("fsdp", None),
        P("fsdp", None),
        P("fsdp", None),
        P("fsdp", None),
        P(None, "fsdp"),
        P("fsdp"),
    )
    wide, replicas = mesh.shape["fsdp"], mesh.shape["dp"]
    fits = replicas == 2 and wide == COLS * COLS
    return jax.shard_map(
        fast_body if fits else plain_body,
        mesh=mesh,
        in_specs=(rows, rows, rows, P(("fsdp", "dp")), *state, *state, *state),
        out_specs=(rows, rows, P(), *state, *state, *state),
        check_vma=False,
    )
```

```python
import functools
import math

import jax
import jax.numpy as jnp
from jax import lax
from jax.experimental import pallas as pl
from jax.experimental.pallas import tpu as pltpu
from jax.sharding import PartitionSpec as P

D = 512
HEADS = 8
HEAD_DIM = 64
FF = 2048
SEQ = 1024
IMG = 192
BLOCKS = 5
STEP = 5
PARAMS = 3151872
GROUP = 256
PER_GROUP = GROUP // HEAD_DIM

F32 = jnp.float32
BF16 = jnp.bfloat16

norm_eps = 1e-06
adam_eps = 1e-08
decay_rate = 0.05
beta_first = 0.5
beta_second = 0.5
masked_score = -1e30


def dot(left, right):
    return lax.dot_general(left, right, (((1,), (0,)), ((), ())), preferred_element_type=F32)


def dot_nt(left, right):
    return lax.dot_general(left, right, (((1,), (1,)), ((), ())), preferred_element_type=F32)


def dot_tn(left, right):
    return lax.dot_general(left, right, (((0,), (0,)), ((), ())), preferred_element_type=F32)


def norm_forward(values, gain, shift):
    center = values - jnp.mean(values, axis=-1, keepdims=True)
    spread = lax.rsqrt(jnp.mean(center * center, axis=-1, keepdims=True) + norm_eps)
    hat = center * spread
    return hat * gain + shift, hat, spread


def norm_backward(incoming, hat, spread, gain):
    scaled = incoming * gain
    return spread * (
        scaled
        - jnp.mean(scaled, axis=-1, keepdims=True)
        - hat * jnp.mean(scaled * hat, axis=-1, keepdims=True)
    )


def gelu_pair(values):
    half = 0.5 * (1.0 + lax.erf(values * (1.0 / math.sqrt(2.0))))
    bell = jnp.exp(-0.5 * values * values) * (1.0 / math.sqrt(2.0 * math.pi))
    return values * half, half + values * bell


def col_sum(values):
    return jnp.sum(values, axis=0, keepdims=True)


def head_of_lane():
    return lax.broadcasted_iota(jnp.int32, (1, GROUP), 1) // HEAD_DIM


def stack_heads(rows):
    head = head_of_lane()
    zero = jnp.zeros_like(rows)
    return jnp.concatenate([jnp.where(head == h, rows, zero) for h in range(PER_GROUP)], axis=0)


def unstack_heads(stacked):
    head = head_of_lane()
    n = stacked.shape[0] // PER_GROUP
    rows = stacked[(PER_GROUP - 1) * n :]
    for h in range(PER_GROUP - 2, -1, -1):
        rows = jnp.where(head == h, stacked[h * n : (h + 1) * n], rows)
    return rows


def links(seg, counts, s):
    return [
        (seg[s, b * IMG] == seg[s, (b + 1) * IMG]) & ((b + 1) * IMG < counts[s])
        for b in range(BLOCKS - 1)
    ]


def neighbour(b, linked):
    below = slice((b + 1) * IMG, (b + 2) * IMG) if b < BLOCKS - 1 else None
    above = slice((b - 1) * IMG, b * IMG) if b > 0 else None
    with_below = linked[b] if b < BLOCKS - 1 else jnp.bool_(False)
    with_above = linked[b - 1] if b > 0 else jnp.bool_(False)
    offset = jnp.where(with_below | with_above, 0.0, masked_score)
    return below, above, with_below, with_above, offset


def other_rows(ref, cols, below, above, with_below):
    if above is None:
        return ref[below, cols]
    if below is None:
        return ref[above, cols]
    return jnp.where(with_below, ref[below, cols], ref[above, cols])


def attend_block(query, keys, values, offset):
    stacked = stack_heads(query * jnp.asarray(HEAD_DIM**-0.5, BF16))
    scores = dot_nt(keys, stacked)
    own, other = scores[:IMG], scores[IMG:]
    top = jnp.maximum(
        jnp.max(own, axis=0, keepdims=True), jnp.max(other, axis=0, keepdims=True) + offset
    )
    own = jnp.exp(own - top)
    other = jnp.exp(other - (top - offset))
    total = col_sum(own) + col_sum(other)
    inverse = 1.0 / total
    probs = jnp.concatenate([own * inverse, other * inverse], axis=0).astype(BF16)
    return unstack_heads(dot_tn(probs, values)), top + jnp.log(total)


def attend_block_backward(query, keys, values, grad, lse, offset):
    stacked = stack_heads(query * jnp.asarray(HEAD_DIM**-0.5, BF16))
    grads = stack_heads(grad)
    scores = dot_nt(keys, stacked)
    grad_probs = dot_nt(values, grads)
    own = jnp.exp(scores[:IMG] - lse)
    other = jnp.exp(scores[IMG:] - (lse - offset))
    own_t = own * grad_probs[:IMG]
    other_t = other * grad_probs[IMG:]
    delta = col_sum(own_t) + col_sum(other_t)
    grad_scores = jnp.concatenate([own_t - own * delta, other_t - other * delta], axis=0)
    grad_scores = grad_scores.astype(BF16)
    probs = jnp.concatenate([own, other], axis=0).astype(BF16)
    grad_values = dot(probs, grads)
    grad_keys = dot(grad_scores, stacked)
    grad_query = unstack_heads(dot_tn(grad_scores, keys)) * (HEAD_DIM**-0.5)
    return grad_query, grad_keys, grad_values


def forward_kernel(chunk, seg, counts, tokens, vectors, low_qkv, qkv, attended, lse):
    s = pl.program_id(0)
    bias = jnp.concatenate([vectors[2:3, :], jnp.zeros((1, D), F32), vectors[3:4, :]], axis=1)
    for c in range(SEQ // chunk):
        rows = slice(c * chunk, (c + 1) * chunk)
        normed, _, _ = norm_forward(tokens[rows, :].astype(F32), vectors[0:1, :], vectors[1:2, :])
        qkv[rows, :] = (dot(normed.astype(BF16), low_qkv[...]) + bias).astype(BF16)
    linked = links(seg, counts, s)
    for g in range(D // GROUP):
        query_cols, key_cols, value_cols = [
            slice(j * D + g * GROUP, j * D + (g + 1) * GROUP) for j in range(3)
        ]
        out_cols = slice(g * GROUP, (g + 1) * GROUP)
        for b in range(BLOCKS):
            rows = slice(b * IMG, (b + 1) * IMG)
            below, above, with_below, with_above, offset = neighbour(b, linked)
            keys = jnp.concatenate(
                [qkv[rows, key_cols], other_rows(qkv, key_cols, below, above, with_below)], axis=0
            )
            own_values = qkv[rows, value_cols]
            values = jnp.concatenate(
                [own_values, other_rows(qkv, value_cols, below, above, with_below)], axis=0
            )
            mixed, block_lse = attend_block(qkv[rows, query_cols], keys, values, offset)
            mixed = mixed.astype(BF16)
            if b == BLOCKS - 1:
                mixed = jnp.where(b * IMG >= counts[s], own_values, mixed)
            attended[rows, out_cols] = mixed
            lse[g * BLOCKS + b] = block_lse
        attended[BLOCKS * IMG :, out_cols] = qkv[BLOCKS * IMG :, value_cols]


def feed_kernel(
    rows_in,
    chunk,
    counts,
    tokens,
    cotangent,
    attended,
    vectors,
    up_bias,
    low_out,
    low_up,
    low_down,
    layer_out,
    grad_resid,
    grad_attended,
    grad_down,
    grad_up,
    grad_out_w,
    grad_vectors,
    grad_bias,
):
    i = pl.program_id(0)

    @pl.when(i == 0)
    def _():
        for ref in (grad_down, grad_up, grad_out_w, grad_vectors, grad_bias):
            ref[...] = jnp.zeros_like(ref)

    per = SEQ // rows_in
    mixed = attended[...]
    resid = tokens[...].astype(F32) + (dot(mixed, low_out[...]) + vectors[4:5, :])
    normed, hat, spread = norm_forward(resid, vectors[5:6, :], vectors[6:7, :])
    low_two = normed.astype(BF16)
    position = (i % per) * rows_in + lax.broadcasted_iota(jnp.int32, (rows_in, 1), 0)
    grad = jnp.where(position < counts[i // per], cotangent[...].astype(F32), 0.0)
    grad_low = grad.astype(BF16)
    out = jnp.zeros((rows_in, D), F32)
    grad_two = jnp.zeros((rows_in, D), F32)
    for c in range(FF // chunk):
        cols = slice(c * chunk, (c + 1) * chunk)
        hidden = dot(low_two, low_up[:, cols]) + up_bias[:, cols]
        grad_active = dot_nt(grad_low, low_down[cols, :])
        active, slope = gelu_pair(hidden)
        active = active.astype(BF16)
        grad_hidden = grad_active * slope
        grad_hidden_low = grad_hidden.astype(BF16)
        out += dot(active, low_down[cols, :])
        grad_bias[:, cols] += col_sum(grad_hidden)
        grad_down[cols, :] += dot_tn(active, grad_low)
        grad_up[:, cols] += dot_tn(low_two, grad_hidden_low)
        grad_two += dot_nt(grad_hidden_low, low_up[:, cols])
    layer_out[...] = (resid + (out + vectors[7:8, :])).astype(BF16)
    back = grad + norm_backward(grad_two, hat, spread, vectors[5:6, :])
    back_low = back.astype(BF16)
    grad_resid[...] = back
    grad_out_w[...] += dot_tn(mixed, back_low)
    grad_attended[...] = dot_nt(back_low, low_out[...]).astype(BF16)
    grad_vectors[4:5, :] += col_sum(back)
    grad_vectors[5:6, :] += col_sum(grad_two * hat)
    grad_vectors[6:7, :] += col_sum(grad_two)
    grad_vectors[7:8, :] += col_sum(grad)


def backward_kernel(
    chunk,
    seg,
    counts,
    tokens,
    vectors,
    low_qkv,
    qkv,
    grad_attended,
    grad_resid,
    lse,
    token_grad,
    grad_qkv_w,
    grad_vectors,
    grad_qkv,
    key_sum,
    value_sum,
):
    s = pl.program_id(0)

    @pl.when(s == 0)
    def _():
        grad_qkv_w[...] = jnp.zeros_like(grad_qkv_w)
        grad_vectors[...] = jnp.zeros_like(grad_vectors)

    linked = links(seg, counts, s)
    padded = (BLOCKS - 1) * IMG >= counts[s]
    covered = slice(0, BLOCKS * IMG)
    tail = slice(BLOCKS * IMG, SEQ)
    for g in range(D // GROUP):
        query_cols, key_cols, value_cols = [
            slice(j * D + g * GROUP, j * D + (g + 1) * GROUP) for j in range(3)
        ]
        grad_cols = slice(g * GROUP, (g + 1) * GROUP)
        query_bias = jnp.zeros((1, GROUP), F32)
        for b in range(BLOCKS):
            rows = slice(b * IMG, (b + 1) * IMG)
            below, above, with_below, with_above, offset = neighbour(b, linked)
            keys = jnp.concatenate(
                [qkv[rows, key_cols], other_rows(qkv, key_cols, below, above, with_below)], axis=0
            )
            values = jnp.concatenate(
                [qkv[rows, value_cols], other_rows(qkv, value_cols, below, above, with_below)],
                axis=0,
            )
            grad = grad_attended[rows, grad_cols]
            grad_query, grad_keys, grad_values = attend_block_backward(
                qkv[rows, query_cols], keys, values, grad, lse[g * BLOCKS + b], offset
            )
            own_keys, own_values = grad_keys[:IMG], grad_values[:IMG]
            if b == BLOCKS - 1:
                grad_query = jnp.where(padded, 0.0, grad_query)
                own_keys = jnp.where(padded, 0.0, own_keys)
                own_values = jnp.where(padded, grad.astype(F32), own_values)
            query_bias += col_sum(grad_query)
            grad_qkv[rows, query_cols] = grad_query.astype(BF16)
            if b > 0:
                own_keys += jnp.where(with_above, key_sum[rows, :], 0.0)
                own_values += jnp.where(with_above, value_sum[rows, :], 0.0)
            key_sum[rows, :] = own_keys
            value_sum[rows, :] = own_values
            if below is not None:
                key_sum[below, :] = grad_keys[IMG:]
                value_sum[below, :] = grad_values[IMG:]
            if above is not None:
                key_sum[above, :] += jnp.where(with_above, grad_keys[IMG:], 0.0)
                value_sum[above, :] += jnp.where(with_above, grad_values[IMG:], 0.0)
        grad_tail = grad_attended[tail, grad_cols]
        grad_qkv[tail, query_cols] = jnp.zeros_like(grad_tail)
        grad_qkv[tail, key_cols] = jnp.zeros_like(grad_tail)
        grad_qkv[tail, value_cols] = grad_tail
        grad_qkv[covered, key_cols] = key_sum[...].astype(BF16)
        all_values = value_sum[...]
        grad_qkv[covered, value_cols] = all_values.astype(BF16)
        grad_vectors[2:3, grad_cols] += query_bias
        grad_vectors[3:4, grad_cols] += col_sum(all_values) + col_sum(grad_tail.astype(F32))
    for c in range(SEQ // chunk):
        rows = slice(c * chunk, (c + 1) * chunk)
        normed, hat, spread = norm_forward(
            tokens[rows, :].astype(F32), vectors[0:1, :], vectors[1:2, :]
        )
        grad = grad_qkv[rows, :]
        grad_qkv_w[...] += dot_tn(normed.astype(BF16), grad)
        grad_one = dot_nt(grad, low_qkv[...])
        token_grad[rows, :] = grad_resid[rows, :] + norm_backward(
            grad_one, hat, spread, vectors[0:1, :]
        )
        grad_vectors[0:1, :] += col_sum(grad_one * hat)
        grad_vectors[1:2, :] += col_sum(grad_one)


def vmem_params():
    return pltpu.CompilerParams(vmem_limit_bytes=60 * 2**20)


def by_rows(rows, cols):
    return pl.BlockSpec((rows, cols), lambda i: (i, 0))


def whole(*shape):
    return pl.BlockSpec(shape, lambda i: (0,) * len(shape))


def stats_spec():
    return pl.BlockSpec((2 * BLOCKS, 1, PER_GROUP * IMG), lambda i: (i, 0, 0))


def shaped(shape, dtype):
    return jax.ShapeDtypeStruct(shape, dtype)


SCALAR = pl.BlockSpec(memory_space=pltpu.SMEM)


def run_forward(seg, counts, tokens, vectors, low_qkv):
    rows = tokens.shape[0]
    seqs = rows // SEQ
    return pl.pallas_call(
        functools.partial(forward_kernel, 256),
        grid=(seqs,),
        in_specs=[SCALAR, SCALAR, by_rows(SEQ, D), whole(8, D), whole(D, 3 * D)],
        out_specs=[by_rows(SEQ, 3 * D), by_rows(SEQ, D), stats_spec()],
        out_shape=[
            shaped((rows, 3 * D), BF16),
            shaped((rows, D), BF16),
            shaped((seqs * 2 * BLOCKS, 1, PER_GROUP * IMG), F32),
        ],
        compiler_params=vmem_params(),
        name="attend_forward",
    )(seg, counts, tokens, vectors, low_qkv)


def run_feed(counts, tokens, cotangent, attended, vectors, up_bias, low_out, low_up, low_down):
    rows = tokens.shape[0]
    step = 512
    return pl.pallas_call(
        functools.partial(feed_kernel, step, 512),
        grid=(rows // step,),
        in_specs=[
            SCALAR,
            by_rows(step, D),
            by_rows(step, D),
            by_rows(step, D),
            whole(8, D),
            whole(1, FF),
            whole(D, D),
            whole(D, FF),
            whole(FF, D),
        ],
        out_specs=[
            by_rows(step, D),
            by_rows(step, D),
            by_rows(step, D),
            whole(FF, D),
            whole(D, FF),
            whole(D, D),
            whole(8, D),
            whole(1, FF),
        ],
        out_shape=[
            shaped((rows, D), BF16),
            shaped((rows, D), F32),
            shaped((rows, D), BF16),
            shaped((FF, D), F32),
            shaped((D, FF), F32),
            shaped((D, D), F32),
            shaped((8, D), F32),
            shaped((1, FF), F32),
        ],
        compiler_params=vmem_params(),
        name="feed_forward",
    )(counts, tokens, cotangent, attended, vectors, up_bias, low_out, low_up, low_down)


def run_backward(seg, counts, tokens, vectors, low_qkv, qkv, grad_attended, grad_resid, lse):
    rows = tokens.shape[0]
    return pl.pallas_call(
        functools.partial(backward_kernel, 512),
        grid=(rows // SEQ,),
        in_specs=[
            SCALAR,
            SCALAR,
            by_rows(SEQ, D),
            whole(8, D),
            whole(D, 3 * D),
            by_rows(SEQ, 3 * D),
            by_rows(SEQ, D),
            by_rows(SEQ, D),
            stats_spec(),
        ],
        out_specs=[by_rows(SEQ, D), whole(D, 3 * D), whole(8, D)],
        out_shape=[
            shaped((rows, D), F32),
            shaped((D, 3 * D), F32),
            shaped((8, D), F32),
        ],
        scratch_shapes=[
            pltpu.VMEM((SEQ, 3 * D), BF16),
            pltpu.VMEM((BLOCKS * IMG, GROUP), F32),
            pltpu.VMEM((BLOCKS * IMG, GROUP), F32),
        ],
        compiler_params=vmem_params(),
        name="attend_backward",
    )(seg, counts, tokens, vectors, low_qkv, qkv, grad_attended, grad_resid, lse)


def adam_step(weight, moment, square, grad, factor, rate):
    clipped = grad * factor
    moment_new = beta_first * moment + (1.0 - beta_first) * clipped
    square_new = beta_second * square + (1.0 - beta_second) * clipped * clipped
    first_hat = moment_new / (1.0 - beta_first**STEP)
    second_hat = square_new / (1.0 - beta_second**STEP)
    weight_new = weight - rate * (
        first_hat / (jnp.sqrt(second_hat) + adam_eps) + decay_rate * weight
    )
    return (weight_new, moment_new, square_new)


RATES = (
    2.0 / math.sqrt(D),
    8.0 / math.sqrt(D),
    2.0 / math.sqrt(D),
    2.0 / math.sqrt(FF),
    0.5,
    0.5,
)


MESH = pl.DeviceIdType.MESH
COLS = 4


class Place:
    def __init__(self, planes):
        self.planes = planes
        self.i = lax.axis_index("fsdp")
        self.c = c = lax.axis_index("dp")
        self.q = q = lax.rem(self.i, COLS)
        self.z = self.i // COLS
        x, y = lax.rem(q, 2), q // 2
        self.qx = y * 2 + (1 - x)
        self.qy = (1 - y) * 2 + x
        self.qa = c * self.qx + (1 - c) * self.qy
        self.qb = c * self.qy + (1 - c) * self.qx
        self.qd = COLS - 1 - q
        self.at_a = (self.z * COLS + self.qa, c)
        self.at_b = (self.z * COLS + self.qb, c)
        self.at_x = (self.z * COLS + self.qx, c)
        self.at_y = (self.z * COLS + self.qy, c)
        self.at_d = (self.z * COLS + self.qd, c)
        self.partner = (self.i, 1 - c)

    def plane(self, step):
        return lax.rem(self.z + step, self.planes)

    def along(self, step):
        return (self.plane(step) * COLS + self.q, self.c)

    def greet(self):
        barrier = pltpu.get_barrier_semaphore()
        friends = [self.along(step) for step in range(1, self.planes)]
        friends += [self.at_a, self.at_b, self.at_d, self.partner]
        for device in friends:
            pl.semaphore_signal(barrier, inc=1, device_id=device, device_id_type=MESH)
        pl.semaphore_wait(barrier, len(friends))


def remote(source, target, send, recv, device):
    return pltpu.make_async_remote_copy(
        src_ref=source,
        dst_ref=target,
        send_sem=send,
        recv_sem=recv,
        device_id=device,
        device_id_type=MESH,
    )


class Gather:
    def __init__(self, place, full, send, recv):
        p, c = place, place.c
        n = p.planes
        self.pieces = n

        def move(k, plane, col, device):
            ref = full.at[plane, col, c]
            return remote(ref, ref, send.at[k], recv.at[k], device)

        self.to_z = [move(k, p.z, p.q, p.along(k + 1)) for k in range(n - 1)]
        base = n - 1
        self.to_a = [move(base + d, p.plane(n - d), p.q, p.at_a) for d in range(n)]
        self.to_b = [move(base + n + d, p.plane(n - d), p.q, p.at_b) for d in range(n)]
        self.on_b = [move(base + 2 * n + d, p.plane(n - d), p.qa, p.at_b) for d in range(n)]
        base += 3 * n
        self.to_core = [
            move(base + k, slice(None), col, p.partner)
            for k, col in enumerate((p.q, p.qa, p.qb, p.qd))
        ]

    @staticmethod
    def count(planes):
        return 4 * planes + 3

    def begin(self):
        for copy in self.to_z:
            copy.start()

    def begin_own(self):
        self.to_a[0].start()
        self.to_b[0].start()

    def spread(self):
        for k, copy in enumerate(self.to_z):
            copy.wait_recv()
            self.to_a[k + 1].start()
            self.to_b[k + 1].start()
        self.to_core[0].start()

    def forward(self):
        for k in range(self.pieces):
            self.to_a[k].wait_recv()
            self.on_b[k].start()
        self.to_core[1].start()

    def last(self):
        for copy in self.to_b:
            copy.wait_recv()
        self.to_core[2].start()
        for copy in self.on_b:
            copy.wait_recv()
        self.to_core[3].start()

    def arrive(self):
        for copy in self.to_core:
            copy.wait_recv()

    def drain(self):
        for copy in (*self.to_z, *self.to_a, *self.to_b, *self.on_b, *self.to_core):
            copy.wait_send()


class Scatter:
    def __init__(self, place, total, bufs, result, send, recv):
        self.place, self.total, self.result = place, total, result
        self.in_c, self.out_b, self.in_b = bufs[:3]
        self.out_a, self.in_a, self.out_z, self.in_z = bufs[3:7]
        self.out_c = bufs[7]
        p = place
        self.order = (p.qa, p.qd, p.qb, p.q)
        self.to_core = [
            remote(self.out_c.at[k], self.in_c.at[k], send.at[k], recv.at[k], p.partner)
            for k in range(4)
        ]
        self.to_b = [
            remote(self.out_b.at[k], self.in_b.at[k], send.at[4 + k], recv.at[4 + k], p.at_b)
            for k in range(2)
        ]
        self.to_a = remote(self.out_a, self.in_a, send.at[6], recv.at[6], p.at_a)
        self.to_z = [
            remote(self.out_z.at[k], self.in_z.at[k], send.at[7 + k], recv.at[7 + k], p.along(k + 1))
            for k in range(p.planes - 1)
        ]
        n = 6 + p.planes
        half = result.at[p.c]
        self.to_both = remote(half, half, send.at[n], recv.at[n], p.partner)

    @staticmethod
    def count(planes):
        return planes + 7

    @staticmethod
    def buffers(planes, rows, cols, own=True):
        shapes = [(4, planes)] + [(2, planes)] * 2 + [(planes,)] * 2 + [(planes - 1,)] * 2
        shapes += [(4, planes)] if own else []
        return [pltpu.VMEM((*shape, rows, cols), BF16) for shape in shapes]

    def begin(self):
        for k in range(4):
            self.out_c[k] = self.total[:, self.order[k], 1 - self.place.c].astype(BF16)
            self.to_core[k].start()

    def second(self):
        p = self.place
        for k, col in ((1, p.qd), (0, p.qb)):
            self.to_core[k].wait_recv()
            mine = self.total[:, col, p.c] + self.in_c[k].astype(F32)
            self.out_b[k] = mine.astype(BF16)
            self.to_b[k].start()

    def first(self):
        p = self.place
        self.to_core[2].wait_recv()
        self.to_b[1].wait_recv()
        mine = self.total[:, p.qa, p.c] + self.in_c[2].astype(F32) + self.in_b[1].astype(F32)
        self.out_a[...] = mine.astype(BF16)
        self.to_a.start()

    def planes(self):
        p = self.place
        self.to_core[3].wait_recv()
        self.to_b[0].wait_recv()
        self.to_a.wait_recv()

        def mine(z):
            local = self.total[z, p.q, p.c] + self.in_c[3, z].astype(F32)
            return local + self.in_b[0, z].astype(F32) + self.in_a[z].astype(F32)

        for k in range(p.planes - 1):
            self.out_z[k] = mine(p.plane(k + 1)).astype(BF16)
            self.to_z[k].start()
        self.result[p.c] = mine(p.z)

    def finish(self):
        p = self.place
        for copy in self.to_z:
            copy.wait_recv()
        shard = self.result[p.c]
        for k in range(p.planes - 1):
            shard = shard + self.in_z[k].astype(F32)
        self.result[p.c] = shard
        self.to_both.start()
        square = shard * shard
        lanes = sum(square[:, k : k + 128] for k in range(0, square.shape[1], 128))
        return jnp.sum(lanes.reshape(-1, 8, 128), axis=0)

    def drain(self):
        self.to_both.wait_recv()
        for copy in (*self.to_core, *self.to_b, self.to_a, *self.to_z, self.to_both):
            copy.wait_send()


def sum_over_all(place, part, out, slots, send, recv):
    p = place
    count = p.planes + COLS - 1
    out[0] = part
    copies = [remote(out.at[0], slots.at[count + 1], send.at[0], recv.at[0], p.partner)]
    copies[0].start()
    copies[0].wait_recv()
    chip = part + slots[count + 1]
    out[1] = chip
    slots[p.z] = chip
    lines = [
        remote(out.at[1], slots.at[p.z], send.at[k + 1], recv.at[k + 1], p.along(k + 1))
        for k in range(p.planes - 1)
    ]
    for copy in lines:
        copy.start()
    for copy in lines:
        copy.wait_recv()
    column = slots[0]
    for k in range(1, p.planes):
        column = column + slots[k]
    out[2] = column
    slots[p.planes + p.q] = column
    columns = [
        remote(out.at[2], slots.at[p.planes + p.q], send.at[n], recv.at[n], device)
        for n, device in enumerate((p.at_x, p.at_y, p.at_d), p.planes)
    ]
    for copy in columns:
        copy.start()
    for copy in columns:
        copy.wait_recv()
    total = slots[p.planes]
    for k in range(1, COLS):
        total = total + slots[p.planes + k]
    for copy in (*copies, *lines, *columns):
        copy.wait_send()
    return total


def small_shard(place, vectors, up_bias):
    def tile(rows):
        for axis, full in ((1, 128), (0, 8)):
            short = list(rows.shape)
            short[axis] = full - short[axis]
            if short[axis]:
                rows = jnp.concatenate([rows, jnp.zeros(short, F32)], axis=axis)
        return rows

    rows, bias = tile(vectors[...]), tile(up_bias[...])
    half = jnp.where(place.c == 0, rows, bias)
    return jnp.concatenate([half, jnp.zeros((8, 128), F32)], axis=0).astype(BF16)


ROWS = 512
SPAN = SEQ // IMG * IMG


def five(planes, rows, cols):
    return (planes, COLS, 2, rows, cols)


def flat(value):
    return value.reshape(-1, value.shape[-1])


def layer_kernel(planes, per, long, *refs):
    seg, counts, tokens, cotangent = refs[:4]
    shards, vector_shard, bias_shard = refs[4:8], refs[8], refs[9]
    layer_out, token_grad = refs[10:12]
    results, first_rows, norm, kept = refs[12:18], refs[18], refs[19], refs[20]
    full, small, vectors, up_bias = refs[21:25], refs[25], refs[26], refs[27]
    totals = refs[28:34]
    tok, cot, qkv, mixed, resid, lse, key_sum, value_sum = refs[34:42]
    grad_vectors, grad_bias = refs[42:44]
    bufs = refs[44:89]
    g_send, g_recv, s_send, s_recv = refs[89:93]
    out_tiles, in_tiles, t_send, t_recv, load_sem, out_sem, grad_sem = refs[93:100]
    full_qkv, full_out, full_up, full_down = full
    sum_out, sum_up, sum_down, sum_low, sum_high, sum_small = totals
    p = Place(planes)
    rows_local = tok.shape[0]
    seqs = rows_local // SEQ

    low_one = cot
    load_tokens = pltpu.make_async_copy(tokens, tok, load_sem.at[0])
    load_cotangent = pltpu.make_async_copy(cotangent, cot, load_sem.at[1])
    keep_low = pltpu.make_async_copy(low_one, kept, load_sem.at[2])
    recall_low = pltpu.make_async_copy(kept, low_one, load_sem.at[3])
    load_tokens.start()

    small[p.z, p.q, p.c] = small_shard(p, vector_shard, bias_shard)
    for shard, target in zip(shards, full):
        target[p.z, p.q, p.c] = shard[p.c].astype(BF16)
    p.greet()
    g_small, g_qkv, g_out, g_up, g_down = gathers = [
        Gather(p, ref, g_send.at[k], g_recv.at[k]) for k, ref in enumerate((small, *full))
    ]
    spare = [ref.at[:, :, 0] for ref in full[1:]]
    bufs = [[*bufs[7 * k : 7 * k + 7], spare[k]] for k in range(3)] + [
        bufs[21 + 8 * k : 29 + 8 * k] for k in range(3)
    ]
    scatters = [
        Scatter(p, total, bufs[k], results[k], s_send.at[k], s_recv.at[k])
        for k, total in enumerate(totals)
    ]
    s_out, s_up, s_down, s_low, s_high, s_small = scatters
    g_small.begin()
    g_qkv.begin()
    for item in gathers:
        item.begin_own()
    g_small.spread()
    g_qkv.spread()
    for item in (g_out, g_up, g_down):
        item.begin()
    g_small.forward()
    g_qkv.forward()
    g_out.spread()
    g_small.last()
    g_qkv.last()
    g_small.arrive()
    for s in range(planes * COLS):
        rows = small[s // COLS, s % COLS, 0].astype(F32)
        bias = small[s // COLS, s % COLS, 1].astype(F32)
        vectors[:, s * per : (s + 1) * per] = rows[:8, :per]
        up_bias[:, s * long : (s + 1) * long] = bias[:1, :long]
    load_tokens.wait()
    g_qkv.arrive()

    qkv_bias = jnp.concatenate([vectors[2:3, :], jnp.zeros((1, D), F32), vectors[3:4, :]], axis=1)
    chunk = 256
    beside_qkv = {
        0: [g_out.forward],
        2: [g_up.spread],
        5: [g_out.last],
        7: [g_up.forward],
    }
    for k in range(rows_local // chunk):
        rows = slice(k * chunk, (k + 1) * chunk)
        normed, _, _ = norm_forward(tok[rows, :].astype(F32), vectors[0:1, :], vectors[1:2, :])
        low = normed.astype(BF16)
        low_one[rows, :] = low
        qkv[rows, :] = (dot(low, flat(full_qkv[...])) + qkv_bias).astype(BF16)
        for stage in beside_qkv.get(k, ()):
            stage()
    keep_low.start()

    def block_rows(s, b):
        return pl.ds(s * SEQ + b * IMG, IMG)

    def tail_rows(s):
        return pl.ds(s * SEQ + SPAN, SEQ - SPAN)

    def columns(g):
        return [slice(j * D + g * GROUP, j * D + (g + 1) * GROUP) for j in range(3)]

    def with_other(cols, s, b, with_below):
        own = qkv[block_rows(s, b), cols]
        if b == 0:
            other = qkv[block_rows(s, 1), cols]
        elif b == BLOCKS - 1:
            other = qkv[block_rows(s, b - 1), cols]
        else:
            other = jnp.where(
                with_below, qkv[block_rows(s, b + 1), cols], qkv[block_rows(s, b - 1), cols]
            )
        return jnp.concatenate([own, other], axis=0)

    beside_forward = {
        (0, 0, 1): [g_down.spread],
        (0, 1, 1): [g_up.last],
        (0, 1, 4): [g_down.forward],
        (1, 1, 3): [g_down.last],
    }
    for g in range(D // GROUP):
        query_cols, key_cols, value_cols = columns(g)
        own_cols = slice(g * GROUP, (g + 1) * GROUP)

        def attend(s):
            linked = links(seg, counts, s)
            for b in range(BLOCKS):
                _, _, with_below, _, offset = neighbour(b, linked)
                keys = with_other(key_cols, s, b, with_below)
                values = with_other(value_cols, s, b, with_below)
                block, block_lse = attend_block(
                    qkv[block_rows(s, b), query_cols], keys, values, offset
                )
                block = block.astype(BF16)
                if b == BLOCKS - 1:
                    block = jnp.where(b * IMG >= counts[s], values[:IMG], block)
                mixed[block_rows(s, b), own_cols] = block
                lse[(s * 2 + g) * BLOCKS + b] = block_lse
                for stage in beside_forward.get((g, s, b), ()):
                    stage()
            mixed[tail_rows(s), own_cols] = qkv[tail_rows(s), value_cols]

        for s in range(seqs):
            attend(s)
        if g == 0:
            keep_low.wait()
            load_cotangent.start()

    for item in (g_out, g_up, g_down):
        item.arrive()
    load_cotangent.wait()

    for ref in (sum_out, sum_up, sum_down, sum_small, grad_vectors, grad_bias):
        ref[...] = jnp.zeros_like(ref)
    width = FF // planes

    def feed(i, carry):
        rows = pl.ds(pl.multiple_of(i * ROWS, ROWS), ROWS)
        block = mixed[rows, :]
        low_out = flat(full_out[...])
        res = tok[rows, :].astype(F32) + (dot(block, low_out) + vectors[4:5, :])
        normed, hat, spread = norm_forward(res, vectors[5:6, :], vectors[6:7, :])
        low_two = normed.astype(BF16)
        position = (i % (SEQ // ROWS)) * ROWS + lax.broadcasted_iota(jnp.int32, (ROWS, 1), 0)
        grad = jnp.where(position < counts[i // (SEQ // ROWS)], cot[rows, :].astype(F32), 0.0)
        grad_low = grad.astype(BF16)
        out = jnp.zeros((ROWS, D), F32)
        grad_two = jnp.zeros((ROWS, D), F32)
        for k in range(planes):
            cols = slice(k * width, (k + 1) * width)
            up = flat(full_up[:, :, :, :, cols])
            down = flat(full_down[k])
            hidden = dot(low_two, up) + up_bias[:, cols]
            grad_active = dot_nt(grad_low, down)
            active, slope = gelu_pair(hidden)
            active = active.astype(BF16)
            grad_hidden = grad_active * slope
            grad_hidden_low = grad_hidden.astype(BF16)
            out += dot(active, down)
            grad_bias[:, cols] += col_sum(grad_hidden)
            sum_down[k] += dot_tn(active, grad_low).reshape(sum_down.shape[1:])
            sum_up[:, :, :, :, cols] += dot_tn(low_two, grad_hidden_low).reshape(
                *sum_up.shape[:-1], width
            )
            grad_two += dot_nt(grad_hidden_low, up)
        cot[rows, :] = (res + (out + vectors[7:8, :])).astype(BF16)
        pltpu.make_async_copy(cot.at[rows], layer_out.at[rows], out_sem.at[i]).start()
        back = grad + norm_backward(grad_two, hat, spread, vectors[5:6, :])
        back_low = back.astype(BF16)
        resid[rows, :] = back
        sum_out[...] += dot_tn(block, back_low).reshape(sum_out.shape)
        mixed[rows, :] = dot_nt(back_low, low_out).astype(BF16)
        grad_vectors[4:5, :] += col_sum(back)
        grad_vectors[5:6, :] += col_sum(grad_two * hat)
        grad_vectors[6:7, :] += col_sum(grad_two)
        grad_vectors[7:8, :] += col_sum(grad)
        return carry

    lax.fori_loop(0, rows_local // ROWS, feed, 0)

    for item in gathers:
        item.drain()
    s_down.begin()
    s_up.begin()
    s_out.begin()
    parts = [slice(k * ROWS, (k + 1) * ROWS) for k in range(rows_local // ROWS)]
    layer_copies = [
        pltpu.make_async_copy(cot.at[rows], layer_out.at[rows], out_sem.at[k])
        for k, rows in enumerate(parts)
    ]

    def recall():
        for copy in layer_copies:
            copy.wait()
        recall_low.start()

    squares = []
    beside_attention = {
        (0, 0, 0): [s_down.second],
        (0, 0, 1): [s_up.second],
        (0, 0, 2): [s_out.second],
        (0, 1, 1): [s_down.first],
        (0, 1, 3): [recall],
        (1, 0, 0): [s_up.first],
        (1, 0, 1): [s_down.planes],
        (1, 0, 2): [s_low.second],
        (1, 0, 3): [s_out.first],
        (1, 1, 0): [s_up.planes],
        (1, 1, 2): [s_out.planes],
        (1, 1, 3): [s_low.first],
        (1, 1, 4): [s_down.finish],
    }
    for g in range(D // GROUP):
        query_cols, key_cols, value_cols = columns(g)
        own_cols = slice(g * GROUP, (g + 1) * GROUP)

        def attend_back(s, query_bias):
            linked = links(seg, counts, s)
            padded = (BLOCKS - 1) * IMG >= counts[s]
            for b in range(BLOCKS):
                below, above, with_below, with_above, offset = neighbour(b, linked)
                rows = slice(b * IMG, (b + 1) * IMG)
                keys = with_other(key_cols, s, b, with_below)
                values = with_other(value_cols, s, b, with_below)
                grad = mixed[block_rows(s, b), own_cols]
                grad_query, grad_keys, grad_values = attend_block_backward(
                    qkv[block_rows(s, b), query_cols],
                    keys,
                    values,
                    grad,
                    lse[(s * 2 + g) * BLOCKS + b],
                    offset,
                )
                own_keys, own_values = grad_keys[:IMG], grad_values[:IMG]
                if b == BLOCKS - 1:
                    grad_query = jnp.where(padded, 0.0, grad_query)
                    own_keys = jnp.where(padded, 0.0, own_keys)
                    own_values = jnp.where(padded, grad.astype(F32), own_values)
                query_bias += col_sum(grad_query)
                qkv[block_rows(s, b), query_cols] = grad_query.astype(BF16)
                if b > 0:
                    own_keys += jnp.where(with_above, key_sum[rows, :], 0.0)
                    own_values += jnp.where(with_above, value_sum[rows, :], 0.0)
                key_sum[rows, :] = own_keys
                value_sum[rows, :] = own_values
                if below is not None:
                    key_sum[below, :] = grad_keys[IMG:]
                    value_sum[below, :] = grad_values[IMG:]
                if above is not None:
                    key_sum[above, :] += jnp.where(with_above, grad_keys[IMG:], 0.0)
                    value_sum[above, :] += jnp.where(with_above, grad_values[IMG:], 0.0)
                for stage in beside_attention.get((g, s, b), ()):
                    squares.append(stage())
            covered = pl.ds(s * SEQ, SPAN)
            grad_tail = mixed[tail_rows(s), own_cols]
            qkv[tail_rows(s), query_cols] = jnp.zeros_like(grad_tail)
            qkv[tail_rows(s), key_cols] = jnp.zeros_like(grad_tail)
            qkv[tail_rows(s), value_cols] = grad_tail
            qkv[covered, key_cols] = key_sum[...].astype(BF16)
            all_values = value_sum[...]
            qkv[covered, value_cols] = all_values.astype(BF16)
            grad_vectors[3:4, own_cols] += col_sum(all_values) + col_sum(grad_tail.astype(F32))
            return query_bias

        query_bias = jnp.zeros((1, GROUP), F32)
        for s in range(seqs):
            query_bias = attend_back(s, query_bias)
        grad_vectors[2:3, own_cols] = query_bias
        if g == 0:
            recall_low.wait()
        total = (sum_low, sum_high)[g]
        for j, cols in enumerate(columns(g)):
            part = dot_tn(low_one[...], qkv[:, cols])
            total[:, :, :, :, j * GROUP : (j + 1) * GROUP] = part.reshape(*total.shape[:-1], GROUP)
        (s_low, s_high)[g].begin()

    for s in range(planes * COLS):
        cols = slice(s * per, (s + 1) * per)
        sum_small[s // COLS, s % COLS, 0, 0:8, 0:per] = grad_vectors[:, cols]
        sum_small[s // COLS, s % COLS, 1, 0:1, 0:long] = grad_bias[:, s * long : (s + 1) * long]
    s_small.begin()

    gain_sum, shift_sum = jnp.zeros((1, D), F32), jnp.zeros((1, D), F32)
    beside_last = {
        0: [s_high.second, s_small.second, s_low.planes],
        1: [s_up.finish, s_high.first],
        2: [s_small.first, s_out.finish, s_high.planes],
        3: [s_small.planes, s_low.finish],
    }
    for k in range(rows_local // ROWS):
        rows = slice(k * ROWS, (k + 1) * ROWS)
        _, hat, spread = norm_forward(tok[rows, :].astype(F32), vectors[0:1, :], vectors[1:2, :])
        grad_one = dot_nt(qkv[rows, :], flat(full_qkv[...]))
        resid[rows, :] += norm_backward(grad_one, hat, spread, vectors[0:1, :])
        pltpu.make_async_copy(resid.at[rows], token_grad.at[rows], grad_sem.at[k]).start()
        gain_sum += col_sum(grad_one * hat)
        shift_sum += col_sum(grad_one)
        for stage in beside_last.get(k, ()):
            squares.append(stage())
    for item in (s_high, s_small):
        squares.append(item.finish())
    part = jnp.zeros((8, 128), F32)
    for item in squares:
        if item is not None:
            part = part + item
    rows = [
        item[:, k * 128 : (k + 1) * 128] for item in (gain_sum, shift_sum) for k in range(D // 128)
    ]
    tiles = jnp.concatenate([*rows, part], axis=0)
    tiles = sum_over_all(p, tiles, out_tiles, in_tiles, t_send, t_recv)
    first_rows[...] = tiles[:8]
    norm[...] = tiles[8:]
    for item in scatters:
        item.drain()
    for k, rows in enumerate(parts):
        pltpu.make_async_copy(resid.at[rows], token_grad.at[rows], grad_sem.at[k]).wait()


def run_layer(planes, seg, counts, tokens, cotangent, masters):
    halves = [item.reshape(2, item.shape[0] // 2, item.shape[1]) for item in masters[:4]]
    per, long = masters[4].shape[1], masters[5].shape[0]
    rows = tokens.shape[0]
    seqs = rows // SEQ
    shapes = [item.shape[1:] for item in halves]
    group = (shapes[0][0], 3 * GROUP)
    sums = [*shapes[1:], group, group, (16, 128)]
    vmem = pl.BlockSpec(memory_space=pltpu.VMEM)
    hbm = pl.BlockSpec(memory_space=pl.ANY)
    dma = pltpu.SemaphoreType.DMA
    scratch = [pltpu.VMEM(five(planes, *shape), BF16) for shape in (*shapes, (16, 128))]
    scratch += [pltpu.VMEM((8, D), F32), pltpu.VMEM((1, FF), F32)]
    scratch += [pltpu.VMEM(five(planes, *shape), F32) for shape in sums]
    scratch += [
        pltpu.VMEM((rows, D), BF16),
        pltpu.VMEM((rows, D), BF16),
        pltpu.VMEM((rows, 3 * D), BF16),
        pltpu.VMEM((rows, D), BF16),
        pltpu.VMEM((rows, D), F32),
        pltpu.VMEM((seqs * 2 * BLOCKS, 1, PER_GROUP * IMG), F32),
        pltpu.VMEM((SPAN, GROUP), F32),
        pltpu.VMEM((SPAN, GROUP), F32),
        pltpu.VMEM((8, D), F32),
        pltpu.VMEM((1, FF), F32),
    ]
    for k, shape in enumerate(sums):
        scratch += Scatter.buffers(planes, *shape, own=k >= 3)
    scratch += [dma((5, Gather.count(planes)))] * 2 + [dma((6, Scatter.count(planes)))] * 2
    scratch += [pltpu.VMEM((3, 16, 128), F32), pltpu.VMEM((planes + COLS + 1, 16, 128), F32)]
    scratch += [dma((planes + 3,))] * 2 + [dma((4,))] + [dma((rows // ROWS,))] * 2
    return pl.pallas_call(
        functools.partial(layer_kernel, planes, per, long),
        in_specs=[SCALAR, SCALAR, hbm, hbm] + [vmem] * 6,
        out_specs=[hbm, hbm] + [vmem] * 8 + [hbm],
        out_shape=[shaped((rows, D), BF16), shaped((rows, D), F32)]
        + [shaped((2, *shape), F32) for shape in sums]
        + [shaped((8, 128), F32), shaped((8, 128), F32), shaped((rows, D), BF16)],
        scratch_shapes=scratch,
        compiler_params=pltpu.CompilerParams(
            vmem_limit_bytes=63 * 2**20, collective_id=1, has_side_effects=True
        ),
        name="layer",
    )(seg, counts, tokens, cotangent, *halves, masters[4], masters[5].reshape(1, -1))


def update_kernel(bound, pieces, *refs):
    sources, targets, rest = refs[:28], refs[28:49], refs[49:]
    held, middles = rest[:26], rest[26:28]
    fresh, total = rest[28:46], rest[46]
    in_sems, out_sems, mid_sems = rest[47:]
    into, out_of = [], []
    for n, (source, middle, target) in enumerate(zip(sources[26:], middles, targets[:2])):
        rows = source.shape[0] // pieces
        for k in range(pieces):
            part, sem = pl.ds(k * rows, rows), mid_sems.at[n, k]
            into.append(pltpu.make_async_copy(source.at[part], middle.at[part], sem))
            out_of.append(pltpu.make_async_copy(middle.at[part], target.at[part], sem))
    loads = [
        pltpu.make_async_copy(source, target, in_sems.at[k])
        for k, (source, target) in enumerate(zip(sources, held))
    ]
    stores = [
        pltpu.make_async_copy(source, target, out_sems.at[k])
        for k, (source, target) in enumerate(zip((total, *fresh), targets[2:]))
    ]
    for copy in (*loads, *into):
        copy.start()
    for copy in loads:
        copy.wait()
    results, first_rows, norm = held[:6], held[6], held[7]
    masters, moments, squares = held[8:14], held[14:20], held[20:26]
    i = lax.axis_index("fsdp")
    first = first_rows[...]
    every = jnp.sum(norm[...], axis=(0, 1), keepdims=True)
    every = every + jnp.sum(first * first, axis=(0, 1), keepdims=True)
    root = jnp.sqrt(every)
    total[...] = root
    stores[0].start()
    factor = jnp.minimum(1.0, bound / root)
    out, up, down, low, high, small = results
    low, high = flat(low[...]), flat(high[...])
    qkv = [item[:, j * GROUP : (j + 1) * GROUP] for j in range(3) for item in (low, high)]
    per = masters[4].shape[1]
    rows = small[0, 0:8, 0:per]
    line = lax.broadcasted_iota(jnp.int32, (8, 1), 0)
    for s in range(D // per):
        at = s * per
        gain = first[at // 128 : at // 128 + 1, at % 128 : at % 128 + per]
        at = D + at
        shift = first[at // 128 : at // 128 + 1, at % 128 : at % 128 + per]
        mine = jnp.where(line == 0, gain, jnp.where(line == 1, shift, rows))
        rows = jnp.where(i == s, mine, rows)
    grads = (
        jnp.concatenate(qkv, axis=1),
        flat(out[...]),
        flat(up[...]),
        flat(down[...]),
        rows,
        small[1, 0:1, 0 : masters[5].shape[1]],
    )
    for k in range(6):
        new = adam_step(
            masters[k][...], moments[k][...], squares[k][...], grads[k], factor, RATES[k]
        )
        for at, item in zip((k, 6 + k, 12 + k), new):
            fresh[at][...] = item
            stores[1 + at].start()
        for first_half, second_half in zip(into[k : k + 2], out_of[k : k + 2]) if k % 2 == 0 else ():
            first_half.wait()
            second_half.start()
    for first_half, second_half in zip(into[6:], out_of[6:]):
        first_half.wait()
        second_half.start()
    for copy in (*stores, *out_of):
        copy.wait()


def run_update(bound, layer_out, token_grad, results, masters, moments, squares):
    def lines(items):
        return [*items[:5], items[5].reshape(1, -1)]

    state = lines(masters) + lines(moments) + lines(squares)
    held = [*results, *state]
    hbm = pl.BlockSpec(memory_space=pl.ANY)
    dma = pltpu.SemaphoreType.DMA
    pieces = 4
    passed = (layer_out, token_grad)
    done = pl.pallas_call(
        functools.partial(update_kernel, bound, pieces),
        in_specs=[hbm] * 28,
        out_specs=[hbm] * 21,
        out_shape=[shaped(item.shape, item.dtype) for item in passed]
        + [shaped((1, 1), F32)]
        + [shaped(item.shape, F32) for item in state],
        scratch_shapes=[pltpu.VMEM(item.shape, item.dtype) for item in (*held, *passed, *state)]
        + [pltpu.VMEM((1, 1), F32), dma((26,)), dma((19,)), dma((2, pieces))],
        compiler_params=vmem_params(),
        name="update_state",
    )(*held, *passed)
    fresh = [item.reshape(-1) if k % 6 == 5 else item for k, item in enumerate(done[3:])]
    return (done[0], done[1], done[2].reshape(()), *fresh)


def compute(tokens, cotangent, segment_ids, valid_counts, full):
    low_qkv, low_out, low_up, low_down, vectors, up_bias = full
    qkv, attended, lse = run_forward(segment_ids, valid_counts, tokens, vectors, low_qkv)
    (
        layer_out,
        grad_resid,
        grad_attended,
        grad_down,
        grad_up,
        grad_out_w,
        late,
        grad_bias,
    ) = run_feed(
        valid_counts, tokens, cotangent, attended, vectors, up_bias, low_out, low_up, low_down
    )
    token_grad, grad_qkv_w, early = run_backward(
        segment_ids,
        valid_counts,
        tokens,
        vectors,
        low_qkv,
        qkv,
        grad_attended,
        grad_resid,
        lse,
    )
    return layer_out, token_grad, (grad_qkv_w, grad_out_w, grad_up, grad_down), early, late, grad_bias


def fast_body(tokens, cotangent, segment_ids, valid_counts, *state):
    masters, moments, squares = state[:6], state[6:12], state[12:18]
    wide = lax.axis_size("fsdp")
    layer_out, token_grad, *results, _ = run_layer(
        wide // COLS, segment_ids, valid_counts, tokens, cotangent, masters
    )
    bound = 0.005 * math.sqrt(tokens.shape[0] * wide * lax.axis_size("dp") * PARAMS)
    return run_update(bound, layer_out, token_grad, results, masters, moments, squares)


def plain_body(tokens, cotangent, segment_ids, valid_counts, *state):
    masters, moments, squares = state[:6], state[6:12], state[12:18]
    wide = lax.axis_size("fsdp")
    replicas = lax.axis_size("dp")
    low = [item.astype(BF16) for item in masters]
    full = [
        lax.all_gather(item, "fsdp", axis=1 if k == 4 else 0, tiled=True)
        for k, item in enumerate(low)
    ]
    full[4] = full[4].astype(F32)
    full[5] = full[5].astype(F32).reshape(1, FF)
    layer_out, token_grad, totals, early, late, bias = compute(
        tokens, cotangent, segment_ids, valid_counts, full
    )
    grads = []
    for k, item in enumerate((*totals, early + late, bias.reshape(FF))):
        shard = lax.psum_scatter(item, "fsdp", scatter_dimension=1 if k == 4 else 0, tiled=True)
        grads.append(lax.psum(shard.astype(BF16), "dp").astype(F32))
    local_total = jnp.sum(grads[0] * grads[0])
    for item in grads[1:]:
        local_total = local_total + jnp.sum(item * item)
    grad_norm = jnp.sqrt(lax.psum(local_total, "fsdp"))
    bound = 0.005 * math.sqrt(tokens.shape[0] * wide * replicas * PARAMS)
    factor = jnp.minimum(1.0, bound / grad_norm)
    fresh = [
        adam_step(masters[k], moments[k], squares[k], grads[k], factor, RATES[k]) for k in range(6)
    ]
    return (
        layer_out,
        token_grad,
        grad_norm,
        *(item[0] for item in fresh),
        *(item[1] for item in fresh),
        *(item[2] for item in fresh),
    )


def solution(mesh):
    rows = P(("fsdp", "dp"), None)
    state = (
        P("fsdp", None),
        P("fsdp", None),
        P("fsdp", None),
        P("fsdp", None),
        P(None, "fsdp"),
        P("fsdp"),
    )
    wide, replicas = mesh.shape["fsdp"], mesh.shape["dp"]
    fits = replicas == 2 and wide == COLS * COLS
    return jax.shard_map(
        fast_body if fits else plain_body,
        mesh=mesh,
        in_specs=(rows, rows, rows, P(("fsdp", "dp")), *state, *state, *state),
        out_specs=(rows, rows, P(), *state, *state, *state),
        check_vma=False,
    )
```

```python
import functools
import math

import jax
import jax.numpy as jnp
from jax import lax
from jax.experimental import pallas as pl
from jax.experimental.pallas import tpu as pltpu
from jax.sharding import PartitionSpec as P

D = 512
HEADS = 8
HEAD_DIM = 64
FF = 2048
SEQ = 1024
IMG = 192
BLOCKS = 5
STEP = 5
PARAMS = 3151872
GROUP = 256
PER_GROUP = GROUP // HEAD_DIM

F32 = jnp.float32
BF16 = jnp.bfloat16

norm_eps = 1e-06
adam_eps = 1e-08
decay_rate = 0.05
beta_first = 0.5
beta_second = 0.5
masked_score = -1e30


def dot(left, right):
    return lax.dot_general(left, right, (((1,), (0,)), ((), ())), preferred_element_type=F32)


def dot_nt(left, right):
    return lax.dot_general(left, right, (((1,), (1,)), ((), ())), preferred_element_type=F32)


def dot_tn(left, right):
    return lax.dot_general(left, right, (((0,), (0,)), ((), ())), preferred_element_type=F32)


def norm_forward(values, gain, shift):
    center = values - jnp.mean(values, axis=-1, keepdims=True)
    spread = lax.rsqrt(jnp.mean(center * center, axis=-1, keepdims=True) + norm_eps)
    hat = center * spread
    return hat * gain + shift, hat, spread


def norm_backward(incoming, hat, spread, gain):
    scaled = incoming * gain
    return spread * (
        scaled
        - jnp.mean(scaled, axis=-1, keepdims=True)
        - hat * jnp.mean(scaled * hat, axis=-1, keepdims=True)
    )


def gelu_pair(values):
    half = 0.5 * (1.0 + lax.erf(values * (1.0 / math.sqrt(2.0))))
    bell = jnp.exp(-0.5 * values * values) * (1.0 / math.sqrt(2.0 * math.pi))
    return values * half, half + values * bell


def col_sum(values):
    return jnp.sum(values, axis=0, keepdims=True)


def head_of_lane():
    return lax.broadcasted_iota(jnp.int32, (1, GROUP), 1) // HEAD_DIM


def stack_heads(rows):
    head = head_of_lane()
    zero = jnp.zeros_like(rows)
    return jnp.concatenate([jnp.where(head == h, rows, zero) for h in range(PER_GROUP)], axis=0)


def unstack_heads(stacked):
    head = head_of_lane()
    n = stacked.shape[0] // PER_GROUP
    rows = stacked[(PER_GROUP - 1) * n :]
    for h in range(PER_GROUP - 2, -1, -1):
        rows = jnp.where(head == h, stacked[h * n : (h + 1) * n], rows)
    return rows


def links(seg, counts, s):
    return [
        (seg[s, b * IMG] == seg[s, (b + 1) * IMG]) & ((b + 1) * IMG < counts[s])
        for b in range(BLOCKS - 1)
    ]


def neighbour(b, linked):
    below = slice((b + 1) * IMG, (b + 2) * IMG) if b < BLOCKS - 1 else None
    above = slice((b - 1) * IMG, b * IMG) if b > 0 else None
    with_below = linked[b] if b < BLOCKS - 1 else jnp.bool_(False)
    with_above = linked[b - 1] if b > 0 else jnp.bool_(False)
    offset = jnp.where(with_below | with_above, 0.0, masked_score)
    return below, above, with_below, with_above, offset


def other_rows(ref, cols, below, above, with_below):
    if above is None:
        return ref[below, cols]
    if below is None:
        return ref[above, cols]
    return jnp.where(with_below, ref[below, cols], ref[above, cols])


def attend_block(query, keys, values, offset):
    stacked = stack_heads(query * jnp.asarray(HEAD_DIM**-0.5, BF16))
    scores = dot_nt(keys, stacked)
    own, other = scores[:IMG], scores[IMG:]
    top = jnp.maximum(
        jnp.max(own, axis=0, keepdims=True), jnp.max(other, axis=0, keepdims=True) + offset
    )
    own = jnp.exp(own - top)
    other = jnp.exp(other - (top - offset))
    total = col_sum(own) + col_sum(other)
    inverse = 1.0 / total
    probs = jnp.concatenate([own * inverse, other * inverse], axis=0).astype(BF16)
    return unstack_heads(dot_tn(probs, values)), top + jnp.log(total)


def attend_block_backward(query, keys, values, grad, lse, offset):
    stacked = stack_heads(query * jnp.asarray(HEAD_DIM**-0.5, BF16))
    grads = stack_heads(grad)
    scores = dot_nt(keys, stacked)
    grad_probs = dot_nt(values, grads)
    own = jnp.exp(scores[:IMG] - lse)
    other = jnp.exp(scores[IMG:] - (lse - offset))
    own_t = own * grad_probs[:IMG]
    other_t = other * grad_probs[IMG:]
    delta = col_sum(own_t) + col_sum(other_t)
    grad_scores = jnp.concatenate([own_t - own * delta, other_t - other * delta], axis=0)
    grad_scores = grad_scores.astype(BF16)
    probs = jnp.concatenate([own, other], axis=0).astype(BF16)
    grad_values = dot(probs, grads)
    grad_keys = dot(grad_scores, stacked)
    grad_query = unstack_heads(dot_tn(grad_scores, keys)) * (HEAD_DIM**-0.5)
    return grad_query, grad_keys, grad_values


def forward_kernel(chunk, seg, counts, tokens, vectors, low_qkv, qkv, attended, lse):
    s = pl.program_id(0)
    bias = jnp.concatenate([vectors[2:3, :], jnp.zeros((1, D), F32), vectors[3:4, :]], axis=1)
    for c in range(SEQ // chunk):
        rows = slice(c * chunk, (c + 1) * chunk)
        normed, _, _ = norm_forward(tokens[rows, :].astype(F32), vectors[0:1, :], vectors[1:2, :])
        qkv[rows, :] = (dot(normed.astype(BF16), low_qkv[...]) + bias).astype(BF16)
    linked = links(seg, counts, s)
    for g in range(D // GROUP):
        query_cols, key_cols, value_cols = [
            slice(j * D + g * GROUP, j * D + (g + 1) * GROUP) for j in range(3)
        ]
        out_cols = slice(g * GROUP, (g + 1) * GROUP)
        for b in range(BLOCKS):
            rows = slice(b * IMG, (b + 1) * IMG)
            below, above, with_below, with_above, offset = neighbour(b, linked)
            keys = jnp.concatenate(
                [qkv[rows, key_cols], other_rows(qkv, key_cols, below, above, with_below)], axis=0
            )
            own_values = qkv[rows, value_cols]
            values = jnp.concatenate(
                [own_values, other_rows(qkv, value_cols, below, above, with_below)], axis=0
            )
            mixed, block_lse = attend_block(qkv[rows, query_cols], keys, values, offset)
            mixed = mixed.astype(BF16)
            if b == BLOCKS - 1:
                mixed = jnp.where(b * IMG >= counts[s], own_values, mixed)
            attended[rows, out_cols] = mixed
            lse[g * BLOCKS + b] = block_lse
        attended[BLOCKS * IMG :, out_cols] = qkv[BLOCKS * IMG :, value_cols]


def feed_kernel(
    rows_in,
    chunk,
    counts,
    tokens,
    cotangent,
    attended,
    vectors,
    up_bias,
    low_out,
    low_up,
    low_down,
    layer_out,
    grad_resid,
    grad_attended,
    grad_down,
    grad_up,
    grad_out_w,
    grad_vectors,
    grad_bias,
):
    i = pl.program_id(0)

    @pl.when(i == 0)
    def _():
        for ref in (grad_down, grad_up, grad_out_w, grad_vectors, grad_bias):
            ref[...] = jnp.zeros_like(ref)

    per = SEQ // rows_in
    mixed = attended[...]
    resid = tokens[...].astype(F32) + (dot(mixed, low_out[...]) + vectors[4:5, :])
    normed, hat, spread = norm_forward(resid, vectors[5:6, :], vectors[6:7, :])
    low_two = normed.astype(BF16)
    position = (i % per) * rows_in + lax.broadcasted_iota(jnp.int32, (rows_in, 1), 0)
    grad = jnp.where(position < counts[i // per], cotangent[...].astype(F32), 0.0)
    grad_low = grad.astype(BF16)
    out = jnp.zeros((rows_in, D), F32)
    grad_two = jnp.zeros((rows_in, D), F32)
    for c in range(FF // chunk):
        cols = slice(c * chunk, (c + 1) * chunk)
        hidden = dot(low_two, low_up[:, cols]) + up_bias[:, cols]
        grad_active = dot_nt(grad_low, low_down[cols, :])
        active, slope = gelu_pair(hidden)
        active = active.astype(BF16)
        grad_hidden = grad_active * slope
        grad_hidden_low = grad_hidden.astype(BF16)
        out += dot(active, low_down[cols, :])
        grad_bias[:, cols] += col_sum(grad_hidden)
        grad_down[cols, :] += dot_tn(active, grad_low)
        grad_up[:, cols] += dot_tn(low_two, grad_hidden_low)
        grad_two += dot_nt(grad_hidden_low, low_up[:, cols])
    layer_out[...] = (resid + (out + vectors[7:8, :])).astype(BF16)
    back = grad + norm_backward(grad_two, hat, spread, vectors[5:6, :])
    back_low = back.astype(BF16)
    grad_resid[...] = back
    grad_out_w[...] += dot_tn(mixed, back_low)
    grad_attended[...] = dot_nt(back_low, low_out[...]).astype(BF16)
    grad_vectors[4:5, :] += col_sum(back)
    grad_vectors[5:6, :] += col_sum(grad_two * hat)
    grad_vectors[6:7, :] += col_sum(grad_two)
    grad_vectors[7:8, :] += col_sum(grad)


def backward_kernel(
    chunk,
    seg,
    counts,
    tokens,
    vectors,
    low_qkv,
    qkv,
    grad_attended,
    grad_resid,
    lse,
    token_grad,
    grad_qkv_w,
    grad_vectors,
    grad_qkv,
    key_sum,
    value_sum,
):
    s = pl.program_id(0)

    @pl.when(s == 0)
    def _():
        grad_qkv_w[...] = jnp.zeros_like(grad_qkv_w)
        grad_vectors[...] = jnp.zeros_like(grad_vectors)

    linked = links(seg, counts, s)
    padded = (BLOCKS - 1) * IMG >= counts[s]
    covered = slice(0, BLOCKS * IMG)
    tail = slice(BLOCKS * IMG, SEQ)
    for g in range(D // GROUP):
        query_cols, key_cols, value_cols = [
            slice(j * D + g * GROUP, j * D + (g + 1) * GROUP) for j in range(3)
        ]
        grad_cols = slice(g * GROUP, (g + 1) * GROUP)
        query_bias = jnp.zeros((1, GROUP), F32)
        for b in range(BLOCKS):
            rows = slice(b * IMG, (b + 1) * IMG)
            below, above, with_below, with_above, offset = neighbour(b, linked)
            keys = jnp.concatenate(
                [qkv[rows, key_cols], other_rows(qkv, key_cols, below, above, with_below)], axis=0
            )
            values = jnp.concatenate(
                [qkv[rows, value_cols], other_rows(qkv, value_cols, below, above, with_below)],
                axis=0,
            )
            grad = grad_attended[rows, grad_cols]
            grad_query, grad_keys, grad_values = attend_block_backward(
                qkv[rows, query_cols], keys, values, grad, lse[g * BLOCKS + b], offset
            )
            own_keys, own_values = grad_keys[:IMG], grad_values[:IMG]
            if b == BLOCKS - 1:
                grad_query = jnp.where(padded, 0.0, grad_query)
                own_keys = jnp.where(padded, 0.0, own_keys)
                own_values = jnp.where(padded, grad.astype(F32), own_values)
            query_bias += col_sum(grad_query)
            grad_qkv[rows, query_cols] = grad_query.astype(BF16)
            if b > 0:
                own_keys += jnp.where(with_above, key_sum[rows, :], 0.0)
                own_values += jnp.where(with_above, value_sum[rows, :], 0.0)
            key_sum[rows, :] = own_keys
            value_sum[rows, :] = own_values
            if below is not None:
                key_sum[below, :] = grad_keys[IMG:]
                value_sum[below, :] = grad_values[IMG:]
            if above is not None:
                key_sum[above, :] += jnp.where(with_above, grad_keys[IMG:], 0.0)
                value_sum[above, :] += jnp.where(with_above, grad_values[IMG:], 0.0)
        grad_tail = grad_attended[tail, grad_cols]
        grad_qkv[tail, query_cols] = jnp.zeros_like(grad_tail)
        grad_qkv[tail, key_cols] = jnp.zeros_like(grad_tail)
        grad_qkv[tail, value_cols] = grad_tail
        grad_qkv[covered, key_cols] = key_sum[...].astype(BF16)
        all_values = value_sum[...]
        grad_qkv[covered, value_cols] = all_values.astype(BF16)
        grad_vectors[2:3, grad_cols] += query_bias
        grad_vectors[3:4, grad_cols] += col_sum(all_values) + col_sum(grad_tail.astype(F32))
    for c in range(SEQ // chunk):
        rows = slice(c * chunk, (c + 1) * chunk)
        normed, hat, spread = norm_forward(
            tokens[rows, :].astype(F32), vectors[0:1, :], vectors[1:2, :]
        )
        grad = grad_qkv[rows, :]
        grad_qkv_w[...] += dot_tn(normed.astype(BF16), grad)
        grad_one = dot_nt(grad, low_qkv[...])
        token_grad[rows, :] = grad_resid[rows, :] + norm_backward(
            grad_one, hat, spread, vectors[0:1, :]
        )
        grad_vectors[0:1, :] += col_sum(grad_one * hat)
        grad_vectors[1:2, :] += col_sum(grad_one)


def vmem_params():
    return pltpu.CompilerParams(vmem_limit_bytes=60 * 2**20)


def by_rows(rows, cols):
    return pl.BlockSpec((rows, cols), lambda i: (i, 0))


def whole(*shape):
    return pl.BlockSpec(shape, lambda i: (0,) * len(shape))


def stats_spec():
    return pl.BlockSpec((2 * BLOCKS, 1, PER_GROUP * IMG), lambda i: (i, 0, 0))


def shaped(shape, dtype):
    return jax.ShapeDtypeStruct(shape, dtype)


SCALAR = pl.BlockSpec(memory_space=pltpu.SMEM)


def run_forward(seg, counts, tokens, vectors, low_qkv):
    rows = tokens.shape[0]
    seqs = rows // SEQ
    return pl.pallas_call(
        functools.partial(forward_kernel, 256),
        grid=(seqs,),
        in_specs=[SCALAR, SCALAR, by_rows(SEQ, D), whole(8, D), whole(D, 3 * D)],
        out_specs=[by_rows(SEQ, 3 * D), by_rows(SEQ, D), stats_spec()],
        out_shape=[
            shaped((rows, 3 * D), BF16),
            shaped((rows, D), BF16),
            shaped((seqs * 2 * BLOCKS, 1, PER_GROUP * IMG), F32),
        ],
        compiler_params=vmem_params(),
        name="attend_forward",
    )(seg, counts, tokens, vectors, low_qkv)


def run_feed(counts, tokens, cotangent, attended, vectors, up_bias, low_out, low_up, low_down):
    rows = tokens.shape[0]
    step = 512
    return pl.pallas_call(
        functools.partial(feed_kernel, step, 512),
        grid=(rows // step,),
        in_specs=[
            SCALAR,
            by_rows(step, D),
            by_rows(step, D),
            by_rows(step, D),
            whole(8, D),
            whole(1, FF),
            whole(D, D),
            whole(D, FF),
            whole(FF, D),
        ],
        out_specs=[
            by_rows(step, D),
            by_rows(step, D),
            by_rows(step, D),
            whole(FF, D),
            whole(D, FF),
            whole(D, D),
            whole(8, D),
            whole(1, FF),
        ],
        out_shape=[
            shaped((rows, D), BF16),
            shaped((rows, D), F32),
            shaped((rows, D), BF16),
            shaped((FF, D), F32),
            shaped((D, FF), F32),
            shaped((D, D), F32),
            shaped((8, D), F32),
            shaped((1, FF), F32),
        ],
        compiler_params=vmem_params(),
        name="feed_forward",
    )(counts, tokens, cotangent, attended, vectors, up_bias, low_out, low_up, low_down)


def run_backward(seg, counts, tokens, vectors, low_qkv, qkv, grad_attended, grad_resid, lse):
    rows = tokens.shape[0]
    return pl.pallas_call(
        functools.partial(backward_kernel, 512),
        grid=(rows // SEQ,),
        in_specs=[
            SCALAR,
            SCALAR,
            by_rows(SEQ, D),
            whole(8, D),
            whole(D, 3 * D),
            by_rows(SEQ, 3 * D),
            by_rows(SEQ, D),
            by_rows(SEQ, D),
            stats_spec(),
        ],
        out_specs=[by_rows(SEQ, D), whole(D, 3 * D), whole(8, D)],
        out_shape=[
            shaped((rows, D), F32),
            shaped((D, 3 * D), F32),
            shaped((8, D), F32),
        ],
        scratch_shapes=[
            pltpu.VMEM((SEQ, 3 * D), BF16),
            pltpu.VMEM((BLOCKS * IMG, GROUP), F32),
            pltpu.VMEM((BLOCKS * IMG, GROUP), F32),
        ],
        compiler_params=vmem_params(),
        name="attend_backward",
    )(seg, counts, tokens, vectors, low_qkv, qkv, grad_attended, grad_resid, lse)


def adam_step(weight, moment, square, grad, factor, rate):
    clipped = grad * factor
    moment_new = beta_first * moment + (1.0 - beta_first) * clipped
    square_new = beta_second * square + (1.0 - beta_second) * clipped * clipped
    first_hat = moment_new / (1.0 - beta_first**STEP)
    second_hat = square_new / (1.0 - beta_second**STEP)
    weight_new = weight - rate * (
        first_hat / (jnp.sqrt(second_hat) + adam_eps) + decay_rate * weight
    )
    return (weight_new, moment_new, square_new)


RATES = (
    2.0 / math.sqrt(D),
    8.0 / math.sqrt(D),
    2.0 / math.sqrt(D),
    2.0 / math.sqrt(FF),
    0.5,
    0.5,
)


MESH = pl.DeviceIdType.MESH
COLS = 4


class Place:
    def __init__(self, planes):
        self.planes = planes
        self.i = lax.axis_index("fsdp")
        self.c = c = lax.axis_index("dp")
        self.q = q = lax.rem(self.i, COLS)
        self.z = self.i // COLS
        x, y = lax.rem(q, 2), q // 2
        self.qx = y * 2 + (1 - x)
        self.qy = (1 - y) * 2 + x
        self.qa = c * self.qx + (1 - c) * self.qy
        self.qb = c * self.qy + (1 - c) * self.qx
        self.qd = COLS - 1 - q
        self.at_a = (self.z * COLS + self.qa, c)
        self.at_b = (self.z * COLS + self.qb, c)
        self.at_x = (self.z * COLS + self.qx, c)
        self.at_y = (self.z * COLS + self.qy, c)
        self.at_d = (self.z * COLS + self.qd, c)
        self.partner = (self.i, 1 - c)

    def plane(self, step):
        return lax.rem(self.z + step, self.planes)

    def along(self, step):
        return (self.plane(step) * COLS + self.q, self.c)

    def greet(self):
        barrier = pltpu.get_barrier_semaphore()
        friends = [self.along(step) for step in range(1, self.planes)]
        friends += [self.at_a, self.at_b, self.at_d, self.partner]
        for device in friends:
            pl.semaphore_signal(barrier, inc=1, device_id=device, device_id_type=MESH)
        pl.semaphore_wait(barrier, len(friends))


def remote(source, target, send, recv, device):
    return pltpu.make_async_remote_copy(
        src_ref=source,
        dst_ref=target,
        send_sem=send,
        recv_sem=recv,
        device_id=device,
        device_id_type=MESH,
    )


class Gather:
    def __init__(self, place, full, send, recv):
        p, c = place, place.c
        n = p.planes
        self.pieces = n

        def move(k, plane, col, device):
            ref = full.at[plane, col, c]
            return remote(ref, ref, send.at[k], recv.at[k], device)

        self.to_z = [move(k, p.z, p.q, p.along(k + 1)) for k in range(n - 1)]
        base = n - 1
        self.to_a = [move(base + d, p.plane(n - d), p.q, p.at_a) for d in range(n)]
        self.to_b = [move(base + n + d, p.plane(n - d), p.q, p.at_b) for d in range(n)]
        self.on_b = [move(base + 2 * n + d, p.plane(n - d), p.qa, p.at_b) for d in range(n)]
        base += 3 * n
        self.to_core = [
            move(base + k, slice(None), col, p.partner)
            for k, col in enumerate((p.q, p.qa, p.qb, p.qd))
        ]

    @staticmethod
    def count(planes):
        return 4 * planes + 3

    def begin(self):
        for copy in self.to_z:
            copy.start()

    def begin_own(self):
        self.to_a[0].start()
        self.to_b[0].start()

    def spread(self):
        for k, copy in enumerate(self.to_z):
            copy.wait_recv()
            self.to_a[k + 1].start()
            self.to_b[k + 1].start()
        self.to_core[0].start()

    def forward(self):
        for k in range(self.pieces):
            self.to_a[k].wait_recv()
            self.on_b[k].start()
        self.to_core[1].start()

    def last(self):
        for copy in self.to_b:
            copy.wait_recv()
        self.to_core[2].start()
        for copy in self.on_b:
            copy.wait_recv()
        self.to_core[3].start()

    def arrive(self):
        for copy in self.to_core:
            copy.wait_recv()

    def drain(self):
        for copy in (*self.to_z, *self.to_a, *self.to_b, *self.on_b, *self.to_core):
            copy.wait_send()


class Scatter:
    def __init__(self, place, total, bufs, result, send, recv, squares):
        self.place, self.total, self.result, self.squares = place, total, result, squares
        self.in_c, self.out_b, self.in_b = bufs[:3]
        self.out_a, self.in_a, self.out_z, self.in_z = bufs[3:7]
        self.out_c = bufs[7]
        p = place
        self.order = (p.qa, p.qd, p.qb, p.q)
        self.to_core = [
            remote(self.out_c.at[k], self.in_c.at[k], send.at[k], recv.at[k], p.partner)
            for k in range(4)
        ]
        self.to_b = [
            remote(self.out_b.at[k], self.in_b.at[k], send.at[4 + k], recv.at[4 + k], p.at_b)
            for k in range(2)
        ]
        self.to_a = remote(self.out_a, self.in_a, send.at[6], recv.at[6], p.at_a)
        self.to_z = [
            remote(self.out_z.at[k], self.in_z.at[k], send.at[7 + k], recv.at[7 + k], p.along(k + 1))
            for k in range(p.planes - 1)
        ]
        n = 6 + p.planes
        half = result.at[p.c]
        self.to_both = remote(half, half, send.at[n], recv.at[n], p.partner)

    @staticmethod
    def count(planes):
        return planes + 7

    @staticmethod
    def buffers(planes, rows, cols, own=True):
        shapes = [(4, planes)] + [(2, planes)] * 2 + [(planes,)] * 2 + [(planes - 1,)] * 2
        shapes += [(4, planes)] if own else []
        return [pltpu.VMEM((*shape, rows, cols), BF16) for shape in shapes]

    def begin(self):
        for k in range(4):
            self.out_c[k] = self.total[:, self.order[k], 1 - self.place.c].astype(BF16)
            self.to_core[k].start()

    def second(self):
        p = self.place
        for k, col in ((1, p.qd), (0, p.qb)):
            self.to_core[k].wait_recv()
            mine = self.total[:, col, p.c] + self.in_c[k].astype(F32)
            self.out_b[k] = mine.astype(BF16)
            self.to_b[k].start()

    def first(self):
        p = self.place
        self.to_core[2].wait_recv()
        self.to_b[1].wait_recv()
        mine = self.total[:, p.qa, p.c] + self.in_c[2].astype(F32) + self.in_b[1].astype(F32)
        self.out_a[...] = mine.astype(BF16)
        self.to_a.start()

    def planes(self):
        p = self.place
        self.to_core[3].wait_recv()
        self.to_b[0].wait_recv()
        self.to_a.wait_recv()

        def mine(z):
            local = self.total[z, p.q, p.c] + self.in_c[3, z].astype(F32)
            return local + self.in_b[0, z].astype(F32) + self.in_a[z].astype(F32)

        for k in range(p.planes - 1):
            self.out_z[k] = mine(p.plane(k + 1)).astype(BF16)
            self.to_z[k].start()
        self.result[p.c] = mine(p.z)

    def finish(self):
        p = self.place
        for copy in self.to_z:
            copy.wait_recv()
        shard = self.result[p.c]
        for k in range(p.planes - 1):
            shard = shard + self.in_z[k].astype(F32)
        self.result[p.c] = shard
        self.to_both.start()
        square = shard * shard
        lanes = sum(square[:, k : k + 128] for k in range(0, square.shape[1], 128))
        self.squares[...] += jnp.sum(lanes.reshape(-1, 8, 128), axis=0)

    def drain(self):
        self.to_both.wait_recv()
        for copy in (*self.to_core, *self.to_b, self.to_a, *self.to_z, self.to_both):
            copy.wait_send()


def sum_over_all(place, part, out, slots, send, recv):
    p = place
    count = p.planes + COLS - 1
    out[0] = part
    copies = [remote(out.at[0], slots.at[count + 1], send.at[0], recv.at[0], p.partner)]
    copies[0].start()
    copies[0].wait_recv()
    chip = part + slots[count + 1]
    out[1] = chip
    slots[p.z] = chip
    lines = [
        remote(out.at[1], slots.at[p.z], send.at[k + 1], recv.at[k + 1], p.along(k + 1))
        for k in range(p.planes - 1)
    ]
    for copy in lines:
        copy.start()
    for copy in lines:
        copy.wait_recv()
    column = slots[0]
    for k in range(1, p.planes):
        column = column + slots[k]
    out[2] = column
    slots[p.planes + p.q] = column
    columns = [
        remote(out.at[2], slots.at[p.planes + p.q], send.at[n], recv.at[n], device)
        for n, device in enumerate((p.at_x, p.at_y, p.at_d), p.planes)
    ]
    for copy in columns:
        copy.start()
    for copy in columns:
        copy.wait_recv()
    total = slots[p.planes]
    for k in range(1, COLS):
        total = total + slots[p.planes + k]
    for copy in (*copies, *lines, *columns):
        copy.wait_send()
    return total


def small_shard(place, vectors, up_bias):
    def tile(rows):
        for axis, full in ((1, 128), (0, 8)):
            short = list(rows.shape)
            short[axis] = full - short[axis]
            if short[axis]:
                rows = jnp.concatenate([rows, jnp.zeros(short, F32)], axis=axis)
        return rows

    rows, bias = tile(vectors[...]), tile(up_bias[...])
    half = jnp.where(place.c == 0, rows, bias)
    return jnp.concatenate([half, jnp.zeros((8, 128), F32)], axis=0).astype(BF16)


ROWS = 512
SPAN = SEQ // IMG * IMG


def five(planes, rows, cols):
    return (planes, COLS, 2, rows, cols)


def flat(value):
    return value.reshape(-1, value.shape[-1])


def layer_kernel(planes, per, long, *refs):
    seg, counts, tokens, cotangent = refs[:4]
    shards, vector_shard, bias_shard = refs[4:8], refs[8], refs[9]
    layer_out, token_grad = refs[10:12]
    results, first_rows, norm, kept = refs[12:18], refs[18], refs[19], refs[20]
    full, small, vectors, up_bias = refs[21:25], refs[25], refs[26], refs[27]
    totals = refs[28:34]
    tok, cot, qkv, mixed, resid, lse, key_sum, value_sum = refs[34:42]
    grad_vectors, grad_bias = refs[42:44]
    bufs = refs[44:89]
    g_send, g_recv, s_send, s_recv = refs[89:93]
    out_tiles, in_tiles, t_send, t_recv, load_sem, out_sem, grad_sem = refs[93:100]
    square_sum = refs[100]
    full_qkv, full_out, full_up, full_down = full
    sum_out, sum_up, sum_down, sum_low, sum_high, sum_small = totals
    p = Place(planes)
    rows_local = tok.shape[0]
    seqs = rows_local // SEQ

    low_one = cot
    load_tokens = pltpu.make_async_copy(tokens, tok, load_sem.at[0])
    load_cotangent = pltpu.make_async_copy(cotangent, cot, load_sem.at[1])
    keep_low = pltpu.make_async_copy(low_one, kept, load_sem.at[2])
    recall_low = pltpu.make_async_copy(kept, low_one, load_sem.at[3])
    load_tokens.start()

    small[p.z, p.q, p.c] = small_shard(p, vector_shard, bias_shard)
    for shard, target in zip(shards, full):
        target[p.z, p.q, p.c] = shard[p.c].astype(BF16)
    p.greet()
    g_small, g_qkv, g_out, g_up, g_down = gathers = [
        Gather(p, ref, g_send.at[k], g_recv.at[k]) for k, ref in enumerate((small, *full))
    ]
    spare = [ref.at[:, :, 0] for ref in full[1:]]
    bufs = [[*bufs[7 * k : 7 * k + 7], spare[k]] for k in range(3)] + [
        bufs[21 + 8 * k : 29 + 8 * k] for k in range(3)
    ]
    scatters = [
        Scatter(p, total, bufs[k], results[k], s_send.at[k], s_recv.at[k], square_sum)
        for k, total in enumerate(totals)
    ]
    s_out, s_up, s_down, s_low, s_high, s_small = scatters
    g_small.begin()
    g_qkv.begin()
    for item in gathers:
        item.begin_own()
    g_small.spread()
    g_qkv.spread()
    for item in (g_out, g_up, g_down):
        item.begin()
    g_small.forward()
    g_qkv.forward()
    g_out.spread()
    g_small.last()
    g_qkv.last()
    g_small.arrive()
    for s in range(planes * COLS):
        rows = small[s // COLS, s % COLS, 0].astype(F32)
        bias = small[s // COLS, s % COLS, 1].astype(F32)
        vectors[:, s * per : (s + 1) * per] = rows[:8, :per]
        up_bias[:, s * long : (s + 1) * long] = bias[:1, :long]
    load_tokens.wait()
    g_qkv.arrive()

    qkv_bias = jnp.concatenate([vectors[2:3, :], jnp.zeros((1, D), F32), vectors[3:4, :]], axis=1)
    chunk = 256
    beside_qkv = {
        0: [g_out.forward],
        2: [g_up.spread],
        5: [g_out.last],
        7: [g_up.forward],
    }

    def stages_at(k, table):
        for at, stages in table.items():

            @pl.when(k == at)
            def _(stages=stages):
                for stage in stages:
                    stage()

    @pl.loop(0, rows_local // chunk)
    def _(k):
        rows = pl.ds(pl.multiple_of(k * chunk, chunk), chunk)
        normed, _, _ = norm_forward(tok[rows, :].astype(F32), vectors[0:1, :], vectors[1:2, :])
        low = normed.astype(BF16)
        low_one[rows, :] = low
        qkv[rows, :] = (dot(low, flat(full_qkv[...])) + qkv_bias).astype(BF16)
        stages_at(k, beside_qkv)

    g_down.spread()
    keep_low.start()

    def block_rows(s, b):
        return pl.ds(pl.multiple_of(s * SEQ + b * IMG, 64), IMG)

    def tail_rows(s):
        return pl.ds(pl.multiple_of(s * SEQ + SPAN, 64), SEQ - SPAN)

    def columns(g):
        return [slice(j * D + g * GROUP, j * D + (g + 1) * GROUP) for j in range(3)]

    def with_other(cols, s, b, with_below):
        own = qkv[block_rows(s, b), cols]
        if b == 0:
            other = qkv[block_rows(s, 1), cols]
        elif b == BLOCKS - 1:
            other = qkv[block_rows(s, b - 1), cols]
        else:
            other = jnp.where(
                with_below, qkv[block_rows(s, b + 1), cols], qkv[block_rows(s, b - 1), cols]
            )
        return jnp.concatenate([own, other], axis=0)

    for g in range(D // GROUP):
        query_cols, key_cols, value_cols = columns(g)
        own_cols = slice(g * GROUP, (g + 1) * GROUP)

        def attend(s):
            linked = links(seg, counts, s)
            for b in range(BLOCKS):
                _, _, with_below, _, offset = neighbour(b, linked)
                keys = with_other(key_cols, s, b, with_below)
                values = with_other(value_cols, s, b, with_below)
                block, block_lse = attend_block(
                    qkv[block_rows(s, b), query_cols], keys, values, offset
                )
                block = block.astype(BF16)
                if b == BLOCKS - 1:
                    block = jnp.where(b * IMG >= counts[s], values[:IMG], block)
                mixed[block_rows(s, b), own_cols] = block
                lse[(s * 2 + g) * BLOCKS + b] = block_lse
            mixed[tail_rows(s), own_cols] = qkv[tail_rows(s), value_cols]

        pl.loop(0, seqs)(attend)
        if g == 0:
            g_up.last()
            g_down.forward()
            keep_low.wait()
            load_cotangent.start()
        else:
            g_down.last()

    for item in (g_out, g_up, g_down):
        item.arrive()
    load_cotangent.wait()

    for ref in (sum_out, sum_up, sum_down, sum_small, grad_vectors, grad_bias, square_sum):
        ref[...] = jnp.zeros_like(ref)
    width = FF // planes

    def feed(i, carry):
        rows = pl.ds(pl.multiple_of(i * ROWS, ROWS), ROWS)
        block = mixed[rows, :]
        low_out = flat(full_out[...])
        res = tok[rows, :].astype(F32) + (dot(block, low_out) + vectors[4:5, :])
        normed, hat, spread = norm_forward(res, vectors[5:6, :], vectors[6:7, :])
        low_two = normed.astype(BF16)
        position = (i % (SEQ // ROWS)) * ROWS + lax.broadcasted_iota(jnp.int32, (ROWS, 1), 0)
        grad = jnp.where(position < counts[i // (SEQ // ROWS)], cot[rows, :].astype(F32), 0.0)
        grad_low = grad.astype(BF16)
        out = jnp.zeros((ROWS, D), F32)
        grad_two = jnp.zeros((ROWS, D), F32)
        for k in range(planes):
            cols = slice(k * width, (k + 1) * width)
            up = flat(full_up[:, :, :, :, cols])
            down = flat(full_down[k])
            hidden = dot(low_two, up) + up_bias[:, cols]
            grad_active = dot_nt(grad_low, down)
            active, slope = gelu_pair(hidden)
            active = active.astype(BF16)
            grad_hidden = grad_active * slope
            grad_hidden_low = grad_hidden.astype(BF16)
            out += dot(active, down)
            grad_bias[:, cols] += col_sum(grad_hidden)
            sum_down[k] += dot_tn(active, grad_low).reshape(sum_down.shape[1:])
            sum_up[:, :, :, :, cols] += dot_tn(low_two, grad_hidden_low).reshape(
                *sum_up.shape[:-1], width
            )
            grad_two += dot_nt(grad_hidden_low, up)
        cot[rows, :] = (res + (out + vectors[7:8, :])).astype(BF16)
        pltpu.make_async_copy(cot.at[rows], layer_out.at[rows], out_sem.at[i]).start()
        back = grad + norm_backward(grad_two, hat, spread, vectors[5:6, :])
        back_low = back.astype(BF16)
        resid[rows, :] = back
        sum_out[...] += dot_tn(block, back_low).reshape(sum_out.shape)
        mixed[rows, :] = dot_nt(back_low, low_out).astype(BF16)
        grad_vectors[4:5, :] += col_sum(back)
        grad_vectors[5:6, :] += col_sum(grad_two * hat)
        grad_vectors[6:7, :] += col_sum(grad_two)
        grad_vectors[7:8, :] += col_sum(grad)
        return carry

    lax.fori_loop(0, rows_local // ROWS, feed, 0)

    for item in gathers:
        item.drain()
    s_down.begin()
    s_up.begin()
    s_out.begin()
    parts = [slice(k * ROWS, (k + 1) * ROWS) for k in range(rows_local // ROWS)]
    layer_copies = [
        pltpu.make_async_copy(cot.at[rows], layer_out.at[rows], out_sem.at[k])
        for k, rows in enumerate(parts)
    ]

    def recall():
        for copy in layer_copies:
            copy.wait()
        recall_low.start()

    beside_attention = {
        (0, 0, 1): [s_down.second, s_up.second, s_out.second],
        (0, 1, 1): [s_down.first, recall],
        (1, 0, 1): [s_up.first, s_down.planes, s_low.second],
        (1, 1, 1): [s_out.first, s_up.planes],
    }
    for g in range(D // GROUP):
        query_cols, key_cols, value_cols = columns(g)
        own_cols = slice(g * GROUP, (g + 1) * GROUP)

        def attend_back(s, query_bias):
            linked = links(seg, counts, s)
            padded = (BLOCKS - 1) * IMG >= counts[s]
            for b in range(BLOCKS):
                below, above, with_below, with_above, offset = neighbour(b, linked)
                rows = slice(b * IMG, (b + 1) * IMG)
                keys = with_other(key_cols, s, b, with_below)
                values = with_other(value_cols, s, b, with_below)
                grad = mixed[block_rows(s, b), own_cols]
                grad_query, grad_keys, grad_values = attend_block_backward(
                    qkv[block_rows(s, b), query_cols],
                    keys,
                    values,
                    grad,
                    lse[(s * 2 + g) * BLOCKS + b],
                    offset,
                )
                own_keys, own_values = grad_keys[:IMG], grad_values[:IMG]
                if b == BLOCKS - 1:
                    grad_query = jnp.where(padded, 0.0, grad_query)
                    own_keys = jnp.where(padded, 0.0, own_keys)
                    own_values = jnp.where(padded, grad.astype(F32), own_values)
                query_bias += col_sum(grad_query)
                qkv[block_rows(s, b), query_cols] = grad_query.astype(BF16)
                if b > 0:
                    own_keys += jnp.where(with_above, key_sum[rows, :], 0.0)
                    own_values += jnp.where(with_above, value_sum[rows, :], 0.0)
                key_sum[rows, :] = own_keys
                value_sum[rows, :] = own_values
                if below is not None:
                    key_sum[below, :] = grad_keys[IMG:]
                    value_sum[below, :] = grad_values[IMG:]
                if above is not None:
                    key_sum[above, :] += jnp.where(with_above, grad_keys[IMG:], 0.0)
                    value_sum[above, :] += jnp.where(with_above, grad_values[IMG:], 0.0)
                stages_at(s, {k[1]: v for k, v in beside_attention.items() if k[::2] == (g, b)})
            covered = pl.ds(pl.multiple_of(s * SEQ, SEQ), SPAN)
            grad_tail = mixed[tail_rows(s), own_cols]
            qkv[tail_rows(s), query_cols] = jnp.zeros_like(grad_tail)
            qkv[tail_rows(s), key_cols] = jnp.zeros_like(grad_tail)
            qkv[tail_rows(s), value_cols] = grad_tail
            qkv[covered, key_cols] = key_sum[...].astype(BF16)
            all_values = value_sum[...]
            qkv[covered, value_cols] = all_values.astype(BF16)
            grad_vectors[3:4, own_cols] += col_sum(all_values) + col_sum(grad_tail.astype(F32))
            return query_bias

        grad_vectors[2:3, own_cols] = lax.fori_loop(
            0, seqs, attend_back, jnp.zeros((1, GROUP), F32)
        )
        if g == 0:
            recall_low.wait()
        total = (sum_low, sum_high)[g]
        for j, cols in enumerate(columns(g)):
            part = dot_tn(low_one[...], qkv[:, cols])
            total[:, :, :, :, j * GROUP : (j + 1) * GROUP] = part.reshape(*total.shape[:-1], GROUP)
        (s_low, s_high)[g].begin()
        if g == 1:
            s_low.first()
            s_out.planes()

    for s in range(planes * COLS):
        cols = slice(s * per, (s + 1) * per)
        sum_small[s // COLS, s % COLS, 0, 0:8, 0:per] = grad_vectors[:, cols]
        sum_small[s // COLS, s % COLS, 1, 0:1, 0:long] = grad_bias[:, s * long : (s + 1) * long]
    s_small.begin()

    beside_last = {
        0: [s_high.second, s_small.second, s_down.finish],
        1: [s_high.first, s_small.first, s_low.planes],
        2: [s_high.planes, s_small.planes, s_up.finish],
        3: [s_out.finish, s_low.finish],
    }

    @pl.loop(0, rows_local // ROWS)
    def _(k):
        rows = pl.ds(pl.multiple_of(k * ROWS, ROWS), ROWS)
        _, hat, spread = norm_forward(tok[rows, :].astype(F32), vectors[0:1, :], vectors[1:2, :])
        grad_one = dot_nt(qkv[rows, :], flat(full_qkv[...]))
        resid[rows, :] += norm_backward(grad_one, hat, spread, vectors[0:1, :])
        pltpu.make_async_copy(resid.at[rows], token_grad.at[rows], grad_sem.at[k]).start()
        grad_vectors[0:1, :] += col_sum(grad_one * hat)
        grad_vectors[1:2, :] += col_sum(grad_one)
        stages_at(k, beside_last)

    for item in (s_high, s_small):
        item.finish()
    part = square_sum[...]
    gain_sum, shift_sum = grad_vectors[0:1, :], grad_vectors[1:2, :]
    rows = [
        item[:, k * 128 : (k + 1) * 128] for item in (gain_sum, shift_sum) for k in range(D // 128)
    ]
    tiles = jnp.concatenate([*rows, part], axis=0)
    tiles = sum_over_all(p, tiles, out_tiles, in_tiles, t_send, t_recv)
    first_rows[...] = tiles[:8]
    norm[...] = tiles[8:]
    for item in scatters:
        item.drain()
    for k, rows in enumerate(parts):
        pltpu.make_async_copy(resid.at[rows], token_grad.at[rows], grad_sem.at[k]).wait()


def run_layer(planes, seg, counts, tokens, cotangent, masters):
    halves = [item.reshape(2, item.shape[0] // 2, item.shape[1]) for item in masters[:4]]
    per, long = masters[4].shape[1], masters[5].shape[0]
    rows = tokens.shape[0]
    seqs = rows // SEQ
    shapes = [item.shape[1:] for item in halves]
    group = (shapes[0][0], 3 * GROUP)
    sums = [*shapes[1:], group, group, (16, 128)]
    vmem = pl.BlockSpec(memory_space=pltpu.VMEM)
    hbm = pl.BlockSpec(memory_space=pl.ANY)
    dma = pltpu.SemaphoreType.DMA
    scratch = [pltpu.VMEM(five(planes, *shape), BF16) for shape in (*shapes, (16, 128))]
    scratch += [pltpu.VMEM((8, D), F32), pltpu.VMEM((1, FF), F32)]
    scratch += [pltpu.VMEM(five(planes, *shape), F32) for shape in sums]
    scratch += [
        pltpu.VMEM((rows, D), BF16),
        pltpu.VMEM((rows, D), BF16),
        pltpu.VMEM((rows, 3 * D), BF16),
        pltpu.VMEM((rows, D), BF16),
        pltpu.VMEM((rows, D), F32),
        pltpu.VMEM((seqs * 2 * BLOCKS, 1, PER_GROUP * IMG), F32),
        pltpu.VMEM((SPAN, GROUP), F32),
        pltpu.VMEM((SPAN, GROUP), F32),
        pltpu.VMEM((8, D), F32),
        pltpu.VMEM((1, FF), F32),
    ]
    for k, shape in enumerate(sums):
        scratch += Scatter.buffers(planes, *shape, own=k >= 3)
    scratch += [dma((5, Gather.count(planes)))] * 2 + [dma((6, Scatter.count(planes)))] * 2
    scratch += [pltpu.VMEM((3, 16, 128), F32), pltpu.VMEM((planes + COLS + 1, 16, 128), F32)]
    scratch += [dma((planes + 3,))] * 2 + [dma((4,))] + [dma((rows // ROWS,))] * 2
    scratch += [pltpu.VMEM((8, 128), F32)]
    return pl.pallas_call(
        functools.partial(layer_kernel, planes, per, long),
        in_specs=[SCALAR, SCALAR, hbm, hbm] + [vmem] * 6,
        out_specs=[hbm, hbm] + [vmem] * 8 + [hbm],
        out_shape=[shaped((rows, D), BF16), shaped((rows, D), F32)]
        + [shaped((2, *shape), F32) for shape in sums]
        + [shaped((8, 128), F32), shaped((8, 128), F32), shaped((rows, D), BF16)],
        scratch_shapes=scratch,
        compiler_params=pltpu.CompilerParams(
            vmem_limit_bytes=63 * 2**20, collective_id=1, has_side_effects=True
        ),
        name="layer",
    )(seg, counts, tokens, cotangent, *halves, masters[4], masters[5].reshape(1, -1))


def update_kernel(bound, pieces, *refs):
    sources, targets, rest = refs[:28], refs[28:49], refs[49:]
    held, middles = rest[:26], rest[26:28]
    fresh, total = rest[28:46], rest[46]
    in_sems, out_sems, mid_sems = rest[47:]
    into, out_of = [], []
    for n, (source, middle, target) in enumerate(zip(sources[26:], middles, targets[:2])):
        rows = source.shape[0] // pieces
        for k in range(pieces):
            part, sem = pl.ds(k * rows, rows), mid_sems.at[n, k]
            into.append(pltpu.make_async_copy(source.at[part], middle.at[part], sem))
            out_of.append(pltpu.make_async_copy(middle.at[part], target.at[part], sem))
    loads = [
        pltpu.make_async_copy(source, target, in_sems.at[k])
        for k, (source, target) in enumerate(zip(sources, held))
    ]
    stores = [
        pltpu.make_async_copy(source, target, out_sems.at[k])
        for k, (source, target) in enumerate(zip((total, *fresh), targets[2:]))
    ]
    for copy in (*loads, *into):
        copy.start()
    for copy in loads:
        copy.wait()
    results, first_rows, norm = held[:6], held[6], held[7]
    masters, moments, squares = held[8:14], held[14:20], held[20:26]
    i = lax.axis_index("fsdp")
    first = first_rows[...]
    every = jnp.sum(norm[...], axis=(0, 1), keepdims=True)
    every = every + jnp.sum(first * first, axis=(0, 1), keepdims=True)
    root = jnp.sqrt(every)
    total[...] = root
    stores[0].start()
    factor = jnp.minimum(1.0, bound / root)
    out, up, down, low, high, small = results
    low, high = flat(low[...]), flat(high[...])
    qkv = [item[:, j * GROUP : (j + 1) * GROUP] for j in range(3) for item in (low, high)]
    per = masters[4].shape[1]
    rows = small[0, 0:8, 0:per]
    line = lax.broadcasted_iota(jnp.int32, (8, 1), 0)
    for s in range(D // per):
        at = s * per
        gain = first[at // 128 : at // 128 + 1, at % 128 : at % 128 + per]
        at = D + at
        shift = first[at // 128 : at // 128 + 1, at % 128 : at % 128 + per]
        mine = jnp.where(line == 0, gain, jnp.where(line == 1, shift, rows))
        rows = jnp.where(i == s, mine, rows)
    grads = (
        jnp.concatenate(qkv, axis=1),
        flat(out[...]),
        flat(up[...]),
        flat(down[...]),
        rows,
        small[1, 0:1, 0 : masters[5].shape[1]],
    )
    for k in range(6):
        new = adam_step(
            masters[k][...], moments[k][...], squares[k][...], grads[k], factor, RATES[k]
        )
        for at, item in zip((k, 6 + k, 12 + k), new):
            fresh[at][...] = item
            stores[1 + at].start()
        for first_half, second_half in zip(into[k : k + 2], out_of[k : k + 2]) if k % 2 == 0 else ():
            first_half.wait()
            second_half.start()
    for first_half, second_half in zip(into[6:], out_of[6:]):
        first_half.wait()
        second_half.start()
    for copy in (*stores, *out_of):
        copy.wait()


def run_update(bound, layer_out, token_grad, results, masters, moments, squares):
    def lines(items):
        return [*items[:5], items[5].reshape(1, -1)]

    state = lines(masters) + lines(moments) + lines(squares)
    held = [*results, *state]
    hbm = pl.BlockSpec(memory_space=pl.ANY)
    dma = pltpu.SemaphoreType.DMA
    pieces = 4
    passed = (layer_out, token_grad)
    done = pl.pallas_call(
        functools.partial(update_kernel, bound, pieces),
        in_specs=[hbm] * 28,
        out_specs=[hbm] * 21,
        out_shape=[shaped(item.shape, item.dtype) for item in passed]
        + [shaped((1, 1), F32)]
        + [shaped(item.shape, F32) for item in state],
        scratch_shapes=[pltpu.VMEM(item.shape, item.dtype) for item in (*held, *passed, *state)]
        + [pltpu.VMEM((1, 1), F32), dma((26,)), dma((19,)), dma((2, pieces))],
        compiler_params=vmem_params(),
        name="update_state",
    )(*held, *passed)
    fresh = [item.reshape(-1) if k % 6 == 5 else item for k, item in enumerate(done[3:])]
    return (done[0], done[1], done[2].reshape(()), *fresh)


def compute(tokens, cotangent, segment_ids, valid_counts, full):
    low_qkv, low_out, low_up, low_down, vectors, up_bias = full
    qkv, attended, lse = run_forward(segment_ids, valid_counts, tokens, vectors, low_qkv)
    (
        layer_out,
        grad_resid,
        grad_attended,
        grad_down,
        grad_up,
        grad_out_w,
        late,
        grad_bias,
    ) = run_feed(
        valid_counts, tokens, cotangent, attended, vectors, up_bias, low_out, low_up, low_down
    )
    token_grad, grad_qkv_w, early = run_backward(
        segment_ids,
        valid_counts,
        tokens,
        vectors,
        low_qkv,
        qkv,
        grad_attended,
        grad_resid,
        lse,
    )
    return layer_out, token_grad, (grad_qkv_w, grad_out_w, grad_up, grad_down), early, late, grad_bias


def fast_body(tokens, cotangent, segment_ids, valid_counts, *state):
    masters, moments, squares = state[:6], state[6:12], state[12:18]
    wide = lax.axis_size("fsdp")
    layer_out, token_grad, *results, _ = run_layer(
        wide // COLS, segment_ids, valid_counts, tokens, cotangent, masters
    )
    bound = 0.005 * math.sqrt(tokens.shape[0] * wide * lax.axis_size("dp") * PARAMS)
    return run_update(bound, layer_out, token_grad, results, masters, moments, squares)


def plain_body(tokens, cotangent, segment_ids, valid_counts, *state):
    masters, moments, squares = state[:6], state[6:12], state[12:18]
    wide = lax.axis_size("fsdp")
    replicas = lax.axis_size("dp")
    low = [item.astype(BF16) for item in masters]
    full = [
        lax.all_gather(item, "fsdp", axis=1 if k == 4 else 0, tiled=True)
        for k, item in enumerate(low)
    ]
    full[4] = full[4].astype(F32)
    full[5] = full[5].astype(F32).reshape(1, FF)
    layer_out, token_grad, totals, early, late, bias = compute(
        tokens, cotangent, segment_ids, valid_counts, full
    )
    grads = []
    for k, item in enumerate((*totals, early + late, bias.reshape(FF))):
        shard = lax.psum_scatter(item, "fsdp", scatter_dimension=1 if k == 4 else 0, tiled=True)
        grads.append(lax.psum(shard.astype(BF16), "dp").astype(F32))
    local_total = jnp.sum(grads[0] * grads[0])
    for item in grads[1:]:
        local_total = local_total + jnp.sum(item * item)
    grad_norm = jnp.sqrt(lax.psum(local_total, "fsdp"))
    bound = 0.005 * math.sqrt(tokens.shape[0] * wide * replicas * PARAMS)
    factor = jnp.minimum(1.0, bound / grad_norm)
    fresh = [
        adam_step(masters[k], moments[k], squares[k], grads[k], factor, RATES[k]) for k in range(6)
    ]
    return (
        layer_out,
        token_grad,
        grad_norm,
        *(item[0] for item in fresh),
        *(item[1] for item in fresh),
        *(item[2] for item in fresh),
    )


def solution(mesh):
    rows = P(("fsdp", "dp"), None)
    state = (
        P("fsdp", None),
        P("fsdp", None),
        P("fsdp", None),
        P("fsdp", None),
        P(None, "fsdp"),
        P("fsdp"),
    )
    wide, replicas = mesh.shape["fsdp"], mesh.shape["dp"]
    fits = replicas == 2 and wide == COLS * COLS
    return jax.shard_map(
        fast_body if fits else plain_body,
        mesh=mesh,
        in_specs=(rows, rows, rows, P(("fsdp", "dp")), *state, *state, *state),
        out_specs=(rows, rows, P(), *state, *state, *state),
        check_vma=False,
    )
```

```python
import functools
import math

import jax
import jax.numpy as jnp
from jax import lax
from jax.experimental import pallas as pl
from jax.experimental.pallas import tpu as pltpu
from jax.sharding import PartitionSpec as P

D = 512
HEADS = 8
HEAD_DIM = 64
FF = 2048
SEQ = 1024
IMG = 192
BLOCKS = 5
STEP = 5
PARAMS = 3151872
GROUP = 256
PER_GROUP = GROUP // HEAD_DIM

F32 = jnp.float32
BF16 = jnp.bfloat16

norm_eps = 1e-06
adam_eps = 1e-08
decay_rate = 0.05
beta_first = 0.5
beta_second = 0.5
masked_score = -1e30


def dot(left, right):
    return lax.dot_general(left, right, (((1,), (0,)), ((), ())), preferred_element_type=F32)


def dot_nt(left, right):
    return lax.dot_general(left, right, (((1,), (1,)), ((), ())), preferred_element_type=F32)


def dot_tn(left, right):
    return lax.dot_general(left, right, (((0,), (0,)), ((), ())), preferred_element_type=F32)


def norm_forward(values, gain, shift):
    center = values - jnp.mean(values, axis=-1, keepdims=True)
    spread = lax.rsqrt(jnp.mean(center * center, axis=-1, keepdims=True) + norm_eps)
    hat = center * spread
    return hat * gain + shift, hat, spread


def norm_backward(incoming, hat, spread, gain):
    scaled = incoming * gain
    return spread * (
        scaled
        - jnp.mean(scaled, axis=-1, keepdims=True)
        - hat * jnp.mean(scaled * hat, axis=-1, keepdims=True)
    )


def gelu_pair(values):
    half = 0.5 * (1.0 + lax.erf(values * (1.0 / math.sqrt(2.0))))
    bell = jnp.exp(-0.5 * values * values) * (1.0 / math.sqrt(2.0 * math.pi))
    return values * half, half + values * bell


def col_sum(values):
    return jnp.sum(values, axis=0, keepdims=True)


def head_of_lane():
    return lax.broadcasted_iota(jnp.int32, (1, GROUP), 1) // HEAD_DIM


def stack_heads(rows):
    head = head_of_lane()
    zero = jnp.zeros_like(rows)
    return jnp.concatenate([jnp.where(head == h, rows, zero) for h in range(PER_GROUP)], axis=0)


def unstack_heads(stacked):
    head = head_of_lane()
    n = stacked.shape[0] // PER_GROUP
    rows = stacked[(PER_GROUP - 1) * n :]
    for h in range(PER_GROUP - 2, -1, -1):
        rows = jnp.where(head == h, stacked[h * n : (h + 1) * n], rows)
    return rows


def links(seg, counts, s):
    return [
        (seg[s, b * IMG] == seg[s, (b + 1) * IMG]) & ((b + 1) * IMG < counts[s])
        for b in range(BLOCKS - 1)
    ]


def neighbour(b, linked):
    below = slice((b + 1) * IMG, (b + 2) * IMG) if b < BLOCKS - 1 else None
    above = slice((b - 1) * IMG, b * IMG) if b > 0 else None
    with_below = linked[b] if b < BLOCKS - 1 else jnp.bool_(False)
    with_above = linked[b - 1] if b > 0 else jnp.bool_(False)
    offset = jnp.where(with_below | with_above, 0.0, masked_score)
    return below, above, with_below, with_above, offset


def other_rows(ref, cols, below, above, with_below):
    if above is None:
        return ref[below, cols]
    if below is None:
        return ref[above, cols]
    return jnp.where(with_below, ref[below, cols], ref[above, cols])


def attend_block(query, keys, values, offset):
    stacked = stack_heads(query * jnp.asarray(HEAD_DIM**-0.5, BF16))
    scores = dot_nt(keys, stacked)
    own, other = scores[:IMG], scores[IMG:]
    top = jnp.maximum(
        jnp.max(own, axis=0, keepdims=True), jnp.max(other, axis=0, keepdims=True) + offset
    )
    own = jnp.exp(own - top)
    other = jnp.exp(other - (top - offset))
    total = col_sum(own) + col_sum(other)
    inverse = 1.0 / total
    probs = jnp.concatenate([own * inverse, other * inverse], axis=0).astype(BF16)
    return unstack_heads(dot_tn(probs, values)), top + jnp.log(total)


def attend_block_backward(query, keys, values, grad, lse, offset):
    stacked = stack_heads(query * jnp.asarray(HEAD_DIM**-0.5, BF16))
    grads = stack_heads(grad)
    scores = dot_nt(keys, stacked)
    grad_probs = dot_nt(values, grads)
    own = jnp.exp(scores[:IMG] - lse)
    other = jnp.exp(scores[IMG:] - (lse - offset))
    own_t = own * grad_probs[:IMG]
    other_t = other * grad_probs[IMG:]
    delta = col_sum(own_t) + col_sum(other_t)
    grad_scores = jnp.concatenate([own_t - own * delta, other_t - other * delta], axis=0)
    grad_scores = grad_scores.astype(BF16)
    probs = jnp.concatenate([own, other], axis=0).astype(BF16)
    grad_values = dot(probs, grads)
    grad_keys = dot(grad_scores, stacked)
    grad_query = unstack_heads(dot_tn(grad_scores, keys)) * (HEAD_DIM**-0.5)
    return grad_query, grad_keys, grad_values


def forward_kernel(chunk, seg, counts, tokens, vectors, low_qkv, qkv, attended, lse):
    s = pl.program_id(0)
    bias = jnp.concatenate([vectors[2:3, :], jnp.zeros((1, D), F32), vectors[3:4, :]], axis=1)
    for c in range(SEQ // chunk):
        rows = slice(c * chunk, (c + 1) * chunk)
        normed, _, _ = norm_forward(tokens[rows, :].astype(F32), vectors[0:1, :], vectors[1:2, :])
        qkv[rows, :] = (dot(normed.astype(BF16), low_qkv[...]) + bias).astype(BF16)
    linked = links(seg, counts, s)
    for g in range(D // GROUP):
        query_cols, key_cols, value_cols = [
            slice(j * D + g * GROUP, j * D + (g + 1) * GROUP) for j in range(3)
        ]
        out_cols = slice(g * GROUP, (g + 1) * GROUP)
        for b in range(BLOCKS):
            rows = slice(b * IMG, (b + 1) * IMG)
            below, above, with_below, with_above, offset = neighbour(b, linked)
            keys = jnp.concatenate(
                [qkv[rows, key_cols], other_rows(qkv, key_cols, below, above, with_below)], axis=0
            )
            own_values = qkv[rows, value_cols]
            values = jnp.concatenate(
                [own_values, other_rows(qkv, value_cols, below, above, with_below)], axis=0
            )
            mixed, block_lse = attend_block(qkv[rows, query_cols], keys, values, offset)
            mixed = mixed.astype(BF16)
            if b == BLOCKS - 1:
                mixed = jnp.where(b * IMG >= counts[s], own_values, mixed)
            attended[rows, out_cols] = mixed
            lse[g * BLOCKS + b] = block_lse
        attended[BLOCKS * IMG :, out_cols] = qkv[BLOCKS * IMG :, value_cols]


def feed_kernel(
    rows_in,
    chunk,
    counts,
    tokens,
    cotangent,
    attended,
    vectors,
    up_bias,
    low_out,
    low_up,
    low_down,
    layer_out,
    grad_resid,
    grad_attended,
    grad_down,
    grad_up,
    grad_out_w,
    grad_vectors,
    grad_bias,
):
    i = pl.program_id(0)

    @pl.when(i == 0)
    def _():
        for ref in (grad_down, grad_up, grad_out_w, grad_vectors, grad_bias):
            ref[...] = jnp.zeros_like(ref)

    per = SEQ // rows_in
    mixed = attended[...]
    resid = tokens[...].astype(F32) + (dot(mixed, low_out[...]) + vectors[4:5, :])
    normed, hat, spread = norm_forward(resid, vectors[5:6, :], vectors[6:7, :])
    low_two = normed.astype(BF16)
    position = (i % per) * rows_in + lax.broadcasted_iota(jnp.int32, (rows_in, 1), 0)
    grad = jnp.where(position < counts[i // per], cotangent[...].astype(F32), 0.0)
    grad_low = grad.astype(BF16)
    out = jnp.zeros((rows_in, D), F32)
    grad_two = jnp.zeros((rows_in, D), F32)
    for c in range(FF // chunk):
        cols = slice(c * chunk, (c + 1) * chunk)
        hidden = dot(low_two, low_up[:, cols]) + up_bias[:, cols]
        grad_active = dot_nt(grad_low, low_down[cols, :])
        active, slope = gelu_pair(hidden)
        active = active.astype(BF16)
        grad_hidden = grad_active * slope
        grad_hidden_low = grad_hidden.astype(BF16)
        out += dot(active, low_down[cols, :])
        grad_bias[:, cols] += col_sum(grad_hidden)
        grad_down[cols, :] += dot_tn(active, grad_low)
        grad_up[:, cols] += dot_tn(low_two, grad_hidden_low)
        grad_two += dot_nt(grad_hidden_low, low_up[:, cols])
    layer_out[...] = (resid + (out + vectors[7:8, :])).astype(BF16)
    back = grad + norm_backward(grad_two, hat, spread, vectors[5:6, :])
    back_low = back.astype(BF16)
    grad_resid[...] = back
    grad_out_w[...] += dot_tn(mixed, back_low)
    grad_attended[...] = dot_nt(back_low, low_out[...]).astype(BF16)
    grad_vectors[4:5, :] += col_sum(back)
    grad_vectors[5:6, :] += col_sum(grad_two * hat)
    grad_vectors[6:7, :] += col_sum(grad_two)
    grad_vectors[7:8, :] += col_sum(grad)


def backward_kernel(
    chunk,
    seg,
    counts,
    tokens,
    vectors,
    low_qkv,
    qkv,
    grad_attended,
    grad_resid,
    lse,
    token_grad,
    grad_qkv_w,
    grad_vectors,
    grad_qkv,
    key_sum,
    value_sum,
):
    s = pl.program_id(0)

    @pl.when(s == 0)
    def _():
        grad_qkv_w[...] = jnp.zeros_like(grad_qkv_w)
        grad_vectors[...] = jnp.zeros_like(grad_vectors)

    linked = links(seg, counts, s)
    padded = (BLOCKS - 1) * IMG >= counts[s]
    covered = slice(0, BLOCKS * IMG)
    tail = slice(BLOCKS * IMG, SEQ)
    for g in range(D // GROUP):
        query_cols, key_cols, value_cols = [
            slice(j * D + g * GROUP, j * D + (g + 1) * GROUP) for j in range(3)
        ]
        grad_cols = slice(g * GROUP, (g + 1) * GROUP)
        query_bias = jnp.zeros((1, GROUP), F32)
        for b in range(BLOCKS):
            rows = slice(b * IMG, (b + 1) * IMG)
            below, above, with_below, with_above, offset = neighbour(b, linked)
            keys = jnp.concatenate(
                [qkv[rows, key_cols], other_rows(qkv, key_cols, below, above, with_below)], axis=0
            )
            values = jnp.concatenate(
                [qkv[rows, value_cols], other_rows(qkv, value_cols, below, above, with_below)],
                axis=0,
            )
            grad = grad_attended[rows, grad_cols]
            grad_query, grad_keys, grad_values = attend_block_backward(
                qkv[rows, query_cols], keys, values, grad, lse[g * BLOCKS + b], offset
            )
            own_keys, own_values = grad_keys[:IMG], grad_values[:IMG]
            if b == BLOCKS - 1:
                grad_query = jnp.where(padded, 0.0, grad_query)
                own_keys = jnp.where(padded, 0.0, own_keys)
                own_values = jnp.where(padded, grad.astype(F32), own_values)
            query_bias += col_sum(grad_query)
            grad_qkv[rows, query_cols] = grad_query.astype(BF16)
            if b > 0:
                own_keys += jnp.where(with_above, key_sum[rows, :], 0.0)
                own_values += jnp.where(with_above, value_sum[rows, :], 0.0)
            key_sum[rows, :] = own_keys
            value_sum[rows, :] = own_values
            if below is not None:
                key_sum[below, :] = grad_keys[IMG:]
                value_sum[below, :] = grad_values[IMG:]
            if above is not None:
                key_sum[above, :] += jnp.where(with_above, grad_keys[IMG:], 0.0)
                value_sum[above, :] += jnp.where(with_above, grad_values[IMG:], 0.0)
        grad_tail = grad_attended[tail, grad_cols]
        grad_qkv[tail, query_cols] = jnp.zeros_like(grad_tail)
        grad_qkv[tail, key_cols] = jnp.zeros_like(grad_tail)
        grad_qkv[tail, value_cols] = grad_tail
        grad_qkv[covered, key_cols] = key_sum[...].astype(BF16)
        all_values = value_sum[...]
        grad_qkv[covered, value_cols] = all_values.astype(BF16)
        grad_vectors[2:3, grad_cols] += query_bias
        grad_vectors[3:4, grad_cols] += col_sum(all_values) + col_sum(grad_tail.astype(F32))
    for c in range(SEQ // chunk):
        rows = slice(c * chunk, (c + 1) * chunk)
        normed, hat, spread = norm_forward(
            tokens[rows, :].astype(F32), vectors[0:1, :], vectors[1:2, :]
        )
        grad = grad_qkv[rows, :]
        grad_qkv_w[...] += dot_tn(normed.astype(BF16), grad)
        grad_one = dot_nt(grad, low_qkv[...])
        token_grad[rows, :] = grad_resid[rows, :] + norm_backward(
            grad_one, hat, spread, vectors[0:1, :]
        )
        grad_vectors[0:1, :] += col_sum(grad_one * hat)
        grad_vectors[1:2, :] += col_sum(grad_one)


def vmem_params():
    return pltpu.CompilerParams(vmem_limit_bytes=60 * 2**20)


def by_rows(rows, cols):
    return pl.BlockSpec((rows, cols), lambda i: (i, 0))


def whole(*shape):
    return pl.BlockSpec(shape, lambda i: (0,) * len(shape))


def stats_spec():
    return pl.BlockSpec((2 * BLOCKS, 1, PER_GROUP * IMG), lambda i: (i, 0, 0))


def shaped(shape, dtype):
    return jax.ShapeDtypeStruct(shape, dtype)


SCALAR = pl.BlockSpec(memory_space=pltpu.SMEM)


def run_forward(seg, counts, tokens, vectors, low_qkv):
    rows = tokens.shape[0]
    seqs = rows // SEQ
    return pl.pallas_call(
        functools.partial(forward_kernel, 256),
        grid=(seqs,),
        in_specs=[SCALAR, SCALAR, by_rows(SEQ, D), whole(8, D), whole(D, 3 * D)],
        out_specs=[by_rows(SEQ, 3 * D), by_rows(SEQ, D), stats_spec()],
        out_shape=[
            shaped((rows, 3 * D), BF16),
            shaped((rows, D), BF16),
            shaped((seqs * 2 * BLOCKS, 1, PER_GROUP * IMG), F32),
        ],
        compiler_params=vmem_params(),
        name="attend_forward",
    )(seg, counts, tokens, vectors, low_qkv)


def run_feed(counts, tokens, cotangent, attended, vectors, up_bias, low_out, low_up, low_down):
    rows = tokens.shape[0]
    step = 512
    return pl.pallas_call(
        functools.partial(feed_kernel, step, 512),
        grid=(rows // step,),
        in_specs=[
            SCALAR,
            by_rows(step, D),
            by_rows(step, D),
            by_rows(step, D),
            whole(8, D),
            whole(1, FF),
            whole(D, D),
            whole(D, FF),
            whole(FF, D),
        ],
        out_specs=[
            by_rows(step, D),
            by_rows(step, D),
            by_rows(step, D),
            whole(FF, D),
            whole(D, FF),
            whole(D, D),
            whole(8, D),
            whole(1, FF),
        ],
        out_shape=[
            shaped((rows, D), BF16),
            shaped((rows, D), F32),
            shaped((rows, D), BF16),
            shaped((FF, D), F32),
            shaped((D, FF), F32),
            shaped((D, D), F32),
            shaped((8, D), F32),
            shaped((1, FF), F32),
        ],
        compiler_params=vmem_params(),
        name="feed_forward",
    )(counts, tokens, cotangent, attended, vectors, up_bias, low_out, low_up, low_down)


def run_backward(seg, counts, tokens, vectors, low_qkv, qkv, grad_attended, grad_resid, lse):
    rows = tokens.shape[0]
    return pl.pallas_call(
        functools.partial(backward_kernel, 512),
        grid=(rows // SEQ,),
        in_specs=[
            SCALAR,
            SCALAR,
            by_rows(SEQ, D),
            whole(8, D),
            whole(D, 3 * D),
            by_rows(SEQ, 3 * D),
            by_rows(SEQ, D),
            by_rows(SEQ, D),
            stats_spec(),
        ],
        out_specs=[by_rows(SEQ, D), whole(D, 3 * D), whole(8, D)],
        out_shape=[
            shaped((rows, D), F32),
            shaped((D, 3 * D), F32),
            shaped((8, D), F32),
        ],
        scratch_shapes=[
            pltpu.VMEM((SEQ, 3 * D), BF16),
            pltpu.VMEM((BLOCKS * IMG, GROUP), F32),
            pltpu.VMEM((BLOCKS * IMG, GROUP), F32),
        ],
        compiler_params=vmem_params(),
        name="attend_backward",
    )(seg, counts, tokens, vectors, low_qkv, qkv, grad_attended, grad_resid, lse)


def adam_step(weight, moment, square, grad, factor, rate):
    clipped = grad * factor
    moment_new = beta_first * moment + (1.0 - beta_first) * clipped
    square_new = beta_second * square + (1.0 - beta_second) * clipped * clipped
    first_hat = moment_new / (1.0 - beta_first**STEP)
    second_hat = square_new / (1.0 - beta_second**STEP)
    weight_new = weight - rate * (
        first_hat / (jnp.sqrt(second_hat) + adam_eps) + decay_rate * weight
    )
    return (weight_new, moment_new, square_new)


RATES = (
    2.0 / math.sqrt(D),
    8.0 / math.sqrt(D),
    2.0 / math.sqrt(D),
    2.0 / math.sqrt(FF),
    0.5,
    0.5,
)


MESH = pl.DeviceIdType.MESH
COLS = 4


class Place:
    def __init__(self, planes):
        self.planes = planes
        self.i = lax.axis_index("fsdp")
        self.c = c = lax.axis_index("dp")
        self.q = q = lax.rem(self.i, COLS)
        self.z = self.i // COLS
        x, y = lax.rem(q, 2), q // 2
        self.qx = y * 2 + (1 - x)
        self.qy = (1 - y) * 2 + x
        self.qa = c * self.qx + (1 - c) * self.qy
        self.qb = c * self.qy + (1 - c) * self.qx
        self.qd = COLS - 1 - q
        self.at_a = (self.z * COLS + self.qa, c)
        self.at_b = (self.z * COLS + self.qb, c)
        self.at_x = (self.z * COLS + self.qx, c)
        self.at_y = (self.z * COLS + self.qy, c)
        self.at_d = (self.z * COLS + self.qd, c)
        self.partner = (self.i, 1 - c)

    def plane(self, step):
        return lax.rem(self.z + step, self.planes)

    def along(self, step):
        return (self.plane(step) * COLS + self.q, self.c)

    def greet(self):
        barrier = pltpu.get_barrier_semaphore()
        friends = [self.along(step) for step in range(1, self.planes)]
        friends += [self.at_a, self.at_b, self.at_d, self.partner]
        for device in friends:
            pl.semaphore_signal(barrier, inc=1, device_id=device, device_id_type=MESH)
        pl.semaphore_wait(barrier, len(friends))


def remote(source, target, send, recv, device):
    return pltpu.make_async_remote_copy(
        src_ref=source,
        dst_ref=target,
        send_sem=send,
        recv_sem=recv,
        device_id=device,
        device_id_type=MESH,
    )


class Gather:
    def __init__(self, place, full, send, recv):
        p, c = place, place.c
        n = p.planes
        self.pieces = n

        def move(k, plane, col, device):
            ref = full.at[plane, col, c]
            return remote(ref, ref, send.at[k], recv.at[k], device)

        self.to_z = [move(k, p.z, p.q, p.along(k + 1)) for k in range(n - 1)]
        base = n - 1
        self.to_a = [move(base + d, p.plane(n - d), p.q, p.at_a) for d in range(n)]
        self.to_b = [move(base + n + d, p.plane(n - d), p.q, p.at_b) for d in range(n)]
        self.on_b = [move(base + 2 * n + d, p.plane(n - d), p.qa, p.at_b) for d in range(n)]
        base += 3 * n
        self.to_core = [
            move(base + k, slice(None), col, p.partner)
            for k, col in enumerate((p.q, p.qa, p.qb, p.qd))
        ]

    @staticmethod
    def count(planes):
        return 4 * planes + 3

    def begin(self):
        for copy in self.to_z:
            copy.start()

    def begin_own(self):
        self.to_a[0].start()
        self.to_b[0].start()

    def spread(self):
        for k, copy in enumerate(self.to_z):
            copy.wait_recv()
            self.to_a[k + 1].start()
            self.to_b[k + 1].start()
        self.to_core[0].start()

    def forward(self):
        for k in range(self.pieces):
            self.to_a[k].wait_recv()
            self.on_b[k].start()
        self.to_core[1].start()

    def last(self):
        for copy in self.to_b:
            copy.wait_recv()
        self.to_core[2].start()
        for copy in self.on_b:
            copy.wait_recv()
        self.to_core[3].start()

    def arrive(self):
        for copy in self.to_core:
            copy.wait_recv()

    def drain(self):
        for copy in (*self.to_z, *self.to_a, *self.to_b, *self.on_b, *self.to_core):
            copy.wait_send()


class Scatter:
    def __init__(self, place, total, bufs, result, send, recv, squares):
        self.place, self.total, self.result, self.squares = place, total, result, squares
        self.in_c, self.out_b, self.in_b = bufs[:3]
        self.out_a, self.in_a, self.out_z, self.in_z = bufs[3:7]
        self.out_c = bufs[7]
        p = place
        self.order = (p.qa, p.qd, p.qb, p.q)
        self.to_core = [
            remote(self.out_c.at[k], self.in_c.at[k], send.at[k], recv.at[k], p.partner)
            for k in range(4)
        ]
        self.to_b = [
            remote(self.out_b.at[k], self.in_b.at[k], send.at[4 + k], recv.at[4 + k], p.at_b)
            for k in range(2)
        ]
        self.to_a = remote(self.out_a, self.in_a, send.at[6], recv.at[6], p.at_a)
        self.to_z = [
            remote(self.out_z.at[k], self.in_z.at[k], send.at[7 + k], recv.at[7 + k], p.along(k + 1))
            for k in range(p.planes - 1)
        ]
        n = 6 + p.planes
        half = result.at[p.c]
        self.to_both = remote(half, half, send.at[n], recv.at[n], p.partner)

    @staticmethod
    def count(planes):
        return planes + 7

    @staticmethod
    def buffers(planes, rows, cols, own=True):
        shapes = [(4, planes)] + [(2, planes)] * 2 + [(planes,)] * 2 + [(planes - 1,)] * 2
        shapes += [(4, planes)] if own else []
        return [pltpu.VMEM((*shape, rows, cols), BF16) for shape in shapes]

    def begin(self):
        for k in range(4):
            self.out_c[k] = self.total[:, self.order[k], 1 - self.place.c].astype(BF16)
            self.to_core[k].start()

    def second(self):
        p = self.place
        for k, col in ((1, p.qd), (0, p.qb)):
            self.to_core[k].wait_recv()
            mine = self.total[:, col, p.c] + self.in_c[k].astype(F32)
            self.out_b[k] = mine.astype(BF16)
            self.to_b[k].start()

    def first(self):
        p = self.place
        self.to_core[2].wait_recv()
        self.to_b[1].wait_recv()
        mine = self.total[:, p.qa, p.c] + self.in_c[2].astype(F32) + self.in_b[1].astype(F32)
        self.out_a[...] = mine.astype(BF16)
        self.to_a.start()

    def planes(self):
        p = self.place
        self.to_core[3].wait_recv()
        self.to_b[0].wait_recv()
        self.to_a.wait_recv()

        def mine(z):
            local = self.total[z, p.q, p.c] + self.in_c[3, z].astype(F32)
            return local + self.in_b[0, z].astype(F32) + self.in_a[z].astype(F32)

        for k in range(p.planes - 1):
            self.out_z[k] = mine(p.plane(k + 1)).astype(BF16)
            self.to_z[k].start()
        self.result[p.c] = mine(p.z)

    def finish(self):
        p = self.place
        for copy in self.to_z:
            copy.wait_recv()
        shard = self.result[p.c]
        for k in range(p.planes - 1):
            shard = shard + self.in_z[k].astype(F32)
        self.result[p.c] = shard
        self.to_both.start()
        square = shard * shard
        lanes = sum(square[:, k : k + 128] for k in range(0, square.shape[1], 128))
        self.squares[...] += jnp.sum(lanes.reshape(-1, 8, 128), axis=0)

    def drain(self):
        self.to_both.wait_recv()
        for copy in (*self.to_core, *self.to_b, self.to_a, *self.to_z, self.to_both):
            copy.wait_send()


def sum_over_all(place, part, out, slots, send, recv):
    p = place
    count = p.planes + COLS - 1
    out[0] = part
    copies = [remote(out.at[0], slots.at[count + 1], send.at[0], recv.at[0], p.partner)]
    copies[0].start()
    copies[0].wait_recv()
    chip = part + slots[count + 1]
    out[1] = chip
    slots[p.z] = chip
    lines = [
        remote(out.at[1], slots.at[p.z], send.at[k + 1], recv.at[k + 1], p.along(k + 1))
        for k in range(p.planes - 1)
    ]
    for copy in lines:
        copy.start()
    for copy in lines:
        copy.wait_recv()
    column = slots[0]
    for k in range(1, p.planes):
        column = column + slots[k]
    out[2] = column
    slots[p.planes + p.q] = column
    columns = [
        remote(out.at[2], slots.at[p.planes + p.q], send.at[n], recv.at[n], device)
        for n, device in enumerate((p.at_x, p.at_y, p.at_d), p.planes)
    ]
    for copy in columns:
        copy.start()
    for copy in columns:
        copy.wait_recv()
    total = slots[p.planes]
    for k in range(1, COLS):
        total = total + slots[p.planes + k]
    for copy in (*copies, *lines, *columns):
        copy.wait_send()
    return total


def small_shard(place, vectors, up_bias):
    def tile(rows):
        for axis, full in ((1, 128), (0, 8)):
            short = list(rows.shape)
            short[axis] = full - short[axis]
            if short[axis]:
                rows = jnp.concatenate([rows, jnp.zeros(short, F32)], axis=axis)
        return rows

    rows, bias = tile(vectors[...]), tile(up_bias[...])
    half = jnp.where(place.c == 0, rows, bias)
    return jnp.concatenate([half, jnp.zeros((8, 128), F32)], axis=0).astype(BF16)


ROWS = 512
SPAN = SEQ // IMG * IMG


def five(planes, rows, cols):
    return (planes, COLS, 2, rows, cols)


def flat(value):
    return value.reshape(-1, value.shape[-1])


def layer_kernel(planes, per, long, *refs):
    seg, counts, tokens, cotangent = refs[:4]
    shards, vector_shard, bias_shard = refs[4:8], refs[8], refs[9]
    layer_out, token_grad = refs[10:12]
    results, first_rows, norm, kept = refs[12:18], refs[18], refs[19], refs[20]
    full, small, vectors, up_bias = refs[21:25], refs[25], refs[26], refs[27]
    totals = refs[28:34]
    tok, cot, qkv, mixed, resid, lse, key_sum, value_sum = refs[34:42]
    grad_vectors, grad_bias = refs[42:44]
    bufs = refs[44:89]
    g_send, g_recv, s_send, s_recv = refs[89:93]
    out_tiles, in_tiles, t_send, t_recv, load_sem, out_sem, grad_sem = refs[93:100]
    square_sum = refs[100]
    full_qkv, full_out, full_up, full_down = full
    sum_out, sum_up, sum_down, sum_low, sum_high, sum_small = totals
    p = Place(planes)
    rows_local = tok.shape[0]
    seqs = rows_local // SEQ

    low_one = cot
    load_tokens = pltpu.make_async_copy(tokens, tok, load_sem.at[0])
    load_cotangent = pltpu.make_async_copy(cotangent, cot, load_sem.at[1])
    keep_low = pltpu.make_async_copy(low_one, kept, load_sem.at[2])
    recall_low = pltpu.make_async_copy(kept, low_one, load_sem.at[3])
    load_tokens.start()

    small[p.z, p.q, p.c] = small_shard(p, vector_shard, bias_shard)
    for shard, target in zip(shards, full):
        target[p.z, p.q, p.c] = shard[p.c].astype(BF16)
    p.greet()
    g_small, g_qkv, g_out, g_up, g_down = gathers = [
        Gather(p, ref, g_send.at[k], g_recv.at[k]) for k, ref in enumerate((small, *full))
    ]
    spare = [ref.at[:, :, 0] for ref in full[1:]]
    bufs = [[*bufs[7 * k : 7 * k + 7], spare[k]] for k in range(3)] + [
        bufs[21 + 8 * k : 29 + 8 * k] for k in range(3)
    ]
    scatters = [
        Scatter(p, total, bufs[k], results[k], s_send.at[k], s_recv.at[k], square_sum)
        for k, total in enumerate(totals)
    ]
    s_out, s_up, s_down, s_low, s_high, s_small = scatters
    g_small.begin()
    g_qkv.begin()
    for item in gathers:
        item.begin_own()
    g_small.spread()
    g_qkv.spread()
    for item in (g_out, g_up, g_down):
        item.begin()
    g_small.forward()
    g_qkv.forward()
    g_out.spread()
    g_small.last()
    g_qkv.last()
    g_small.arrive()
    for s in range(planes * COLS):
        rows = small[s // COLS, s % COLS, 0].astype(F32)
        bias = small[s // COLS, s % COLS, 1].astype(F32)
        vectors[:, s * per : (s + 1) * per] = rows[:8, :per]
        up_bias[:, s * long : (s + 1) * long] = bias[:1, :long]
    load_tokens.wait()
    g_qkv.arrive()

    qkv_bias = jnp.concatenate([vectors[2:3, :], jnp.zeros((1, D), F32), vectors[3:4, :]], axis=1)
    chunk = 256
    beside_qkv = {
        0: [g_out.forward],
        2: [g_up.spread],
        5: [g_out.last],
        7: [g_up.forward],
    }

    def stages_at(k, table):
        for at, stages in table.items():

            @pl.when(k == at)
            def _(stages=stages):
                for stage in stages:
                    stage()

    @pl.loop(0, rows_local // chunk)
    def _(k):
        rows = pl.ds(pl.multiple_of(k * chunk, chunk), chunk)
        normed, _, _ = norm_forward(tok[rows, :].astype(F32), vectors[0:1, :], vectors[1:2, :])
        low = normed.astype(BF16)
        low_one[rows, :] = low
        qkv[rows, :] = (dot(low, flat(full_qkv[...])) + qkv_bias).astype(BF16)
        stages_at(k, beside_qkv)

    g_down.spread()
    keep_low.start()

    def block_rows(s, b):
        return pl.ds(pl.multiple_of(s * SEQ + b * IMG, 64), IMG)

    def tail_rows(s):
        return pl.ds(pl.multiple_of(s * SEQ + SPAN, 64), SEQ - SPAN)

    def columns(g):
        return [slice(j * D + g * GROUP, j * D + (g + 1) * GROUP) for j in range(3)]

    def with_other(cols, s, b, with_below):
        own = qkv[block_rows(s, b), cols]
        if b == 0:
            other = qkv[block_rows(s, 1), cols]
        elif b == BLOCKS - 1:
            other = qkv[block_rows(s, b - 1), cols]
        else:
            other = jnp.where(
                with_below, qkv[block_rows(s, b + 1), cols], qkv[block_rows(s, b - 1), cols]
            )
        return jnp.concatenate([own, other], axis=0)

    for g in range(D // GROUP):
        query_cols, key_cols, value_cols = columns(g)
        own_cols = slice(g * GROUP, (g + 1) * GROUP)

        def attend(s):
            linked = links(seg, counts, s)
            for b in range(BLOCKS):
                _, _, with_below, _, offset = neighbour(b, linked)
                keys = with_other(key_cols, s, b, with_below)
                values = with_other(value_cols, s, b, with_below)
                block, block_lse = attend_block(
                    qkv[block_rows(s, b), query_cols], keys, values, offset
                )
                block = block.astype(BF16)
                if b == BLOCKS - 1:
                    block = jnp.where(b * IMG >= counts[s], values[:IMG], block)
                mixed[block_rows(s, b), own_cols] = block
                lse[(s * 2 + g) * BLOCKS + b] = block_lse
            mixed[tail_rows(s), own_cols] = qkv[tail_rows(s), value_cols]

        pl.loop(0, seqs)(attend)
        if g == 0:
            g_up.last()
            g_down.forward()
            keep_low.wait()
            load_cotangent.start()
        else:
            g_down.last()

    for item in (g_out, g_up, g_down):
        item.arrive()
    load_cotangent.wait()

    for ref in (sum_out, sum_up, sum_down, sum_small, grad_vectors, grad_bias, square_sum):
        ref[...] = jnp.zeros_like(ref)
    width = FF // planes

    def feed(i, carry):
        rows = pl.ds(pl.multiple_of(i * ROWS, ROWS), ROWS)
        block = mixed[rows, :]
        low_out = flat(full_out[...])
        res = tok[rows, :].astype(F32) + (dot(block, low_out) + vectors[4:5, :])
        normed, hat, spread = norm_forward(res, vectors[5:6, :], vectors[6:7, :])
        low_two = normed.astype(BF16)
        position = (i % (SEQ // ROWS)) * ROWS + lax.broadcasted_iota(jnp.int32, (ROWS, 1), 0)
        grad = jnp.where(position < counts[i // (SEQ // ROWS)], cot[rows, :].astype(F32), 0.0)
        grad_low = grad.astype(BF16)
        out = jnp.zeros((ROWS, D), F32)
        grad_two = jnp.zeros((ROWS, D), F32)
        for k in range(planes):
            cols = slice(k * width, (k + 1) * width)
            up = flat(full_up[:, :, :, :, cols])
            down = flat(full_down[k])
            hidden = dot(low_two, up) + up_bias[:, cols]
            grad_active = dot_nt(grad_low, down)
            active, slope = gelu_pair(hidden)
            active = active.astype(BF16)
            grad_hidden = grad_active * slope
            grad_hidden_low = grad_hidden.astype(BF16)
            out += dot(active, down)
            grad_bias[:, cols] += col_sum(grad_hidden)
            sum_down[k] += dot_tn(active, grad_low).reshape(sum_down.shape[1:])
            sum_up[:, :, :, :, cols] += dot_tn(low_two, grad_hidden_low).reshape(
                *sum_up.shape[:-1], width
            )
            grad_two += dot_nt(grad_hidden_low, up)
        cot[rows, :] = (res + (out + vectors[7:8, :])).astype(BF16)
        pltpu.make_async_copy(cot.at[rows], layer_out.at[rows], out_sem.at[i]).start()
        back = grad + norm_backward(grad_two, hat, spread, vectors[5:6, :])
        back_low = back.astype(BF16)
        resid[rows, :] = back
        sum_out[...] += dot_tn(block, back_low).reshape(sum_out.shape)
        mixed[rows, :] = dot_nt(back_low, low_out).astype(BF16)
        grad_vectors[4:5, :] += col_sum(back)
        grad_vectors[5:6, :] += col_sum(grad_two * hat)
        grad_vectors[6:7, :] += col_sum(grad_two)
        grad_vectors[7:8, :] += col_sum(grad)
        return carry

    lax.fori_loop(0, rows_local // ROWS, feed, 0)

    for item in gathers:
        item.drain()
    s_down.begin()
    s_up.begin()
    s_out.begin()
    parts = [slice(k * ROWS, (k + 1) * ROWS) for k in range(rows_local // ROWS)]
    layer_copies = [
        pltpu.make_async_copy(cot.at[rows], layer_out.at[rows], out_sem.at[k])
        for k, rows in enumerate(parts)
    ]

    def recall():
        for copy in layer_copies:
            copy.wait()
        recall_low.start()

    beside_attention = {
        (0, 0, 1): [s_down.second, s_up.second, s_out.second],
        (0, 1, 1): [s_down.first, recall],
        (1, 0, 1): [s_up.first, s_down.planes, s_low.second],
        (1, 1, 1): [s_out.first, s_up.planes],
    }
    for g in range(D // GROUP):
        query_cols, key_cols, value_cols = columns(g)
        own_cols = slice(g * GROUP, (g + 1) * GROUP)

        def attend_back(s, query_bias):
            linked = links(seg, counts, s)
            padded = (BLOCKS - 1) * IMG >= counts[s]
            for b in range(BLOCKS):
                below, above, with_below, with_above, offset = neighbour(b, linked)
                rows = slice(b * IMG, (b + 1) * IMG)
                keys = with_other(key_cols, s, b, with_below)
                values = with_other(value_cols, s, b, with_below)
                grad = mixed[block_rows(s, b), own_cols]
                grad_query, grad_keys, grad_values = attend_block_backward(
                    qkv[block_rows(s, b), query_cols],
                    keys,
                    values,
                    grad,
                    lse[(s * 2 + g) * BLOCKS + b],
                    offset,
                )
                own_keys, own_values = grad_keys[:IMG], grad_values[:IMG]
                if b == BLOCKS - 1:
                    grad_query = jnp.where(padded, 0.0, grad_query)
                    own_keys = jnp.where(padded, 0.0, own_keys)
                    own_values = jnp.where(padded, grad.astype(F32), own_values)
                query_bias += col_sum(grad_query)
                qkv[block_rows(s, b), query_cols] = grad_query.astype(BF16)
                if b > 0:
                    own_keys += jnp.where(with_above, key_sum[rows, :], 0.0)
                    own_values += jnp.where(with_above, value_sum[rows, :], 0.0)
                key_sum[rows, :] = own_keys
                value_sum[rows, :] = own_values
                if below is not None:
                    key_sum[below, :] = grad_keys[IMG:]
                    value_sum[below, :] = grad_values[IMG:]
                if above is not None:
                    key_sum[above, :] += jnp.where(with_above, grad_keys[IMG:], 0.0)
                    value_sum[above, :] += jnp.where(with_above, grad_values[IMG:], 0.0)
                stages_at(s, {k[1]: v for k, v in beside_attention.items() if k[::2] == (g, b)})
            covered = pl.ds(pl.multiple_of(s * SEQ, SEQ), SPAN)
            grad_tail = mixed[tail_rows(s), own_cols]
            qkv[tail_rows(s), query_cols] = jnp.zeros_like(grad_tail)
            qkv[tail_rows(s), key_cols] = jnp.zeros_like(grad_tail)
            qkv[tail_rows(s), value_cols] = grad_tail
            qkv[covered, key_cols] = key_sum[...].astype(BF16)
            all_values = value_sum[...]
            qkv[covered, value_cols] = all_values.astype(BF16)
            grad_vectors[3:4, own_cols] += col_sum(all_values) + col_sum(grad_tail.astype(F32))
            return query_bias

        grad_vectors[2:3, own_cols] = lax.fori_loop(
            0, seqs, attend_back, jnp.zeros((1, GROUP), F32)
        )
        if g == 0:
            recall_low.wait()
        total = (sum_low, sum_high)[g]
        for j, cols in enumerate(columns(g)):
            part = dot_tn(low_one[...], qkv[:, cols])
            total[:, :, :, :, j * GROUP : (j + 1) * GROUP] = part.reshape(*total.shape[:-1], GROUP)
        (s_low, s_high)[g].begin()
        if g == 1:
            s_low.first()
            s_out.planes()

    for s in range(planes * COLS):
        cols = slice(s * per, (s + 1) * per)
        sum_small[s // COLS, s % COLS, 0, 0:8, 0:per] = grad_vectors[:, cols]
        sum_small[s // COLS, s % COLS, 1, 0:1, 0:long] = grad_bias[:, s * long : (s + 1) * long]
    s_small.begin()

    beside_last = {
        0: [s_high.second, s_small.second, s_down.finish],
        1: [s_high.first, s_small.first, s_low.planes],
        2: [s_high.planes, s_small.planes, s_up.finish],
        3: [s_out.finish, s_low.finish],
    }

    @pl.loop(0, rows_local // ROWS)
    def _(k):
        rows = pl.ds(pl.multiple_of(k * ROWS, ROWS), ROWS)
        _, hat, spread = norm_forward(tok[rows, :].astype(F32), vectors[0:1, :], vectors[1:2, :])
        grad_one = dot_nt(qkv[rows, :], flat(full_qkv[...]))
        resid[rows, :] += norm_backward(grad_one, hat, spread, vectors[0:1, :])
        pltpu.make_async_copy(resid.at[rows], token_grad.at[rows], grad_sem.at[k]).start()
        grad_vectors[0:1, :] += col_sum(grad_one * hat)
        grad_vectors[1:2, :] += col_sum(grad_one)
        stages_at(k, beside_last)

    for item in (s_high, s_small):
        item.finish()
    part = square_sum[...]
    gain_sum, shift_sum = grad_vectors[0:1, :], grad_vectors[1:2, :]
    rows = [
        item[:, k * 128 : (k + 1) * 128] for item in (gain_sum, shift_sum) for k in range(D // 128)
    ]
    tiles = jnp.concatenate([*rows, part], axis=0)
    tiles = sum_over_all(p, tiles, out_tiles, in_tiles, t_send, t_recv)
    first_rows[...] = tiles[:8]
    norm[...] = tiles[8:]
    for item in scatters:
        item.drain()
    for k, rows in enumerate(parts):
        pltpu.make_async_copy(resid.at[rows], token_grad.at[rows], grad_sem.at[k]).wait()


def run_layer(planes, seg, counts, tokens, cotangent, masters):
    halves = [item.reshape(2, item.shape[0] // 2, item.shape[1]) for item in masters[:4]]
    per, long = masters[4].shape[1], masters[5].shape[0]
    rows = tokens.shape[0]
    seqs = rows // SEQ
    shapes = [item.shape[1:] for item in halves]
    group = (shapes[0][0], 3 * GROUP)
    sums = [*shapes[1:], group, group, (16, 128)]
    vmem = pl.BlockSpec(memory_space=pltpu.VMEM)
    hbm = pl.BlockSpec(memory_space=pl.ANY)
    dma = pltpu.SemaphoreType.DMA
    scratch = [pltpu.VMEM(five(planes, *shape), BF16) for shape in (*shapes, (16, 128))]
    scratch += [pltpu.VMEM((8, D), F32), pltpu.VMEM((1, FF), F32)]
    scratch += [pltpu.VMEM(five(planes, *shape), F32) for shape in sums]
    scratch += [
        pltpu.VMEM((rows, D), BF16),
        pltpu.VMEM((rows, D), BF16),
        pltpu.VMEM((rows, 3 * D), BF16),
        pltpu.VMEM((rows, D), BF16),
        pltpu.VMEM((rows, D), F32),
        pltpu.VMEM((seqs * 2 * BLOCKS, 1, PER_GROUP * IMG), F32),
        pltpu.VMEM((SPAN, GROUP), F32),
        pltpu.VMEM((SPAN, GROUP), F32),
        pltpu.VMEM((8, D), F32),
        pltpu.VMEM((1, FF), F32),
    ]
    for k, shape in enumerate(sums):
        scratch += Scatter.buffers(planes, *shape, own=k >= 3)
    scratch += [dma((5, Gather.count(planes)))] * 2 + [dma((6, Scatter.count(planes)))] * 2
    scratch += [pltpu.VMEM((3, 16, 128), F32), pltpu.VMEM((planes + COLS + 1, 16, 128), F32)]
    scratch += [dma((planes + 3,))] * 2 + [dma((4,))] + [dma((rows // ROWS,))] * 2
    scratch += [pltpu.VMEM((8, 128), F32)]
    return pl.pallas_call(
        functools.partial(layer_kernel, planes, per, long),
        in_specs=[SCALAR, SCALAR, hbm, hbm] + [vmem] * 6,
        out_specs=[hbm, hbm] + [vmem] * 8 + [hbm],
        out_shape=[shaped((rows, D), BF16), shaped((rows, D), F32)]
        + [shaped((2, *shape), F32) for shape in sums]
        + [shaped((8, 128), F32), shaped((8, 128), F32), shaped((rows, D), BF16)],
        scratch_shapes=scratch,
        compiler_params=pltpu.CompilerParams(
            vmem_limit_bytes=63 * 2**20, collective_id=1, has_side_effects=True
        ),
        name="layer",
    )(seg, counts, tokens, cotangent, *halves, masters[4], masters[5].reshape(1, -1))


def update_kernel(bound, pieces, *refs):
    sources, targets, rest = refs[:28], refs[28:49], refs[49:]
    held, middles = rest[:26], rest[26:28]
    fresh, total = rest[28:46], rest[46]
    in_sems, out_sems, mid_sems = rest[47:]
    into, out_of = [], []
    for n, (source, middle, target) in enumerate(zip(sources[26:], middles, targets[:2])):
        rows = source.shape[0] // pieces
        for k in range(pieces):
            part, sem = pl.ds(k * rows, rows), mid_sems.at[n, k]
            into.append(pltpu.make_async_copy(source.at[part], middle.at[part], sem))
            out_of.append(pltpu.make_async_copy(middle.at[part], target.at[part], sem))
    loads = [
        pltpu.make_async_copy(source, target, in_sems.at[k])
        for k, (source, target) in enumerate(zip(sources, held))
    ]
    stores = [
        pltpu.make_async_copy(source, target, out_sems.at[k])
        for k, (source, target) in enumerate(zip((total, *fresh), targets[2:]))
    ]
    for copy in (*loads, *into):
        copy.start()
    for copy in loads:
        copy.wait()
    for first_half, second_half in zip(into, out_of):
        first_half.wait()
        second_half.start()
    results, first_rows, norm = held[:6], held[6], held[7]
    masters, moments, squares = held[8:14], held[14:20], held[20:26]
    i = lax.axis_index("fsdp")
    first = first_rows[...]
    every = jnp.sum(norm[...], axis=(0, 1), keepdims=True)
    every = every + jnp.sum(first * first, axis=(0, 1), keepdims=True)
    root = jnp.sqrt(every)
    total[...] = root
    stores[0].start()
    factor = jnp.minimum(1.0, bound / root)
    out, up, down, low, high, small = results
    low, high = flat(low[...]), flat(high[...])
    qkv = [item[:, j * GROUP : (j + 1) * GROUP] for j in range(3) for item in (low, high)]
    per = masters[4].shape[1]
    rows = small[0, 0:8, 0:per]
    line = lax.broadcasted_iota(jnp.int32, (8, 1), 0)
    for s in range(D // per):
        at = s * per
        gain = first[at // 128 : at // 128 + 1, at % 128 : at % 128 + per]
        at = D + at
        shift = first[at // 128 : at // 128 + 1, at % 128 : at % 128 + per]
        mine = jnp.where(line == 0, gain, jnp.where(line == 1, shift, rows))
        rows = jnp.where(i == s, mine, rows)
    grads = (
        jnp.concatenate(qkv, axis=1),
        flat(out[...]),
        flat(up[...]),
        flat(down[...]),
        rows,
        small[1, 0:1, 0 : masters[5].shape[1]],
    )
    for k in range(6):
        new = adam_step(
            masters[k][...], moments[k][...], squares[k][...], grads[k], factor, RATES[k]
        )
        for at, item in zip((k, 6 + k, 12 + k), new):
            fresh[at][...] = item
            stores[1 + at].start()
    for copy in (*stores, *out_of):
        copy.wait()


def run_update(bound, layer_out, token_grad, results, masters, moments, squares):
    def lines(items):
        return [*items[:5], items[5].reshape(1, -1)]

    state = lines(masters) + lines(moments) + lines(squares)
    held = [*results, *state]
    hbm = pl.BlockSpec(memory_space=pl.ANY)
    dma = pltpu.SemaphoreType.DMA
    pieces = 4
    passed = (layer_out, token_grad)
    done = pl.pallas_call(
        functools.partial(update_kernel, bound, pieces),
        in_specs=[hbm] * 28,
        out_specs=[hbm] * 21,
        out_shape=[shaped(item.shape, item.dtype) for item in passed]
        + [shaped((1, 1), F32)]
        + [shaped(item.shape, F32) for item in state],
        scratch_shapes=[pltpu.VMEM(item.shape, item.dtype) for item in (*held, *passed, *state)]
        + [pltpu.VMEM((1, 1), F32), dma((26,)), dma((19,)), dma((2, pieces))],
        compiler_params=vmem_params(),
        name="update_state",
    )(*held, *passed)
    fresh = [item.reshape(-1) if k % 6 == 5 else item for k, item in enumerate(done[3:])]
    return (done[0], done[1], done[2].reshape(()), *fresh)


def compute(tokens, cotangent, segment_ids, valid_counts, full):
    low_qkv, low_out, low_up, low_down, vectors, up_bias = full
    qkv, attended, lse = run_forward(segment_ids, valid_counts, tokens, vectors, low_qkv)
    (
        layer_out,
        grad_resid,
        grad_attended,
        grad_down,
        grad_up,
        grad_out_w,
        late,
        grad_bias,
    ) = run_feed(
        valid_counts, tokens, cotangent, attended, vectors, up_bias, low_out, low_up, low_down
    )
    token_grad, grad_qkv_w, early = run_backward(
        segment_ids,
        valid_counts,
        tokens,
        vectors,
        low_qkv,
        qkv,
        grad_attended,
        grad_resid,
        lse,
    )
    return layer_out, token_grad, (grad_qkv_w, grad_out_w, grad_up, grad_down), early, late, grad_bias


def fast_body(tokens, cotangent, segment_ids, valid_counts, *state):
    masters, moments, squares = state[:6], state[6:12], state[12:18]
    wide = lax.axis_size("fsdp")
    layer_out, token_grad, *results, _ = run_layer(
        wide // COLS, segment_ids, valid_counts, tokens, cotangent, masters
    )
    bound = 0.005 * math.sqrt(tokens.shape[0] * wide * lax.axis_size("dp") * PARAMS)
    return run_update(bound, layer_out, token_grad, results, masters, moments, squares)


def plain_body(tokens, cotangent, segment_ids, valid_counts, *state):
    masters, moments, squares = state[:6], state[6:12], state[12:18]
    wide = lax.axis_size("fsdp")
    replicas = lax.axis_size("dp")
    low = [item.astype(BF16) for item in masters]
    full = [
        lax.all_gather(item, "fsdp", axis=1 if k == 4 else 0, tiled=True)
        for k, item in enumerate(low)
    ]
    full[4] = full[4].astype(F32)
    full[5] = full[5].astype(F32).reshape(1, FF)
    layer_out, token_grad, totals, early, late, bias = compute(
        tokens, cotangent, segment_ids, valid_counts, full
    )
    grads = []
    for k, item in enumerate((*totals, early + late, bias.reshape(FF))):
        shard = lax.psum_scatter(item, "fsdp", scatter_dimension=1 if k == 4 else 0, tiled=True)
        grads.append(lax.psum(shard.astype(BF16), "dp").astype(F32))
    local_total = jnp.sum(grads[0] * grads[0])
    for item in grads[1:]:
        local_total = local_total + jnp.sum(item * item)
    grad_norm = jnp.sqrt(lax.psum(local_total, "fsdp"))
    bound = 0.005 * math.sqrt(tokens.shape[0] * wide * replicas * PARAMS)
    factor = jnp.minimum(1.0, bound / grad_norm)
    fresh = [
        adam_step(masters[k], moments[k], squares[k], grads[k], factor, RATES[k]) for k in range(6)
    ]
    return (
        layer_out,
        token_grad,
        grad_norm,
        *(item[0] for item in fresh),
        *(item[1] for item in fresh),
        *(item[2] for item in fresh),
    )


def solution(mesh):
    rows = P(("fsdp", "dp"), None)
    state = (
        P("fsdp", None),
        P("fsdp", None),
        P("fsdp", None),
        P("fsdp", None),
        P(None, "fsdp"),
        P("fsdp"),
    )
    wide, replicas = mesh.shape["fsdp"], mesh.shape["dp"]
    fits = replicas == 2 and wide == COLS * COLS
    return jax.shard_map(
        fast_body if fits else plain_body,
        mesh=mesh,
        in_specs=(rows, rows, rows, P(("fsdp", "dp")), *state, *state, *state),
        out_specs=(rows, rows, P(), *state, *state, *state),
        check_vma=False,
    )
```
